32 devices in a mesh: rep: 16 (over z, y, core), shard: 2 (over x).
Axes of the slice: x: 2, y: 2, z: 4, core: 2. Of those that a mesh axis runs over, the one named last changes fastest.
Arguments:
- tokens: bfloat16 [32, 1024, 960], P(('rep', 'shard')), may hold values from -6 to 6
- segments: int32 [32, 1024], P(('rep', 'shard')), may hold values from 0 to 3, never falling along the last dimension, each value on 1 to 800 neighbouring positions
- gain_attn: bfloat16 [960], P('shard'), may hold values from 0.5 to 1.5
- w_query: bfloat16 [960, 960], P('shard'), may hold values from -0.1875 to 0.1875
- key_weight_matrix: bfloat16 [960, 320], P('shard'), may hold values from -0.1875 to 0.1875
- value_weight_matrix: bfloat16 [960, 320], P('shard'), may hold values from -0.1875 to 0.1875
- w_out: bfloat16 [960, 960], P('shard'), may hold values from -1.5 to 1.5
- gain_mlp: bfloat16 [960], P('shard'), may hold values from 0.5 to 1.5
- w_gate: bfloat16 [960, 2560], P('shard'), may hold values from -0.1875 to 0.1875
- w_up: bfloat16 [960, 2560], P('shard'), may hold values from -0.1875 to 0.1875
- w_down: bfloat16 [2560, 960], P('shard'), may hold values from -0.125 to 0.125
- cotangent: bfloat16 [32, 1024, 960], P(('rep', 'shard')), may hold values from -6 to 6
Outputs:
- mixed: bfloat16 [32, 1024, 960], P(('rep', 'shard'))
- grad_tokens: bfloat16 [32, 1024, 960], P(('rep', 'shard'))
- grad_gain_attn: float32 [960], P('shard')
- grad_query: float32 [960, 960], P('shard')
- grad_key: float32 [960, 320], P('shard')
- grad_value: float32 [960, 320], P('shard')
- grad_out: float32 [960, 960], P('shard')
- grad_gain_mlp: float32 [960], P('shard')
- grad_gate: float32 [960, 2560], P('shard')
- grad_up: float32 [960, 2560], P('shard')
- grad_down: float32 [2560, 960], P('shard')
The draws below stay inside these ranges and needn't reach their ends.
Inputs may be any that keep to these rules, and one draw needn't show every extreme that they name: `segments`: in each sequence the numbers never fall; each document spans 1 to 800 tokens, and some document spans exactly 800.
All inputs are finite; a program needn't handle non-finite values.
Results may differ from the reference program's by a relative error of at most 0.022.
Values may be sent and summed in bfloat16 or wider, within the bound.
No kernel may reach another device: no remote copies, remote signals or barrier semaphores. Data moves between devices by JAX's collectives and lax.ppermute only.
A program may use at most 320 MiB of HBM per device.

```python
import math
import jax
import jax.numpy as jnp
import numpy as np
from jax import lax

MODEL_WIDTH = 960
QUERY_HEADS = 15
KEY_VALUE_HEADS = 5
HEAD_SIZE = 64
FF = 2560
LEN = 1024
DOCS = 4
MOST = 800
SEQS = 32


def block_scale(rng, dims, split, low, top_value):
    def one(axis_at, shards_of):
        heights = jax.random.uniform(jax.random.fold_in(jax.random.fold_in(rng, 6), axis_at), (shards_of,), jnp.float32, low / len(split), top_value / len(split))
        return jnp.repeat(jnp.exp(heights), dims[axis_at] // shards_of).reshape((-1,) + (1,) * (len(dims) - axis_at - 1))

    level = one(*split[0])
    for cut in split[1:]:
        level = level * one(*cut)
    return level


def profile(amount, total, bound, slope):
    weights = [(1 << 20) // math.isqrt(standing ** slope) + 1 for standing in range(2, amount + 1)]
    rest, counts = total - bound - (amount - 1), [1] * (amount - 1)
    while rest > 0:
        candidates = [i for i in range(amount - 1) if counts[i] < bound]
        whole, budget = sum([weights[i] for i in candidates]), rest
        for i in candidates:
            more = min(bound - counts[i], max(1, budget * weights[i] // whole), rest)
            counts[i] = counts[i] + more
            rest = rest - more
    return np.array([bound] + counts)


def uneven(own_key, number_of, total, most, skew):
    if number_of == 2:
        one = jax.random.randint(own_key, (), max(1, total - most), min(most, total - 1) + 1)
        return jnp.stack([one, total - one])
    lengths = jnp.asarray(profile(number_of, total, most, skew), jnp.int32)
    couples = (number_of - 1) // 2
    donor, receiver = lengths[1:1 + 2 * couples:2], lengths[2:2 + 2 * couples:2]
    margin = jnp.minimum(donor - 1, most - receiver)
    moved = jax.random.randint(jax.random.fold_in(own_key, 1), (couples,), 0, 1 << 20) % (margin + 1)
    lengths = lengths.at[1:1 + 2 * couples:2].set(donor - moved).at[2:2 + 2 * couples:2].set(receiver + moved)
    return lengths[jax.random.permutation(jax.random.fold_in(own_key, 2), number_of)]


def bell_draw(rng, dims, spread, bound, split=(), held_as=jnp.bfloat16):
    level = block_scale(rng, dims, split, -0.22, 0.18) if split else 1.0
    entries = jax.random.normal(rng, dims, jnp.float32) * spread * level
    return jnp.minimum(jnp.maximum(entries, -bound), bound).astype(held_as)


def setup_inputs(seed: int = 0) -> dict:
    seeds = jax.random.split(jax.random.key(seed), 13)
    return {
        "tokens": bell_draw(seeds[0], (SEQS, LEN, MODEL_WIDTH), 1.0, 6.0, ((0, 32),)),
        "segments": jax.vmap(lambda own: jnp.searchsorted(jnp.cumsum(uneven(own, DOCS, LEN, MOST, 1)), jnp.arange(LEN), side="right"))(jax.random.split(seeds[1], SEQS)).reshape((SEQS, LEN)).astype(jnp.int32),
        "gain_attn": jnp.clip(1.0 + 0.1 * jax.random.normal(seeds[2], (MODEL_WIDTH,), jnp.float32), 0.5, 1.5).astype(jnp.bfloat16),
        "w_query": bell_draw(seeds[3], (MODEL_WIDTH, QUERY_HEADS * HEAD_SIZE), MODEL_WIDTH ** -0.5, 0.1875, ((0, 2),)),
        "key_weight_matrix": bell_draw(seeds[4], (MODEL_WIDTH, KEY_VALUE_HEADS * HEAD_SIZE), MODEL_WIDTH ** -0.5, 0.1875, ((0, 2),)),
        "value_weight_matrix": bell_draw(seeds[5], (MODEL_WIDTH, KEY_VALUE_HEADS * HEAD_SIZE), MODEL_WIDTH ** -0.5, 0.1875, ((0, 2),)),
        "w_out": bell_draw(seeds[6], (QUERY_HEADS * HEAD_SIZE, MODEL_WIDTH), (max(1, QUERY_HEADS * HEAD_SIZE // 64)) ** -0.5, 1.5, ((0, 2),)),
        "gain_mlp": jnp.clip(1.0 + 0.1 * jax.random.normal(seeds[7], (MODEL_WIDTH,), jnp.float32), 0.5, 1.5).astype(jnp.bfloat16),
        "w_gate": bell_draw(seeds[8], (MODEL_WIDTH, FF), MODEL_WIDTH ** -0.5, 0.1875, ((0, 2),)),
        "w_up": bell_draw(seeds[9], (MODEL_WIDTH, FF), MODEL_WIDTH ** -0.5, 0.1875, ((0, 2),)),
        "w_down": bell_draw(seeds[10], (FF, MODEL_WIDTH), FF ** -0.5, 0.125, ((0, 2),)),
        "cotangent": bell_draw(seeds[11], (SEQS, LEN, MODEL_WIDTH), 1.0, 6.0, ((0, 32),)),
    }


HIGHEST = lax.Precision.HIGHEST
EPS = 1e-05
NEGATIVE = -1e+30

@jax.custom_vjp
def lower_bound(v):
    return lax.optimization_barrier(v.astype(jnp.bfloat16)).astype(jnp.float32)

@jax.custom_vjp
def low_back(v):
    return v

def low_keep(v):
    return (lower_bound(v), None)

def low_pass(kept, grad):
    return (grad,)

def back_keep(v):
    return (v, None)

def back_low(kept, grad):
    return (lower_bound(grad),)
lower_bound.defvjp(low_keep, low_pass)
low_back.defvjp(back_keep, back_low)

def angles(documents):
    segment_length = documents.shape[0]
    places = jnp.arange(segment_length, dtype=jnp.int32)
    begins = jnp.concatenate([jnp.ones((1,), dtype=jnp.bool_), documents[1:] != documents[:-1]])
    starting = lax.cummax(jnp.where(begins, places, 0), axis=0)
    offsets = (places - starting).astype(jnp.float32)
    rates = 10000.0 ** (-2.0 * jnp.arange(HEAD_SIZE // 2).astype(jnp.float32) / HEAD_SIZE)
    phases = offsets[:, None] * rates[None, :]
    return (jnp.cos(phases)[:, None, :], jnp.sin(phases)[:, None, :])

def apply_rotary(value_vectors, cosine_table, sine_table):
    halfway = value_vectors.shape[-1] // 2
    leading = value_vectors[..., :halfway]
    trailing = value_vectors[..., halfway:]
    return jnp.concatenate([leading * cosine_table - trailing * sine_table, trailing * cosine_table + leading * sine_table], axis=-1)

def rms_norm(value_vectors, gain):
    return value_vectors * lax.rsqrt(lax.optimization_barrier(jnp.mean(value_vectors * value_vectors, axis=-1, keepdims=True)) + EPS) * gain

def attend(query_vectors, key_vectors, value_vectors, documents):
    segment_length = query_vectors.shape[0]
    block_slice = min(512, segment_length)
    block_count = segment_length // block_slice
    query_block_list = query_vectors.reshape(block_count, block_slice, KEY_VALUE_HEADS, QUERY_HEADS // KEY_VALUE_HEADS, HEAD_SIZE)
    starts = jnp.arange(block_count, dtype=jnp.int32) * block_slice

    def one_block(pieces):
        query_block, offset = pieces
        scores = jnp.einsum('qgrd,kgd->grqk', query_block, key_vectors, precision=HIGHEST) * HEAD_SIZE ** (-0.5)
        scores = low_back(scores)
        query_rows = offset + jnp.arange(block_slice, dtype=jnp.int32)
        key_rows = jnp.arange(segment_length, dtype=jnp.int32)
        query_docs = lax.dynamic_slice_in_dim(documents, offset.astype(jnp.int32), block_slice)
        allowed = (query_docs[:, None] == documents[None, :]) & (key_rows[None, :] <= query_rows[:, None])
        scores = jnp.where(allowed, scores, NEGATIVE)
        probs = jax.nn.softmax(scores, axis=-1)
        return jnp.einsum('grqk,kgd->qgrd', lower_bound(probs), value_vectors, precision=HIGHEST)
    outputs = lax.map(jax.checkpoint(one_block), (query_block_list, starts))
    return outputs.reshape(segment_length, QUERY_HEADS * HEAD_SIZE)

def layer(inputs, gain_attn, w_query, key_weight_matrix, value_weight_matrix, w_out, gain_mlp, w_gate, w_up, w_down, documents):
    segment_length = inputs.shape[0]
    cosine_table, sine_table = angles(documents)
    attn_in = lower_bound(rms_norm(inputs, gain_attn))
    query_pre = low_back(jnp.dot(attn_in, w_query, precision=HIGHEST))
    key_before_rotation = low_back(jnp.dot(attn_in, key_weight_matrix, precision=HIGHEST))
    value_before_heads = low_back(jnp.dot(attn_in, value_weight_matrix, precision=HIGHEST))
    query_vectors = lower_bound(apply_rotary(query_pre.reshape(segment_length, QUERY_HEADS, HEAD_SIZE), cosine_table, sine_table))
    key_vectors = lower_bound(apply_rotary(key_before_rotation.reshape(segment_length, KEY_VALUE_HEADS, HEAD_SIZE), cosine_table, sine_table))
    value_vectors = lower_bound(value_before_heads.reshape(segment_length, KEY_VALUE_HEADS, HEAD_SIZE))
    heads = lower_bound(low_back(attend(query_vectors, key_vectors, value_vectors, documents)))
    middle = inputs + low_back(jnp.dot(heads, w_out, precision=HIGHEST))
    mlp_in = lower_bound(rms_norm(middle, gain_mlp))
    gate = low_back(jnp.dot(mlp_in, w_gate, precision=HIGHEST))
    upward = low_back(jnp.dot(mlp_in, w_up, precision=HIGHEST))
    hidden = lower_bound(jax.nn.silu(gate) * upward)
    return middle + low_back(jnp.dot(hidden, w_down, precision=HIGHEST))

def reference(tokens, segments, gain_attn, w_query, key_weight_matrix, value_weight_matrix, w_out, gain_mlp, w_gate, w_up, w_down, cotangent):
    weights = tuple((weight.astype(jnp.float32) for weight in (gain_attn, w_query, key_weight_matrix, value_weight_matrix, w_out, gain_mlp, w_gate, w_up, w_down)))

    def one_sequence(carry, pieces):
        inputs, documents, upstream = pieces

        def forward(inputs_now, *weights_now):
            return layer(inputs_now, *weights_now, documents)
        output, pullback = jax.vjp(forward, inputs.astype(jnp.float32), *weights)
        grads = pullback(upstream.astype(jnp.float32))
        summed = tuple((total + grad for total, grad in zip(carry, grads[1:])))
        return (summed, (output.astype(jnp.bfloat16), grads[0].astype(jnp.bfloat16)))
    initial = tuple((jnp.zeros(weight.shape, jnp.float32) for weight in weights))
    sums, (outputs, input_grads) = lax.scan(one_sequence, initial, (tokens, segments, cotangent))
    return (outputs, input_grads, sums[0], sums[1], sums[2], sums[3], sums[4], sums[5], sums[6], sums[7], sums[8])
```

```python
from functools import partial

import jax
import jax.numpy as jnp
from jax import lax
from jax.sharding import PartitionSpec as P

QUERY_HEADS = 15
KEY_VALUE_HEADS = 5
HEAD_SIZE = 64


EPS = 1e-05
NEGATIVE = -1e30


def angles(documents, head_dim):
    segment_length = documents.shape[0]
    places = jnp.arange(segment_length, dtype=jnp.int32)
    begins = jnp.concatenate([jnp.ones((1,), dtype=jnp.bool_), documents[1:] != documents[:-1]])
    starting = lax.cummax(jnp.where(begins, places, 0), axis=0)
    offsets = (places - starting).astype(jnp.float32)
    rates = 10000.0 ** (-2.0 * jnp.arange(head_dim // 2).astype(jnp.float32) / head_dim)
    phases = offsets[:, None] * rates[None, :]
    return (jnp.cos(phases)[:, None, :], jnp.sin(phases)[:, None, :])


def apply_rotary(value_vectors, cosine_table, sine_table):
    halfway = value_vectors.shape[-1] // 2
    leading = value_vectors[..., :halfway]
    trailing = value_vectors[..., halfway:]
    return jnp.concatenate(
        [
            leading * cosine_table - trailing * sine_table,
            trailing * cosine_table + leading * sine_table,
        ],
        axis=-1,
    )


def invert_rotary(value_vectors, cosine_table, sine_table):
    halfway = value_vectors.shape[-1] // 2
    leading = value_vectors[..., :halfway]
    trailing = value_vectors[..., halfway:]
    return jnp.concatenate(
        [
            leading * cosine_table + trailing * sine_table,
            trailing * cosine_table - leading * sine_table,
        ],
        axis=-1,
    )


def masked_scores(query_block, key_vectors, documents, offset):
    block_count = query_block.shape[0]
    scores = jnp.einsum(
        "qgrd,kgd->grqk", query_block, key_vectors, preferred_element_type=jnp.float32
    ) * key_vectors.shape[-1] ** (-0.5)
    query_rows = offset + jnp.arange(block_count, dtype=jnp.int32)
    key_rows = jnp.arange(key_vectors.shape[0], dtype=jnp.int32)
    query_docs = documents[offset : offset + block_count]
    allowed = (query_docs[:, None] == documents[None, :]) & (
        key_rows[None, :] <= query_rows[:, None]
    )
    return jnp.where(allowed, scores, NEGATIVE)


def attend_forward(pieces):
    query_vectors, key_vectors, value_vectors, documents = pieces
    segment_length = query_vectors.shape[0]
    block_slice = min(512, segment_length)
    outputs = []
    totals = []
    for offset in range(0, segment_length, block_slice):
        scores = masked_scores(
            query_vectors[offset : offset + block_slice], key_vectors, documents, offset
        )
        highest = jnp.max(scores, axis=-1, keepdims=True)
        exponents = jnp.exp(scores - highest)
        summed = jnp.sum(exponents, axis=-1, keepdims=True)
        probs = (exponents / summed).astype(jnp.bfloat16)
        outputs.append(
            jnp.einsum("grqk,kgd->qgrd", probs, value_vectors, preferred_element_type=jnp.float32)
        )
        totals.append(highest[..., 0] + jnp.log(summed[..., 0]))
    return (jnp.concatenate(outputs, axis=0), jnp.concatenate(totals, axis=-1))


def attend_backward(pieces):
    query_vectors, key_vectors, value_vectors, documents, upstream, totals = pieces
    segment_length = query_vectors.shape[0]
    block_slice = min(512, segment_length)
    scaling = key_vectors.shape[-1] ** (-0.5)
    key_grad = jnp.zeros(key_vectors.shape, jnp.float32)
    value_grad = jnp.zeros(value_vectors.shape, jnp.float32)
    query_grads = []
    for offset in range(0, segment_length, block_slice):
        query_block = query_vectors[offset : offset + block_slice]
        upstream_block = upstream[offset : offset + block_slice]
        scores = masked_scores(query_block, key_vectors, documents, offset)
        probs = jnp.exp(scores - totals[..., offset : offset + block_slice, None])
        probs_grad = jnp.einsum(
            "qgrd,kgd->grqk", upstream_block, value_vectors, preferred_element_type=jnp.float32
        )
        inner = jnp.sum(probs * probs_grad, axis=-1, keepdims=True)
        score_grad = (probs * (probs_grad - inner)).astype(jnp.bfloat16)
        query_grads.append(
            jnp.einsum(
                "grqk,kgd->qgrd", score_grad, key_vectors, preferred_element_type=jnp.float32
            )
            * scaling
        )
        key_grad = (
            key_grad
            + jnp.einsum(
                "grqk,qgrd->kgd", score_grad, query_block, preferred_element_type=jnp.float32
            )
            * scaling
        )
        value_grad = value_grad + jnp.einsum(
            "grqk,qgrd->kgd",
            probs.astype(jnp.bfloat16),
            upstream_block,
            preferred_element_type=jnp.float32,
        )
    return (jnp.concatenate(query_grads, axis=0), key_grad, value_grad)


def product(left, right):
    return jnp.dot(left, right, preferred_element_type=jnp.float32)


def norm_backward(grad_in, normed, inverse, gain):
    weighted = grad_in * gain
    return inverse * (weighted - normed * jnp.mean(weighted * normed, axis=-1, keepdims=True))


def bit_swap(count, bit):
    return [(i, i ^ bit) for i in range(count)]


def swap_rep(value, bit):
    return lax.ppermute(value, "rep", bit_swap(lax.axis_size("rep"), bit))


def swap_shard(value, bit):
    return lax.ppermute(value, "shard", bit_swap(lax.axis_size("shard"), bit))


def rep_bit(bit):
    return (lax.axis_index("rep") // bit) % 2


def place_pair(mine, other, bit, axis):
    low = jnp.concatenate([mine, other], axis=axis)
    high = jnp.concatenate([other, mine], axis=axis)
    return jnp.where(bit == 0, low, high)


def gather_rows(piece):
    shards = lax.axis_size("shard")
    rows, columns = piece.shape
    quarter = rows // 4
    core, side = rep_bit(1), rep_bit(2)
    part = lax.dynamic_slice_in_dim(piece, (core * 2 + side) * quarter, quarter, 0)
    held = part[None]
    bit = 1
    while bit < shards:
        held = jnp.concatenate([held, swap_shard(held, bit)], axis=0)
        bit *= 2
    others = held[1:]
    others = place_pair(others, swap_rep(others, 2), side, 1)
    others = place_pair(others, swap_rep(others, 1), core, 1)
    me = lax.axis_index("shard")
    if shards == 2:
        return place_pair(piece, others[0], me, 0)
    whole = jnp.zeros((shards, rows, columns), piece.dtype)
    whole = lax.dynamic_update_slice_in_dim(whole, piece[None], me, 0)
    for j in range(1, shards):
        whole = lax.dynamic_update_slice_in_dim(whole, others[j - 1][None], me ^ j, 0)
    return whole.reshape(shards * rows, columns)


def add_up(left, right):
    return (left.astype(jnp.float32) + right.astype(jnp.float32)).astype(jnp.bfloat16)


def halve(value, bit, axis, swap):
    half = value.shape[axis] // 2
    mine = lax.dynamic_slice_in_dim(value, bit * half, half, axis)
    theirs = lax.dynamic_slice_in_dim(value, (1 - bit) * half, half, axis)
    return add_up(mine, swap(theirs))


def halve_shard(value):
    bit = lax.axis_size("shard") // 2
    while bit:
        value = halve(
            value, (lax.axis_index("shard") // bit) % 2, 0, partial(swap_shard, bit=bit)
        )
        bit //= 2
    return value


def reduce_rows(grad, order, axes):
    shards = lax.axis_size("shard")
    rows, columns = grad.shape
    value = grad.astype(jnp.bfloat16).reshape(shards, rows // shards, columns)
    value = halve(value, rep_bit(1), axes[1], partial(swap_rep, bit=1))
    for step in order:
        if step == 0:
            value = halve_shard(value)
        else:
            value = halve(value, rep_bit(step), axes[step], partial(swap_rep, bit=step))
    bit = 8
    while bit < lax.axis_size("rep"):
        value = add_up(value, swap_rep(value, bit))
        bit *= 2
    for step in [s for s in reversed(order) if s] + [1]:
        value = place_pair(value, swap_rep(value, step), rep_bit(step), axes[step])
    return value[0].astype(jnp.float32)


def reduce_gains(grads):
    bit = 1
    while bit < lax.axis_size("rep"):
        grads = grads + swap_rep(grads, bit)
        bit *= 2
    bit = 1
    while bit < lax.axis_size("shard"):
        grads = grads + swap_shard(grads, bit)
        bit *= 2
    own = grads.shape[1] // lax.axis_size("shard")
    return lax.dynamic_slice_in_dim(grads, lax.axis_index("shard") * own, own, 1)


def per_device(
    tokens,
    segments,
    gain_attn,
    w_query,
    key_weight_matrix,
    value_weight_matrix,
    w_out,
    gain_mlp,
    w_gate,
    w_up,
    w_down,
    cotangent,
):
    packed_sequences, segment_length, width = tokens.shape
    row_total_count = packed_sequences * segment_length
    head_groups = QUERY_HEADS // KEY_VALUE_HEADS
    columns = QUERY_HEADS * HEAD_SIZE
    key_columns = KEY_VALUE_HEADS * HEAD_SIZE
    gains = jnp.stack([gain_attn, gain_mlp], axis=1)
    gains = jnp.pad(gains, ((0, 0), (0, 62)))
    first = gather_rows(
        jnp.concatenate([w_query, key_weight_matrix, value_weight_matrix, gains], axis=1)
    )
    end_key = columns + key_columns
    end_value = end_key + key_columns
    attn_set = (
        first[:, end_value],
        first[:, :columns],
        first[:, columns:end_key],
        first[:, end_key:end_value],
        gather_rows(w_out),
    )
    mlp_set = (
        first[:, end_value + 1],
        gather_rows(w_gate),
        gather_rows(w_up),
        gather_rows(w_down),
    )
    cosine_table, sine_table = jax.vmap(partial(angles, head_dim=HEAD_SIZE))(segments)
    norm_one = attn_set[0].astype(jnp.float32)
    inputs_flat = tokens.reshape(row_total_count, width).astype(jnp.float32)
    inverse_one = lax.rsqrt(jnp.mean(inputs_flat * inputs_flat, axis=-1, keepdims=True) + EPS)
    normed_one = inputs_flat * inverse_one
    attn_in = (normed_one * norm_one).astype(jnp.bfloat16)
    query_pre = product(attn_in, attn_set[1])
    key_before_rotation = product(attn_in, attn_set[2])
    value_before_heads = product(attn_in, attn_set[3])
    query_vectors = (
        apply_rotary(
            query_pre.reshape(packed_sequences, segment_length, QUERY_HEADS, HEAD_SIZE),
            cosine_table,
            sine_table,
        )
        .astype(jnp.bfloat16)
        .reshape(packed_sequences, segment_length, KEY_VALUE_HEADS, head_groups, HEAD_SIZE)
    )
    key_vectors = apply_rotary(
        key_before_rotation.reshape(packed_sequences, segment_length, KEY_VALUE_HEADS, HEAD_SIZE),
        cosine_table,
        sine_table,
    ).astype(jnp.bfloat16)
    value_vectors = value_before_heads.reshape(
        packed_sequences, segment_length, KEY_VALUE_HEADS, HEAD_SIZE
    ).astype(jnp.bfloat16)
    attended, totals = lax.map(
        attend_forward, (query_vectors, key_vectors, value_vectors, segments)
    )
    heads = attended.reshape(row_total_count, QUERY_HEADS * HEAD_SIZE).astype(jnp.bfloat16)
    middle = inputs_flat + product(heads, attn_set[4])
    norm_two = mlp_set[0].astype(jnp.float32)
    inverse_two = lax.rsqrt(jnp.mean(middle * middle, axis=-1, keepdims=True) + EPS)
    normed_two = middle * inverse_two
    mlp_in = (normed_two * norm_two).astype(jnp.bfloat16)
    gate_pre = product(mlp_in, mlp_set[1])
    up_pre = product(mlp_in, mlp_set[2])
    activated = jax.nn.silu(gate_pre)
    hidden = (activated * up_pre).astype(jnp.bfloat16)
    result = middle + product(hidden, mlp_set[3])
    mixed = result.astype(jnp.bfloat16).reshape(packed_sequences, segment_length, width)
    mlp_back = mlp_set
    attn_back = attn_set
    out_grad = cotangent.reshape(row_total_count, width)
    grad_down = product(hidden.T, out_grad)
    hidden_grad = product(out_grad, mlp_back[3].T)
    sigmoid_gate = jax.nn.sigmoid(gate_pre)
    gate_grad = (
        hidden_grad * up_pre * sigmoid_gate * (1.0 + gate_pre * (1.0 - sigmoid_gate))
    ).astype(jnp.bfloat16)
    up_grad = (hidden_grad * activated).astype(jnp.bfloat16)
    grad_gate = product(mlp_in.T, gate_grad)
    grad_up = product(mlp_in.T, up_grad)
    mlp_in_grad = product(gate_grad, mlp_back[1].T) + product(up_grad, mlp_back[2].T)
    grad_norm_two = jnp.sum(mlp_in_grad * normed_two, axis=0)
    middle_grad = out_grad.astype(jnp.float32) + norm_backward(
        mlp_in_grad, normed_two, inverse_two, mlp_back[0].astype(jnp.float32)
    )
    wide = {1: 2, 2: 2, 4: 1}
    tall = {1: 1, 2: 1, 4: 1}
    sum_gate = reduce_rows(grad_gate, (0, 2, 4), wide)
    sum_up = reduce_rows(grad_up, (4, 2, 0), wide)
    sum_down = reduce_rows(grad_down, (2, 0, 4), tall)
    branch_grad = middle_grad.astype(jnp.bfloat16)
    grad_out = product(heads.T, branch_grad)
    heads_grad = (
        product(branch_grad, attn_back[4].T)
        .astype(jnp.bfloat16)
        .reshape(packed_sequences, segment_length, KEY_VALUE_HEADS, head_groups, HEAD_SIZE)
    )
    queries_grad, key_vectors_gradient, value_vectors_gradient = lax.map(
        attend_backward, (query_vectors, key_vectors, value_vectors, segments, heads_grad, totals)
    )
    query_back = (
        invert_rotary(
            queries_grad.reshape(packed_sequences, segment_length, QUERY_HEADS, HEAD_SIZE),
            cosine_table,
            sine_table,
        )
        .reshape(row_total_count, QUERY_HEADS * HEAD_SIZE)
        .astype(jnp.bfloat16)
    )
    key_backward_rows = (
        invert_rotary(key_vectors_gradient, cosine_table, sine_table)
        .reshape(row_total_count, KEY_VALUE_HEADS * HEAD_SIZE)
        .astype(jnp.bfloat16)
    )
    value_backward_rows = value_vectors_gradient.reshape(
        row_total_count, KEY_VALUE_HEADS * HEAD_SIZE
    ).astype(jnp.bfloat16)
    grad_query = product(attn_in.T, query_back)
    grad_key = product(attn_in.T, key_backward_rows)
    grad_value = product(attn_in.T, value_backward_rows)
    attn_in_grad = (
        product(query_back, attn_back[1].T)
        + product(key_backward_rows, attn_back[2].T)
        + product(value_backward_rows, attn_back[3].T)
    )
    grad_norm_one = jnp.sum(attn_in_grad * normed_one, axis=0)
    input_grad = middle_grad + norm_backward(
        attn_in_grad, normed_one, inverse_one, attn_back[0].astype(jnp.float32)
    )
    grad_tokens = input_grad.astype(jnp.bfloat16).reshape(packed_sequences, segment_length, width)
    attn_sums = reduce_rows(
        jnp.concatenate([grad_query, grad_key, grad_value, grad_out], axis=1), (0, 4, 2), wide
    )
    gain_sums = reduce_gains(jnp.stack([grad_norm_one, grad_norm_two]))
    return (
        mixed,
        grad_tokens,
        gain_sums[0],
        attn_sums[:, :columns],
        attn_sums[:, columns:end_key],
        attn_sums[:, end_key:end_value],
        attn_sums[:, end_value:],
        gain_sums[1],
        sum_gate,
        sum_up,
        sum_down,
    )


def solution(mesh):
    placed = (
        P(("rep", "shard"), None, None),
        P(("rep", "shard"), None),
        P("shard"),
        P("shard", None),
        P("shard", None),
        P("shard", None),
        P("shard", None),
        P("shard"),
        P("shard", None),
        P("shard", None),
        P("shard", None),
        P(("rep", "shard"), None, None),
    )
    return jax.shard_map(
        per_device,
        mesh=mesh,
        in_specs=placed,
        out_specs=(
            P(("rep", "shard"), None, None),
            P(("rep", "shard"), None, None),
            P("shard"),
            P("shard", None),
            P("shard", None),
            P("shard", None),
            P("shard", None),
            P("shard"),
            P("shard", None),
            P("shard", None),
            P("shard", None),
        ),
        check_vma=False,
    )
```

```python
from functools import partial

import jax
import jax.numpy as jnp
from jax import lax
from jax.experimental import pallas as pl
from jax.experimental.pallas import tpu as pltpu
from jax.sharding import PartitionSpec as P

QUERY_HEADS = 15
KEY_VALUE_HEADS = 5
HEAD_SIZE = 64


EPS = 1e-05
NEGATIVE = -1e30


def angles(documents, head_dim):
    segment_length = documents.shape[0]
    places = jnp.arange(segment_length, dtype=jnp.int32)
    begins = jnp.concatenate([jnp.ones((1,), dtype=jnp.bool_), documents[1:] != documents[:-1]])
    starting = lax.cummax(jnp.where(begins, places, 0), axis=0)
    offsets = (places - starting).astype(jnp.float32)
    rates = 10000.0 ** (-2.0 * jnp.arange(head_dim // 2).astype(jnp.float32) / head_dim)
    phases = offsets[:, None] * rates[None, :]
    return (jnp.cos(phases)[:, None, :], jnp.sin(phases)[:, None, :])


def bit_swap(count, bit):
    return [(i, i ^ bit) for i in range(count)]


def swap_rep(value, bit):
    return lax.ppermute(value, "rep", bit_swap(lax.axis_size("rep"), bit))


def swap_shard(value, bit):
    return lax.ppermute(value, "shard", bit_swap(lax.axis_size("shard"), bit))


def rep_bit(bit):
    return (lax.axis_index("rep") // bit) % 2


def place_pair(mine, other, bit, axis):
    low = jnp.concatenate([mine, other], axis=axis)
    high = jnp.concatenate([other, mine], axis=axis)
    return jnp.where(bit == 0, low, high)


def gather_rows(piece):
    shards = lax.axis_size("shard")
    rows, columns = piece.shape
    quarter = rows // 4
    core, side = rep_bit(1), rep_bit(2)
    part = lax.dynamic_slice_in_dim(piece, (core * 2 + side) * quarter, quarter, 0)
    held = part[None]
    bit = 1
    while bit < shards:
        held = jnp.concatenate([held, swap_shard(held, bit)], axis=0)
        bit *= 2
    others = held[1:]
    others = place_pair(others, swap_rep(others, 2), side, 1)
    others = place_pair(others, swap_rep(others, 1), core, 1)
    me = lax.axis_index("shard")
    if shards == 2:
        return place_pair(piece, others[0], me, 0)
    whole = jnp.zeros((shards, rows, columns), piece.dtype)
    whole = lax.dynamic_update_slice_in_dim(whole, piece[None], me, 0)
    for j in range(1, shards):
        whole = lax.dynamic_update_slice_in_dim(whole, others[j - 1][None], me ^ j, 0)
    return whole.reshape(shards * rows, columns)


def add_up(left, right):
    return (left.astype(jnp.float32) + right.astype(jnp.float32)).astype(jnp.bfloat16)


def halve(value, bit, axis, swap):
    half = value.shape[axis] // 2
    mine = lax.dynamic_slice_in_dim(value, bit * half, half, axis)
    theirs = lax.dynamic_slice_in_dim(value, (1 - bit) * half, half, axis)
    return add_up(mine, swap(theirs))


def halve_shard(value):
    bit = lax.axis_size("shard") // 2
    while bit:
        value = halve(
            value, (lax.axis_index("shard") // bit) % 2, 0, partial(swap_shard, bit=bit)
        )
        bit //= 2
    return value


def reduce_rows(grad, order, axes):
    shards = lax.axis_size("shard")
    rows, columns = grad.shape
    value = grad.astype(jnp.bfloat16).reshape(shards, rows // shards, columns)
    value = halve(value, rep_bit(1), axes[1], partial(swap_rep, bit=1))
    for step in order:
        if step == 0:
            value = halve_shard(value)
        else:
            value = halve(value, rep_bit(step), axes[step], partial(swap_rep, bit=step))
    bit = 8
    while bit < lax.axis_size("rep"):
        value = add_up(value, swap_rep(value, bit))
        bit *= 2
    for step in [s for s in reversed(order) if s] + [1]:
        value = place_pair(value, swap_rep(value, step), rep_bit(step), axes[step])
    return value[0].astype(jnp.float32)


def reduce_gains(grads):
    bit = 1
    while bit < lax.axis_size("rep"):
        grads = grads + swap_rep(grads, bit)
        bit *= 2
    bit = 1
    while bit < lax.axis_size("shard"):
        grads = grads + swap_shard(grads, bit)
        bit *= 2
    own = grads.shape[1] // lax.axis_size("shard")
    return lax.dynamic_slice_in_dim(grads, lax.axis_index("shard") * own, own, 1)


LANES = 128
BLOCK = 256
GROUP = QUERY_HEADS // KEY_VALUE_HEADS
SPAN = (GROUP + 2) * HEAD_SIZE
WIDE = -(-SPAN // LANES) * LANES
SCALE = HEAD_SIZE**-0.5
ROOM = 56 * 1024 * 1024


def dot(left, right):
    return jnp.dot(left, right, preferred_element_type=jnp.float32)


def dot_nt(left, right):
    return lax.dot_general(left, right, (((1,), (1,)), ((), ())), preferred_element_type=jnp.float32)


def dot_tn(left, right):
    return lax.dot_general(left, right, (((0,), (0,)), ((), ())), preferred_element_type=jnp.float32)


def lanes_of(shape):
    return lax.broadcasted_iota(jnp.int32, shape, len(shape) - 1)


def turn(pair, cosine, sine):
    lane = lanes_of(pair.shape) % HEAD_SIZE
    half = HEAD_SIZE // 2
    partner = jnp.where(
        lane < half, pltpu.roll(pair, LANES - half, 1), pltpu.roll(pair, half, 1)
    )
    return pair * cosine + partner * sine


def three_parts(column):
    high = column.astype(jnp.bfloat16)
    rest = column - high.astype(jnp.float32)
    middle = rest.astype(jnp.bfloat16)
    low = (rest - middle.astype(jnp.float32)).astype(jnp.bfloat16)
    return high, middle, low


def put_parts(base, column, first):
    lane = lanes_of(base.shape)
    for k, part in enumerate(three_parts(column)):
        base = jnp.where(lane == first + k, part.astype(jnp.float32), base)
    return base


def call(kernel, grid, in_specs, out_specs, out_shape, scratch=(), flops=0, prefetch=0, move=0):
    return pl.pallas_call(
        kernel,
        grid_spec=pltpu.PrefetchScalarGridSpec(
            num_scalar_prefetch=prefetch,
            grid=grid,
            in_specs=in_specs,
            out_specs=out_specs,
            scratch_shapes=list(scratch),
        ),
        out_shape=out_shape,
        compiler_params=pltpu.CompilerParams(
            dimension_semantics=("arbitrary",) * len(grid), vmem_limit_bytes=ROOM
        ),
        cost_estimate=pl.CostEstimate(flops=flops, bytes_accessed=move, transcendentals=0),
    )


def struct(shape, dtype):
    return jax.ShapeDtypeStruct(shape, dtype)


def whole(shape):
    return pl.BlockSpec(shape, lambda *_: (0,) * len(shape))


def window(at_ref, core, side, rows):
    half = rows // 2
    return core * half + side * (half - rows * 4 // 15)


def fill_rows(at_ref, whole_ref, own_ref, parts):
    rows, tall = own_ref.shape[0], parts[0].shape[0]
    x, side, core = at_ref[0], at_ref[1], at_ref[2]
    whole_ref[pl.ds(pl.multiple_of(x * rows, 16), rows), :] = own_ref[...]
    for k, part in enumerate(parts):
        c, y = core ^ (k // 2), side ^ (k % 2)
        start = (1 - x) * rows + window(at_ref, c, y, rows)
        whole_ref[pl.ds(pl.multiple_of(start, 16), tall), :] = part[...]


def project_kernel(
    at_ref, x_ref, doc_ref, cos_ref, sin_ref, gain_ref, own_ref, p0, p1, p2, p3,
    flip_ref, q_ref, k_ref, v_ref, in_ref, w_ref,
):
    step = pl.program_id(0)

    @pl.when(step == 0)
    def _():
        fill_rows(at_ref, w_ref, own_ref, (p0, p1, p2, p3))
        x = x_ref[...].astype(jnp.float32)
        inverse = lax.rsqrt(jnp.mean(x * x, axis=0, keepdims=True) + EPS)
        flip = (x * inverse * gain_ref[...]).astype(jnp.bfloat16)
        flip_ref[...] = flip
        in_ref[...] = flip.T

    y = dot(in_ref[...], w_ref[:, pl.ds(pl.multiple_of(step * WIDE, LANES), WIDE)])
    cosine, sine = cos_ref[...], sin_ref[...]
    first = turn(y[:, :LANES], cosine, sine)
    second = turn(y[:, LANES : 2 * LANES], cosine, sine)
    lane = lanes_of(first.shape)
    inner = lane < HEAD_SIZE
    doc = doc_ref[...]
    same = ((lane - HEAD_SIZE) == doc).astype(jnp.float32)
    q_ref[0] = jnp.where(inner, first * SCALE, same).astype(jnp.bfloat16)
    q_ref[1] = jnp.where(inner, pltpu.roll(first, HEAD_SIZE, 1) * SCALE, same).astype(jnp.bfloat16)
    q_ref[2] = jnp.where(inner, second * SCALE, same).astype(jnp.bfloat16)
    away = jnp.where(
        lane < HEAD_SIZE + 4,
        jnp.where((lane - HEAD_SIZE) == doc, 0.0, NEGATIVE),
        jnp.where(lane < HEAD_SIZE + 7, 1.0, 0.0),
    )
    k_ref[0] = jnp.where(inner, pltpu.roll(second, HEAD_SIZE, 1), away).astype(jnp.bfloat16)
    ones = jnp.where(lane < HEAD_SIZE + 3, 1.0, 0.0)
    v_ref[0] = jnp.where(inner, y[:, 2 * LANES :], ones).astype(jnp.bfloat16)


def project(at, x, documents, cosine, sine, gain, own, parts):
    width, rows = x.shape
    table = whole((rows, LANES))
    across = own.shape[1]
    return call(
        project_kernel,
        (KEY_VALUE_HEADS,),
        [whole((width, rows)), whole((rows, 1)), table, table, whole((width, 1)), whole(own.shape)]
        + [whole(parts[0].shape)] * 4,
        [
            whole((width, rows)),
            pl.BlockSpec((GROUP, rows, LANES), lambda g, a: (g, 0, 0)),
            pl.BlockSpec((1, rows, LANES), lambda g, a: (g, 0, 0)),
            pl.BlockSpec((1, rows, LANES), lambda g, a: (g, 0, 0)),
        ],
        [
            struct((width, rows), jnp.bfloat16),
            struct((QUERY_HEADS, rows, LANES), jnp.bfloat16),
            struct((KEY_VALUE_HEADS, rows, LANES), jnp.bfloat16),
            struct((KEY_VALUE_HEADS, rows, LANES), jnp.bfloat16),
        ],
        scratch=[pltpu.VMEM((rows, width), jnp.bfloat16), pltpu.VMEM((width, across), jnp.bfloat16)],
        flops=2 * rows * width * WIDE * KEY_VALUE_HEADS,
        prefetch=1,
        move=20_000_000,
    )(at, x, documents, cosine, sine, gain, own, *parts)


def attend_kernel(q_ref, k_ref, v_ref, o_ref, qb_ref):
    rows = q_ref.shape[1]
    deep = GROUP * BLOCK
    row = lax.broadcasted_iota(jnp.int32, (GROUP, BLOCK, BLOCK), 1).reshape(deep, BLOCK)
    below = lanes_of((deep, BLOCK)) <= row
    for i in range(rows // BLOCK):
        here = pl.ds(i * BLOCK, BLOCK)
        q = q_ref[:, here, :].reshape(deep, LANES)
        near = jnp.where(below, dot_nt(q, k_ref[0, here, :]), NEGATIVE)
        top = jnp.max(near, axis=-1, keepdims=True)
        if i:
            past = pl.ds(0, i * BLOCK)
            far = dot_nt(q, k_ref[0, past, :])
            top = jnp.maximum(top, jnp.max(far, axis=-1, keepdims=True))
            total = dot(jnp.exp(far - top).astype(jnp.bfloat16), v_ref[0, past, :])
            total += dot(jnp.exp(near - top).astype(jnp.bfloat16), v_ref[0, here, :])
        else:
            total = dot(jnp.exp(near - top).astype(jnp.bfloat16), v_ref[0, here, :])
        summed = total[:, HEAD_SIZE : HEAD_SIZE + 1]
        out = (total / summed).reshape(GROUP, BLOCK, LANES)
        o_ref[0, here, :] = jnp.concatenate(
            [out[h][:, :HEAD_SIZE] for h in range(GROUP)], axis=1
        ).astype(jnp.bfloat16)
        back = put_parts(q.astype(jnp.float32), -(top + jnp.log(summed)), HEAD_SIZE + 4)
        qb_ref[:, here, :] = back.astype(jnp.bfloat16).reshape(GROUP, BLOCK, LANES)


def attend(q, k, v, first, groups):
    rows = q.shape[1]
    one = pl.BlockSpec((1, rows, LANES), lambda g: (g + first, 0, 0))
    three = pl.BlockSpec((GROUP, rows, LANES), lambda g: (g + first, 0, 0))
    return call(
        attend_kernel,
        (groups,),
        [three, one, one],
        [
            pl.BlockSpec((1, rows, GROUP * HEAD_SIZE), lambda g: (g, 0, 0)),
            pl.BlockSpec((GROUP, rows, LANES), lambda g: (g, 0, 0)),
        ],
        [
            struct((groups, rows, GROUP * HEAD_SIZE), jnp.bfloat16),
            struct((groups * GROUP, rows, LANES), jnp.bfloat16),
        ],
        flops=2 * 4 * rows * rows * LANES * GROUP * groups,
        move=3_000_000 * groups,
    )(q, k, v)


def blend_kernel(
    at_ref, x_ref, dy_ref, o0_ref, o1_ref, gain_ref, own_ref, p0, p1, p2, p3,
    mid_ref, in_ref, flip_ref, back_ref, w_ref,
):
    @pl.when(pl.program_id(0) == 0)
    def _():
        fill_rows(at_ref, w_ref, own_ref, (p0, p1, p2, p3))

    total = x_ref[...].astype(jnp.float32).T
    deep = GROUP * HEAD_SIZE
    early = o0_ref.shape[0]
    for g in range(KEY_VALUE_HEADS):
        heads = o0_ref[g] if g < early else o1_ref[g - early]
        total += dot(heads, w_ref[pl.ds(g * deep, deep), :])
    mid_ref[...] = total
    inverse = lax.rsqrt(jnp.mean(total * total, axis=-1, keepdims=True) + EPS)
    entry = (total * inverse * gain_ref[...]).astype(jnp.bfloat16)
    in_ref[...] = entry
    flip_ref[...] = entry.T
    back_ref[...] = dy_ref[...].T


def head_specs(heads):
    deep = GROUP * HEAD_SIZE
    return [pl.BlockSpec((h.shape[0], BLOCK, deep), lambda i, a: (0, i, 0)) for h in heads]


def blend(at, x, dy, heads, gain, own, parts):
    width, rows = x.shape
    band = pl.BlockSpec((BLOCK, width), lambda i, a: (i, 0))
    side = pl.BlockSpec((width, BLOCK), lambda i, a: (0, i))
    return call(
        blend_kernel,
        (rows // BLOCK,),
        [side, side]
        + head_specs(heads)
        + [whole((1, width)), whole(own.shape)]
        + [whole(parts[0].shape)] * 4,
        [band, band, side, band],
        [
            struct((rows, width), jnp.float32),
            struct((rows, width), jnp.bfloat16),
            struct((width, rows), jnp.bfloat16),
            struct((rows, width), jnp.bfloat16),
        ],
        scratch=[pltpu.VMEM((2 * own.shape[0], width), jnp.bfloat16)],
        flops=2 * rows * width * width,
        prefetch=1,
        move=18_000_000,
    )(at, x, dy, *heads, gain, own, *parts)


def mix_kernel(
    at_ref, in_ref, flip_ref, dy_ref, back_ref, gate_own, g0, g1, up_own, u0, u1, down_own, d0, d1,
    y_ref, din_ref, gg_ref, gu_ref, gd_ref, gate_ref, up_ref, down_ref,
):
    step = pl.program_id(0)
    x, side = at_ref[0], at_ref[1]
    rows = gate_own.shape[0]
    mine = pl.ds(pl.multiple_of(x * rows, 16), rows)
    theirs = pl.ds(pl.multiple_of((1 - x) * rows, 16), rows)
    gate_ref[mine, :] = gate_own[...]
    up_ref[mine, :] = up_own[...]

    @pl.when(step == side)
    def _():
        gate_ref[theirs, :] = g0[...]
        up_ref[theirs, :] = u0[...]

    @pl.when(step != side)
    def _():
        gate_ref[theirs, :] = g1[...]
        up_ref[theirs, :] = u1[...]

    @pl.when(step == x)
    def _():
        down_ref[...] = down_own[...]

    @pl.when(step != x)
    def _():
        down_ref[pl.ds(pl.multiple_of(side * rows, 16), rows), :] = d0[...]
        down_ref[pl.ds(pl.multiple_of((1 - side) * rows, 16), rows), :] = d1[...]

    entry, dy = in_ref[...], dy_ref[...]
    w_gate, w_up, w_down = gate_ref[...], up_ref[...], down_ref[...]
    gate = dot(entry, w_gate)
    up = dot(entry, w_up)
    sigmoid = jax.nn.sigmoid(gate)
    active = gate * sigmoid
    hidden = (active * up).astype(jnp.bfloat16)
    hidden_grad = dot(dy, w_down)
    gate_grad = (hidden_grad * up * sigmoid * (1.0 + gate * (1.0 - sigmoid))).astype(jnp.bfloat16)
    up_grad = (hidden_grad * active).astype(jnp.bfloat16)
    gd_ref[0] = dot(back_ref[...], hidden).astype(jnp.bfloat16)
    gg_ref[...] = dot(flip_ref[...], gate_grad).astype(jnp.bfloat16)
    gu_ref[...] = dot(flip_ref[...], up_grad).astype(jnp.bfloat16)
    y = dot_nt(hidden, w_down)
    din = dot_nt(gate_grad, w_gate) + dot_nt(up_grad, w_up)

    @pl.when(step == 0)
    def _():
        y_ref[...] = y
        din_ref[...] = din

    @pl.when(step > 0)
    def _():
        y_ref[...] += y
        din_ref[...] += din


def mix(at, entry, flip, dy, back, gate, up, down):
    rows, width = entry.shape
    cut = gate[1].shape[1]
    full, turned = whole((rows, width)), whole((width, rows))
    side = pl.BlockSpec((width // 2, cut), lambda i, a: (0, 2 * i + a[3]))
    piece = whole((width // 2, cut))
    grad = pl.BlockSpec((width, cut), lambda i, a: (0, i))
    return call(
        mix_kernel,
        (2,),
        [full, turned, full, turned, side, piece, piece, side, piece, piece]
        + [pl.BlockSpec((width, cut), lambda i, a: (0, a[3])), piece, piece],
        [full, full, grad, grad, pl.BlockSpec((1, width, cut), lambda i, a: (i, 0, 0))],
        [
            struct((rows, width), jnp.float32),
            struct((rows, width), jnp.float32),
            struct((width, 2 * cut), jnp.bfloat16),
            struct((width, 2 * cut), jnp.bfloat16),
            struct((2, width, cut), jnp.bfloat16),
        ],
        scratch=[pltpu.VMEM((width, cut), jnp.bfloat16)] * 3,
        flops=2 * 9 * rows * width * cut * 2,
        prefetch=1,
        move=30_000_000,
    )(at, entry, flip, dy, back, *gate, *up, *down)


def middle_kernel(
    at_ref, mid_ref, y0_ref, y1_ref, d0_ref, d1_ref, dy_ref, o0_ref, o1_ref, gain_ref,
    own_ref, p0, p1, p2, p3, mixed_ref, grad_ref, do_ref, gain_out, w_out, w_total, w_ref,
):
    step = pl.program_id(0)

    @pl.when(step == 0)
    def _():
        fill_rows(at_ref, w_ref, own_ref, (p0, p1, p2, p3))

    middle = mid_ref[...]
    mixed_ref[...] = (middle + y0_ref[...] + y1_ref[...]).T.astype(jnp.bfloat16)
    inverse = lax.rsqrt(jnp.mean(middle * middle, axis=-1, keepdims=True) + EPS)
    normed = middle * inverse
    back = d0_ref[...] + d1_ref[...]
    product = back * normed
    weighted = product * gain_ref[...]
    mean = jnp.mean(weighted, axis=-1, keepdims=True)
    grad = dy_ref[...].astype(jnp.float32) + inverse * (back * gain_ref[...] - normed * mean)
    grad_ref[...] = grad
    branch = grad.astype(jnp.bfloat16)
    deep = GROUP * HEAD_SIZE
    partial_gain = jnp.sum(product, axis=0, keepdims=True)

    @pl.when(step == 0)
    def _():
        gain_out[...] = partial_gain

    @pl.when(step > 0)
    def _():
        gain_out[...] += partial_gain

    lane = lanes_of((BLOCK, LANES))
    for g in range(KEY_VALUE_HEADS):
        span = pl.ds(g * deep, deep)
        heads = o0_ref[g] if g < o0_ref.shape[0] else o1_ref[g - o0_ref.shape[0]]
        part = dot_tn(heads, branch)

        @pl.when(step == 0)
        def _(part=part, span=span):
            w_total[span, :] = part

        @pl.when(step > 0)
        def _(part=part, span=span):
            w_total[span, :] += part

        upstream = dot_nt(branch, w_ref[span, :]).astype(jnp.bfloat16).astype(jnp.float32)
        inner = upstream * heads.astype(jnp.float32)
        for h in range(GROUP):
            at = h * HEAD_SIZE
            delta = jnp.sum(inner[:, at : at + HEAD_SIZE], axis=-1, keepdims=True)
            own = upstream[:, at : at + HEAD_SIZE]
            wide = jnp.concatenate([own, jnp.zeros_like(own)], axis=1)
            do_ref[g * GROUP + h] = put_parts(wide, -delta, HEAD_SIZE).astype(jnp.bfloat16)

    @pl.when(step == pl.num_programs(0) - 1)
    def _():
        w_out[...] = w_total[...].astype(jnp.bfloat16)


def middle_back(at, middle, y0, y1, d0, d1, dy, heads, gain, own, parts):
    rows, width = middle.shape
    band = pl.BlockSpec((BLOCK, width), lambda i, a: (i, 0))
    square = (2 * own.shape[0], width)
    return call(
        middle_kernel,
        (rows // BLOCK,),
        [band] * 6
        + head_specs(heads)
        + [whole((1, width)), whole(own.shape)]
        + [whole(parts[0].shape)] * 4,
        [
            pl.BlockSpec((width, BLOCK), lambda i, a: (0, i)),
            band,
            pl.BlockSpec((QUERY_HEADS, BLOCK, LANES), lambda i, a: (0, i, 0)),
            whole((1, width)),
            whole(square),
        ],
        [
            struct((width, rows), jnp.bfloat16),
            struct((rows, width), jnp.float32),
            struct((QUERY_HEADS, rows, LANES), jnp.bfloat16),
            struct((1, width), jnp.float32),
            struct(square, jnp.bfloat16),
        ],
        scratch=[pltpu.VMEM(square, jnp.float32), pltpu.VMEM(square, jnp.bfloat16)],
        flops=2 * 2 * rows * width * width,
        prefetch=1,
        move=40_000_000,
    )(at, middle, y0, y1, d0, d1, dy, *heads, gain, own, *parts)


def attend_back_kernel(q_ref, k_ref, v_ref, do_ref, cos_ref, sin_ref, out_ref, dq_ref):
    rows = q_ref.shape[1]
    count = rows // BLOCK
    after = lax.broadcasted_iota(jnp.int32, (BLOCK, BLOCK), 0) <= lanes_of((BLOCK, BLOCK))
    key_grads, value_grads = [], []
    for j in range(count):
        here = pl.ds(j * BLOCK, BLOCK)
        k, v = k_ref[0, here, :], v_ref[0, here, :]
        dk = jnp.zeros((BLOCK, LANES), jnp.float32)
        dv = jnp.zeros((BLOCK, LANES), jnp.float32)
        for h in range(GROUP):
            for start, size in ((j * BLOCK, BLOCK), ((j + 1) * BLOCK, rows - (j + 1) * BLOCK)):
                if not size:
                    continue
                span = pl.ds(start, size)
                q, do = q_ref[h, span, :], do_ref[h, span, :]
                scores = dot_nt(k, q)
                if start == j * BLOCK:
                    scores = jnp.where(after, scores, NEGATIVE)
                probs = jnp.exp(scores)
                score_grad = (probs * dot_nt(v, do)).astype(jnp.bfloat16)
                dv += dot(probs.astype(jnp.bfloat16), do)
                dk += dot(score_grad, q)
                dq = dot_tn(score_grad, k)
                if j == 0:
                    dq_ref[h, span, :] = dq
                else:
                    dq_ref[h, span, :] += dq
        key_grads.append(dk)
        value_grads.append(dv)
    cosine, sine = cos_ref[...], -sin_ref[...]
    half = HEAD_SIZE
    parts = [turn(dq_ref[h] * SCALE, cosine, sine)[:, :half] for h in range(GROUP)]
    parts.append(turn(jnp.concatenate(key_grads, axis=0), cosine, sine)[:, :half])
    parts.append(jnp.concatenate(value_grads, axis=0)[:, :half])
    parts.append(jnp.zeros((rows, WIDE - SPAN), jnp.float32))
    out_ref[0] = jnp.concatenate(parts, axis=1).astype(jnp.bfloat16)


def attend_back(q, k, v, do, cosine, sine, first, begin, groups):
    rows = q.shape[1]
    one = pl.BlockSpec((1, rows, LANES), lambda g: (g + first, 0, 0))
    table = whole((rows, LANES))
    return call(
        attend_back_kernel,
        (groups,),
        [
            pl.BlockSpec((GROUP, rows, LANES), lambda g: (g + begin, 0, 0)),
            one,
            one,
            pl.BlockSpec((GROUP, rows, LANES), lambda g: (g + first, 0, 0)),
            table,
            table,
        ],
        pl.BlockSpec((1, rows, WIDE), lambda g: (g, 0, 0)),
        struct((groups, rows, WIDE), jnp.bfloat16),
        scratch=[pltpu.VMEM((GROUP, rows, LANES), jnp.float32)],
        flops=2 * 10 * rows * rows * LANES * GROUP * groups,
        move=3_000_000 * groups,
    )(q, k, v, do, cosine, sine)


def weight_kernel(flip_ref, *refs):
    flip = flip_ref[...]
    parts = []
    for ref in refs[:-1]:
        if len(ref.shape) == 2:
            parts.append(ref[...])
            continue
        for g in range(ref.shape[0]):
            parts.append(dot(flip, ref[g])[:, :SPAN].astype(jnp.bfloat16))
    refs[-1][...] = jnp.concatenate(parts, axis=1)


def weight_grads(flip, pieces):
    width, rows = flip.shape
    half = width // 2
    across = sum(p.shape[1] if p.ndim == 2 else p.shape[0] * SPAN for p in pieces)
    specs = [
        pl.BlockSpec((half, p.shape[1]), lambda i: (i, 0)) if p.ndim == 2 else whole(p.shape)
        for p in pieces
    ]
    return call(
        weight_kernel,
        (2,),
        [pl.BlockSpec((half, rows), lambda i: (i, 0))] + specs,
        pl.BlockSpec((half, across), lambda i: (i, 0)),
        struct((width, across), jnp.bfloat16),
        flops=2 * rows * width * across,
        move=10_000_000,
    )(flip, *pieces)


def finish_kernel(
    at_ref, x_ref, mid_ref, da_ref, db_ref, dc_ref, gain_ref, own_ref, p0, p1, p2, p3,
    out_ref, gain_out, w_ref,
):
    @pl.when(pl.program_id(0) == 0)
    def _():
        fill_rows(at_ref, w_ref, own_ref, (p0, p1, p2, p3))

    x = x_ref[...].astype(jnp.float32).T
    inverse = lax.rsqrt(jnp.mean(x * x, axis=-1, keepdims=True) + EPS)
    normed = x * inverse
    back = jnp.zeros_like(x)
    g = 0
    for ref in (da_ref, db_ref, dc_ref):
        for k in range(ref.shape[0]):
            back += dot_nt(ref[k], w_ref[:, pl.ds(g * WIDE, WIDE)])
            g += 1
    product = back * normed
    partial_gain = jnp.sum(product, axis=0, keepdims=True)

    @pl.when(pl.program_id(0) == 0)
    def _():
        gain_out[...] = partial_gain

    @pl.when(pl.program_id(0) > 0)
    def _():
        gain_out[...] += partial_gain

    mean = jnp.mean(product * gain_ref[...], axis=-1, keepdims=True)
    grad = mid_ref[...] + inverse * (back * gain_ref[...] - normed * mean)
    out_ref[...] = grad.T.astype(jnp.bfloat16)


def finish(at, x, middle_grad, backs, gain, own, parts):
    width, rows = x.shape
    side = pl.BlockSpec((width, BLOCK), lambda i, a: (0, i))
    return call(
        finish_kernel,
        (rows // BLOCK,),
        [side, pl.BlockSpec((BLOCK, width), lambda i, a: (i, 0))]
        + [pl.BlockSpec((b.shape[0], BLOCK, WIDE), lambda i, a: (0, i, 0)) for b in backs]
        + [whole((1, width)), whole(own.shape)]
        + [whole(parts[0].shape)] * 4,
        [side, whole((1, width))],
        [struct((width, rows), jnp.bfloat16), struct((1, width), jnp.float32)],
        scratch=[pltpu.VMEM((2 * own.shape[0], own.shape[1]), jnp.bfloat16)],
        flops=2 * rows * width * WIDE * KEY_VALUE_HEADS,
        prefetch=1,
        move=14_000_000,
    )(at, x, middle_grad, *backs, gain, own, *parts)


def widen_kernel(at_ref, mine_ref, other_ref, out_ref):
    core = at_ref[2]

    @pl.when(pl.program_id(0) == core)
    def _():
        out_ref[...] = mine_ref[0].astype(jnp.float32)

    @pl.when(pl.program_id(0) != core)
    def _():
        out_ref[...] = other_ref[0].astype(jnp.float32)


def widen(at, mine, other, order, spread):
    _, rows, columns = mine.shape

    def place(c, j, a):
        apart = {2: a[1] ^ (j // 2), 4: a[4] ^ (j % 2)}
        return (apart[order[0]] + 2 * apart[order[1]], 0, 0)

    if spread:
        shape = (2 * rows, 4 * columns)
        out = pl.BlockSpec((rows, columns), lambda c, j, a: (j % 2, 2 * (j // 2) + c))
    else:
        shape = (4 * rows, 2 * columns)
        out = pl.BlockSpec((rows, columns), lambda c, j, a: (j, c))
    return call(
        widen_kernel,
        (2, 4),
        [pl.BlockSpec((1, rows, columns), place)] * 2,
        out,
        struct(shape, jnp.float32),
        prefetch=1,
        move=10_000_000,
    )(at, mine, other)


def tie(value, *others):
    return lax.optimization_barrier((value, *others))[0]


def first_rows(w_query, w_key, w_value):
    rows = w_query.shape[0]
    pad = jnp.zeros((rows, WIDE - SPAN), w_query.dtype)
    deep = GROUP * HEAD_SIZE
    columns = []
    for g in range(KEY_VALUE_HEADS):
        columns.append(w_query[:, g * deep : (g + 1) * deep])
        columns.append(w_key[:, g * HEAD_SIZE : (g + 1) * HEAD_SIZE])
        columns.append(w_value[:, g * HEAD_SIZE : (g + 1) * HEAD_SIZE])
        columns.append(pad)
    return jnp.concatenate(columns, axis=1)


def spread_rows(received):
    beside = swap_rep(received, 2)
    return [received, beside, swap_rep(received, 1), swap_rep(beside, 1)]


def start_sum(send, keep):
    return add_up(keep, swap_rep(send, 1))


def one_step(value, step, axes):
    if step == 0:
        return halve_shard(value)
    return halve(value, rep_bit(step), axes[step], partial(swap_rep, bit=step))


def end_sum(value, order):
    bit = 8
    while bit < lax.axis_size("rep"):
        value = add_up(value, swap_rep(value, bit))
        bit *= 2
    return spread_sum(value, order)


def spread_sum(value, order):
    for step in order:
        value = jnp.concatenate([value, swap_rep(value, step)], axis=0)
    return value, swap_rep(value, 1)


def split_cores(grad):
    core = rep_bit(1)
    half = grad.shape[-1] // 2
    send = lax.dynamic_slice_in_dim(grad, (1 - core) * half, half, grad.ndim - 1)
    keep = lax.dynamic_slice_in_dim(grad, core * half, half, grad.ndim - 1)
    return send, keep


def per_device(
    tokens,
    segments,
    gain_attn,
    w_query,
    key_weight_matrix,
    value_weight_matrix,
    w_out,
    gain_mlp,
    w_gate,
    w_up,
    w_down,
    cotangent,
):
    shards = lax.axis_size("shard")
    fast = shards == 2
    rows, width = tokens.shape[1:]
    half = width // 2
    columns = QUERY_HEADS * HEAD_SIZE
    key_columns = KEY_VALUE_HEADS * HEAD_SIZE
    inner = w_gate.shape[1]
    cut = inner // 4
    x_t = tokens[0].T
    dy_t = cotangent[0].T
    tall = half * 4 // 15
    zero = jnp.int32(0)

    if fast:
        x, side, core, depth = lax.axis_index("shard"), rep_bit(2), rep_bit(1), rep_bit(4)
        x, side, core, depth = (v.astype(jnp.int32) for v in (x, side, core, depth))
        other = 1 - core
        start = window(None, core, side, half)
        narrow = partial(lax.dynamic_slice_in_dim, start_index=start, slice_size=tall, axis=0)
        part_first = first_rows(
            narrow(w_query), narrow(key_weight_matrix), narrow(value_weight_matrix)
        )
        came_first = swap_shard(part_first, 1)
        own_first = first_rows(w_query, key_weight_matrix, value_weight_matrix)
        gains = jnp.stack([gain_attn, gain_mlp]).astype(jnp.float32)
        gains = place_pair(gains, swap_shard(gains, 1), x, 1)
        column = (2 * side + other) * cut
        part_out = narrow(w_out)
        part_gate = lax.dynamic_slice_in_dim(w_gate, column, cut, 1)
        part_up = lax.dynamic_slice_in_dim(w_up, column, cut, 1)
        own_down = w_down.T
        part_down = lax.dynamic_slice(own_down, (side * half, other * cut), (half, cut))
        part_out, part_gate = tie(part_out, came_first), tie(part_gate, came_first)
        part_up, part_down = tie(part_up, came_first), tie(part_down, came_first)
        came_out, came_gate = swap_shard(part_out, 1), swap_shard(part_gate, 1)
        came_up, came_down = swap_shard(part_up, 1), swap_shard(part_down, 1)
        parts_first = spread_rows(came_first)
        parts_out = spread_rows(came_out)
        parts_gate, parts_up, parts_down = (
            spread_rows(came) for came in (came_gate, came_up, came_down)
        )
        own_out, own_gate, own_up = w_out, w_gate, w_up
    else:
        x = side = core = depth = zero
        other = 1 - core
        full = gather_rows(first_rows(w_query, key_weight_matrix, value_weight_matrix))
        full_out = gather_rows(w_out)
        starts = [half + window(None, c, y, half) for c in (0, 1) for y in (0, 1)]
        own_first, parts_first = full[:half], [full[s : s + tall] for s in starts]
        own_out, parts_out = full_out[:half], [full_out[s : s + tall] for s in starts]
        gains = gather_rows(jnp.pad(jnp.stack([gain_attn, gain_mlp], axis=1), ((0, 0), (0, 126))))
        gains = gains[:, :2].T.astype(jnp.float32)

        def cut_up(value):
            blocks = [value[half:, k * cut : (k + 1) * cut] for k in range(4)]
            return value[:half], [blocks[1], blocks[3], blocks[0], blocks[2]]

        own_gate, parts_gate = cut_up(gather_rows(w_gate))
        own_up, parts_up = cut_up(gather_rows(w_up))
        full_down = gather_rows(w_down).T
        own_down = full_down[:, : 2 * cut]
        parts_down = [
            full_down[r : r + half, (2 + c) * cut : (3 + c) * cut]
            for c in (1, 0)
            for r in (0, half)
        ]

    at = jnp.stack([x, side, core, core, depth])
    at_other = jnp.stack([x, side, core, other, depth])
    cosine, sine = angles(segments[0], HEAD_SIZE)
    cosine, sine = cosine[:, 0], sine[:, 0]
    cosine, sine = (
        jnp.concatenate([cosine] * 4, axis=1),
        jnp.concatenate([-sine, sine, -sine, sine], axis=1),
    )
    gain_one, gain_two = gains[:1], gains[1:]

    flip_one, q, k, v = project(
        at, x_t, segments[0][:, None], cosine, sine, gain_one.T, own_first, parts_first
    )
    if fast:
        q = tie(q, came_gate)
    heads0, back0 = attend(q, k, v, 0, 3)
    if fast:
        q = tie(q, heads0, came_up)
    heads1, back1 = attend(q, k, v, 3, 2)
    heads = (heads0, heads1)
    if fast:
        heads = (heads0, tie(heads1, came_down))
    middle, entry, flip, dy = blend(at, x_t, dy_t, heads, gain_two, own_out, parts_out)
    y0, d0, gate0, up0, down0 = mix(
        at_other, entry, flip, dy, dy_t,
        (own_gate, *parts_gate[:2]), (own_up, *parts_up[:2]), (own_down, *parts_down[:2]),
    )
    y1, d1, gate1, up1, down1 = mix(
        at, tie(entry, d0), flip, dy, dy_t,
        (own_gate, *parts_gate[2:]), (own_up, *parts_up[2:]), (own_down, *parts_down[2:]),
    )
    wide, tower = {2: 2, 4: 1}, {2: 1, 4: 1}
    if fast:
        cube = (2, half, 2 * cut)
        gate = start_sum(gate0.reshape(cube), gate1.reshape(cube))
        up = start_sum(up0.reshape(cube), up1.reshape(cube))
        down = start_sum(down0, down1)
        y1, gate, up, down = lax.optimization_barrier((y1, gate, up, down))
        gate, up, down = one_step(gate, 0, wide), one_step(up, 4, wide), one_step(down, 2, tower)
    mixed, middle_grad, do, grad_gain_two, grad_out = middle_back(
        at, middle, y0, y1, d0, d1, dy, heads, gain_two, own_out, parts_out
    )
    rope = (cosine, sine)
    backs0 = attend_back(back0, k, v, do, *rope, 0, 0, 1)
    near = weight_grads(flip_one, (grad_out, backs0))
    if fast:
        near = start_sum(*split_cores(near.reshape(2, half, -1)))
        do, gate, up, down = lax.optimization_barrier((do, gate, up, down))
        gate, up, down = one_step(gate, 2, wide), one_step(up, 2, wide), one_step(down, 0, tower)
    backs1 = attend_back(back0, k, v, do, *rope, 1, 1, 2)
    if fast:
        do, backs1, gate, up, down, near = lax.optimization_barrier(
            (do, backs1, gate, up, down, near)
        )
        gate, up, down = one_step(gate, 4, wide), one_step(up, 0, wide), one_step(down, 4, tower)
        near = one_step(near, 2, tower)
    backs2 = attend_back(back1, k, v, do, *rope, 3, 0, 2)
    if fast:
        backs1, gate, up, down, near = lax.optimization_barrier((backs1, gate, up, down, near))
        near = one_step(near, 4, tower)
    far = weight_grads(flip_one, (backs1, backs2))
    grad_tokens, grad_gain_one = finish(
        at, x_t, middle_grad, (backs0, backs1, backs2), gain_one, own_first, parts_first
    )
    gain_sums = reduce_gains(jnp.concatenate([grad_gain_one, grad_gain_two]))
    if fast:
        far = start_sum(*split_cores(far.reshape(2, half, -1)))
        near = one_step(near, 0, tower)
        far = one_step(one_step(one_step(far, 0, tower), 2, tower), 4, tower)
        sum_gate = widen(at, *end_sum(gate, (4, 2)), (4, 2), True)
        sum_up = widen(at, *end_sum(up, (2, 4)), (2, 4), True)
        sum_down = widen(at, *end_sum(down, (4, 2)), (4, 2), False).T
        sum_near = widen(at, *end_sum(near, (4, 2)), (4, 2), False)
        sum_far = widen(at, *end_sum(far, (4, 2)), (4, 2), False)
    else:
        def whole_grad(two, one):
            both = jnp.stack([one.reshape(width, 2, cut), two.reshape(width, 2, cut)], axis=2)
            return both.reshape(width, inner)

        across, upright = {1: 2, 2: 2, 4: 1}, {1: 1, 2: 1, 4: 1}
        sum_gate = reduce_rows(whole_grad(gate0, gate1), (0, 2, 4), across)
        sum_up = reduce_rows(whole_grad(up0, up1), (4, 2, 0), across)
        downs = [d.transpose(1, 0, 2) for d in (down0, down1)]
        sum_down = reduce_rows(whole_grad(*downs).T, (2, 0, 4), upright)
        sum_near = reduce_rows(near, (0, 2, 4), across)
        sum_far = reduce_rows(far, (0, 4, 2), across)
    tall_rows = sum_near.shape[0]
    groups = jnp.concatenate([sum_near[:, columns:], sum_far], axis=1)
    groups = groups.reshape(tall_rows, KEY_VALUE_HEADS, SPAN)
    deep = GROUP * HEAD_SIZE
    return (
        mixed.T[None],
        grad_tokens.T[None],
        gain_sums[0],
        groups[:, :, :deep].reshape(tall_rows, columns),
        groups[:, :, deep : deep + HEAD_SIZE].reshape(tall_rows, key_columns),
        groups[:, :, deep + HEAD_SIZE :].reshape(tall_rows, key_columns),
        sum_near[:, :columns],
        gain_sums[1],
        sum_gate,
        sum_up,
        sum_down,
    )


def solution(mesh):
    placed = (
        P(("rep", "shard"), None, None),
        P(("rep", "shard"), None),
        P("shard"),
        P("shard", None),
        P("shard", None),
        P("shard", None),
        P("shard", None),
        P("shard"),
        P("shard", None),
        P("shard", None),
        P("shard", None),
        P(("rep", "shard"), None, None),
    )
    return jax.shard_map(
        per_device,
        mesh=mesh,
        in_specs=placed,
        out_specs=(
            P(("rep", "shard"), None, None),
            P(("rep", "shard"), None, None),
            P("shard"),
            P("shard", None),
            P("shard", None),
            P("shard", None),
            P("shard", None),
            P("shard"),
            P("shard", None),
            P("shard", None),
            P("shard", None),
        ),
        check_vma=False,
    )
```

```python
from functools import partial

import jax
import jax.numpy as jnp
from jax import lax
from jax.experimental import pallas as pl
from jax.experimental.pallas import tpu as pltpu
from jax.sharding import PartitionSpec as P

QUERY_HEADS = 15
KEY_VALUE_HEADS = 5
HEAD_SIZE = 64


EPS = 1e-05
NEGATIVE = -1e30


def angles(documents, head_dim):
    segment_length = documents.shape[0]
    places = jnp.arange(segment_length, dtype=jnp.int32)
    begins = jnp.concatenate([jnp.ones((1,), dtype=jnp.bool_), documents[1:] != documents[:-1]])
    starting = lax.cummax(jnp.where(begins, places, 0), axis=0)
    offsets = (places - starting).astype(jnp.float32)
    rates = 10000.0 ** (-2.0 * jnp.arange(head_dim // 2).astype(jnp.float32) / head_dim)
    phases = offsets[:, None] * rates[None, :]
    return (jnp.cos(phases)[:, None, :], jnp.sin(phases)[:, None, :])


def bit_swap(count, bit):
    return [(i, i ^ bit) for i in range(count)]


def swap_rep(value, bit):
    return lax.ppermute(value, "rep", bit_swap(lax.axis_size("rep"), bit))


def swap_shard(value, bit):
    return lax.ppermute(value, "shard", bit_swap(lax.axis_size("shard"), bit))


def rep_bit(bit):
    return (lax.axis_index("rep") // bit) % 2


def place_pair(mine, other, bit, axis):
    low = jnp.concatenate([mine, other], axis=axis)
    high = jnp.concatenate([other, mine], axis=axis)
    return jnp.where(bit == 0, low, high)


def gather_rows(piece):
    shards = lax.axis_size("shard")
    rows, columns = piece.shape
    quarter = rows // 4
    core, side = rep_bit(1), rep_bit(2)
    part = lax.dynamic_slice_in_dim(piece, (core * 2 + side) * quarter, quarter, 0)
    held = part[None]
    bit = 1
    while bit < shards:
        held = jnp.concatenate([held, swap_shard(held, bit)], axis=0)
        bit *= 2
    others = held[1:]
    others = place_pair(others, swap_rep(others, 2), side, 1)
    others = place_pair(others, swap_rep(others, 1), core, 1)
    me = lax.axis_index("shard")
    if shards == 2:
        return place_pair(piece, others[0], me, 0)
    whole = jnp.zeros((shards, rows, columns), piece.dtype)
    whole = lax.dynamic_update_slice_in_dim(whole, piece[None], me, 0)
    for j in range(1, shards):
        whole = lax.dynamic_update_slice_in_dim(whole, others[j - 1][None], me ^ j, 0)
    return whole.reshape(shards * rows, columns)


def add_up(left, right):
    return (left.astype(jnp.float32) + right.astype(jnp.float32)).astype(jnp.bfloat16)


def halve(value, bit, axis, swap):
    half = value.shape[axis] // 2
    mine = lax.dynamic_slice_in_dim(value, bit * half, half, axis)
    theirs = lax.dynamic_slice_in_dim(value, (1 - bit) * half, half, axis)
    return add_up(mine, swap(theirs))


def halve_shard(value):
    bit = lax.axis_size("shard") // 2
    while bit:
        value = halve(
            value, (lax.axis_index("shard") // bit) % 2, 0, partial(swap_shard, bit=bit)
        )
        bit //= 2
    return value


def reduce_rows(grad, order, axes):
    shards = lax.axis_size("shard")
    rows, columns = grad.shape
    value = grad.astype(jnp.bfloat16).reshape(shards, rows // shards, columns)
    value = halve(value, rep_bit(1), axes[1], partial(swap_rep, bit=1))
    for step in order:
        if step == 0:
            value = halve_shard(value)
        else:
            value = halve(value, rep_bit(step), axes[step], partial(swap_rep, bit=step))
    bit = 8
    while bit < lax.axis_size("rep"):
        value = add_up(value, swap_rep(value, bit))
        bit *= 2
    for step in [s for s in reversed(order) if s] + [1]:
        value = place_pair(value, swap_rep(value, step), rep_bit(step), axes[step])
    return value[0].astype(jnp.float32)


def reduce_gains(grads):
    bit = 1
    while bit < lax.axis_size("rep"):
        grads = grads + swap_rep(grads, bit)
        bit *= 2
    bit = 1
    while bit < lax.axis_size("shard"):
        grads = grads + swap_shard(grads, bit)
        bit *= 2
    own = grads.shape[1] // lax.axis_size("shard")
    return lax.dynamic_slice_in_dim(grads, lax.axis_index("shard") * own, own, 1)


LANES = 128
BLOCK = 256
GROUP = QUERY_HEADS // KEY_VALUE_HEADS
SPAN = (GROUP + 2) * HEAD_SIZE
WIDE = -(-SPAN // LANES) * LANES
SCALE = HEAD_SIZE**-0.5
ROOM = 56 * 1024 * 1024


def dot(left, right):
    return jnp.dot(left, right, preferred_element_type=jnp.float32)


def dot_nt(left, right):
    return lax.dot_general(left, right, (((1,), (1,)), ((), ())), preferred_element_type=jnp.float32)


def dot_tn(left, right):
    return lax.dot_general(left, right, (((0,), (0,)), ((), ())), preferred_element_type=jnp.float32)


def lanes_of(shape):
    return lax.broadcasted_iota(jnp.int32, shape, len(shape) - 1)


def turn(pair, cosine, sine):
    lane = lanes_of(pair.shape) % HEAD_SIZE
    half = HEAD_SIZE // 2
    partner = jnp.where(
        lane < half, pltpu.roll(pair, LANES - half, 1), pltpu.roll(pair, half, 1)
    )
    return pair * cosine + partner * sine


def three_parts(column):
    high = column.astype(jnp.bfloat16)
    rest = column - high.astype(jnp.float32)
    middle = rest.astype(jnp.bfloat16)
    low = (rest - middle.astype(jnp.float32)).astype(jnp.bfloat16)
    return high, middle, low


def put_parts(base, column, first):
    lane = lanes_of(base.shape)
    for k, part in enumerate(three_parts(column)):
        base = jnp.where(lane == first + k, part.astype(jnp.float32), base)
    return base


def call(kernel, grid, in_specs, out_specs, out_shape, scratch=(), flops=0, prefetch=0, move=0):
    return pl.pallas_call(
        kernel,
        grid_spec=pltpu.PrefetchScalarGridSpec(
            num_scalar_prefetch=prefetch,
            grid=grid,
            in_specs=in_specs,
            out_specs=out_specs,
            scratch_shapes=list(scratch),
        ),
        out_shape=out_shape,
        compiler_params=pltpu.CompilerParams(
            dimension_semantics=("arbitrary",) * len(grid), vmem_limit_bytes=ROOM
        ),
        cost_estimate=pl.CostEstimate(flops=flops, bytes_accessed=move, transcendentals=0),
    )


def struct(shape, dtype):
    return jax.ShapeDtypeStruct(shape, dtype)


def whole(shape):
    return pl.BlockSpec(shape, lambda *_: (0,) * len(shape))


def window(at_ref, core, side, rows):
    half = rows // 2
    return core * half + side * (half - rows * 4 // 15)


def fill_rows(at_ref, whole_ref, own_ref, parts):
    rows, tall = own_ref.shape[0], parts[0].shape[0]
    x, side, core = at_ref[0], at_ref[1], at_ref[2]
    whole_ref[pl.ds(pl.multiple_of(x * rows, 16), rows), :] = own_ref[...]
    for k, part in enumerate(parts):
        c, y = core ^ (k // 2), side ^ (k % 2)
        start = (1 - x) * rows + window(at_ref, c, y, rows)
        whole_ref[pl.ds(pl.multiple_of(start, 16), tall), :] = part[...]


def project_kernel(
    at_ref, x_ref, doc_ref, cos_ref, sin_ref, gain_ref, wq_ref, wk_ref, wv_ref, p0, p1, p2, p3,
    flip_ref, q_ref, k_ref, v_ref, w_ref, in_ref, own_ref,
):
    step = pl.program_id(0)

    @pl.when(step == 0)
    def _():
        w_key, w_value = wk_ref[...].T, wv_ref[...].T
        deep = GROUP * HEAD_SIZE
        pad = jnp.zeros((own_ref.shape[0], WIDE - SPAN), jnp.bfloat16)
        columns = []
        for g in range(KEY_VALUE_HEADS):
            span = slice(g * HEAD_SIZE, (g + 1) * HEAD_SIZE)
            columns += [wq_ref[:, g * deep : (g + 1) * deep], w_key[:, span], w_value[:, span], pad]
        own_ref[...] = jnp.concatenate(columns, axis=1)
        fill_rows(at_ref, w_ref, own_ref, (p0, p1, p2, p3))
        x = x_ref[...].astype(jnp.float32)
        inverse = lax.rsqrt(jnp.mean(x * x, axis=0, keepdims=True) + EPS)
        flip = (x * inverse * gain_ref[...]).astype(jnp.bfloat16)
        flip_ref[...] = flip
        in_ref[...] = flip.T

    y = dot(in_ref[...], w_ref[:, pl.ds(pl.multiple_of(step * WIDE, LANES), WIDE)])
    cosine, sine = cos_ref[...], sin_ref[...]
    first = turn(y[:, :LANES], cosine, sine)
    second = turn(y[:, LANES : 2 * LANES], cosine, sine)
    lane = lanes_of(first.shape)
    inner = lane < HEAD_SIZE
    doc = doc_ref[...]
    same = ((lane - HEAD_SIZE) == doc).astype(jnp.float32)
    q_ref[0] = jnp.where(inner, first * SCALE, same).astype(jnp.bfloat16)
    q_ref[1] = jnp.where(inner, pltpu.roll(first, HEAD_SIZE, 1) * SCALE, same).astype(jnp.bfloat16)
    q_ref[2] = jnp.where(inner, second * SCALE, same).astype(jnp.bfloat16)
    away = jnp.where(
        lane < HEAD_SIZE + 4,
        jnp.where((lane - HEAD_SIZE) == doc, 0.0, NEGATIVE),
        jnp.where(lane < HEAD_SIZE + 7, 1.0, 0.0),
    )
    k_ref[0] = jnp.where(inner, pltpu.roll(second, HEAD_SIZE, 1), away).astype(jnp.bfloat16)
    ones = jnp.where(lane < HEAD_SIZE + 3, 1.0, 0.0)
    v_ref[0] = jnp.where(inner, y[:, 2 * LANES :], ones).astype(jnp.bfloat16)


def project(at, x, documents, cosine, sine, gain, own, parts):
    width, rows = x.shape
    table = whole((rows, LANES))
    across = parts[0].shape[1]
    return call(
        project_kernel,
        (KEY_VALUE_HEADS,),
        [whole((width, rows)), whole((rows, 1)), table, table, whole((width, 1))]
        + [whole(w.shape) for w in own]
        + [whole(parts[0].shape)] * 4,
        [
            whole((width, rows)),
            pl.BlockSpec((GROUP, rows, LANES), lambda g, a: (g, 0, 0)),
            pl.BlockSpec((1, rows, LANES), lambda g, a: (g, 0, 0)),
            pl.BlockSpec((1, rows, LANES), lambda g, a: (g, 0, 0)),
            whole((width, across)),
        ],
        [
            struct((width, rows), jnp.bfloat16),
            struct((QUERY_HEADS, rows, LANES), jnp.bfloat16),
            struct((KEY_VALUE_HEADS, rows, LANES), jnp.bfloat16),
            struct((KEY_VALUE_HEADS, rows, LANES), jnp.bfloat16),
            struct((width, across), jnp.bfloat16),
        ],
        scratch=[
            pltpu.VMEM((rows, width), jnp.bfloat16),
            pltpu.VMEM((width // 2, across), jnp.bfloat16),
        ],
        flops=2 * rows * width * WIDE * KEY_VALUE_HEADS,
        prefetch=1,
        move=20_000_000,
    )(at, x, documents, cosine, sine, gain, *own, *parts)


def attend_kernel(q_ref, k_ref, v_ref, o_ref, qb_ref):
    rows = q_ref.shape[1]
    deep = GROUP * BLOCK
    row = lax.broadcasted_iota(jnp.int32, (GROUP, BLOCK, BLOCK), 1).reshape(deep, BLOCK)
    below = lanes_of((deep, BLOCK)) <= row
    for i in range(rows // BLOCK):
        here = pl.ds(i * BLOCK, BLOCK)
        q = q_ref[:, here, :].reshape(deep, LANES)
        near = jnp.where(below, dot_nt(q, k_ref[0, here, :]), NEGATIVE)
        top = jnp.max(near, axis=-1, keepdims=True)
        if i:
            past = pl.ds(0, i * BLOCK)
            far = dot_nt(q, k_ref[0, past, :])
            top = jnp.maximum(top, jnp.max(far, axis=-1, keepdims=True))
            total = dot(jnp.exp(far - top).astype(jnp.bfloat16), v_ref[0, past, :])
            total += dot(jnp.exp(near - top).astype(jnp.bfloat16), v_ref[0, here, :])
        else:
            total = dot(jnp.exp(near - top).astype(jnp.bfloat16), v_ref[0, here, :])
        summed = total[:, HEAD_SIZE : HEAD_SIZE + 1]
        out = (total / summed).reshape(GROUP, BLOCK, LANES)
        o_ref[0, here, :] = jnp.concatenate(
            [out[h][:, :HEAD_SIZE] for h in range(GROUP)], axis=1
        ).astype(jnp.bfloat16)
        back = put_parts(q.astype(jnp.float32), -(top + jnp.log(summed)), HEAD_SIZE + 4)
        qb_ref[:, here, :] = back.astype(jnp.bfloat16).reshape(GROUP, BLOCK, LANES)


def attend(q, k, v, first, groups):
    rows = q.shape[1]
    one = pl.BlockSpec((1, rows, LANES), lambda g: (g + first, 0, 0))
    three = pl.BlockSpec((GROUP, rows, LANES), lambda g: (g + first, 0, 0))
    return call(
        attend_kernel,
        (groups,),
        [three, one, one],
        [
            pl.BlockSpec((1, rows, GROUP * HEAD_SIZE), lambda g: (g, 0, 0)),
            pl.BlockSpec((GROUP, rows, LANES), lambda g: (g, 0, 0)),
        ],
        [
            struct((groups, rows, GROUP * HEAD_SIZE), jnp.bfloat16),
            struct((groups * GROUP, rows, LANES), jnp.bfloat16),
        ],
        flops=2 * 4 * rows * rows * LANES * GROUP * groups,
        move=3_000_000 * groups,
    )(q, k, v)


def blend_kernel(
    at_ref, x_ref, dy_ref, o0_ref, o1_ref, gain_ref, own_ref, p0, p1, p2, p3,
    mid_ref, in_ref, flip_ref, back_ref, w_ref,
):
    @pl.when(pl.program_id(0) == 0)
    def _():
        fill_rows(at_ref, w_ref, own_ref, (p0, p1, p2, p3))

    total = x_ref[...].astype(jnp.float32).T
    deep = GROUP * HEAD_SIZE
    early = o0_ref.shape[0]
    for g in range(KEY_VALUE_HEADS):
        heads = o0_ref[g] if g < early else o1_ref[g - early]
        total += dot(heads, w_ref[pl.ds(g * deep, deep), :])
    mid_ref[...] = total
    inverse = lax.rsqrt(jnp.mean(total * total, axis=-1, keepdims=True) + EPS)
    entry = (total * inverse * gain_ref[...]).astype(jnp.bfloat16)
    in_ref[...] = entry
    flip_ref[...] = entry.T
    back_ref[...] = dy_ref[...].T


def head_specs(heads):
    deep = GROUP * HEAD_SIZE
    return [pl.BlockSpec((h.shape[0], BLOCK, deep), lambda i, a: (0, i, 0)) for h in heads]


def blend(at, x, dy, heads, gain, own, parts):
    width, rows = x.shape
    band = pl.BlockSpec((BLOCK, width), lambda i, a: (i, 0))
    side = pl.BlockSpec((width, BLOCK), lambda i, a: (0, i))
    return call(
        blend_kernel,
        (rows // BLOCK,),
        [side, side]
        + head_specs(heads)
        + [whole((1, width)), whole(own.shape)]
        + [whole(parts[0].shape)] * 4,
        [band, band, side, band],
        [
            struct((rows, width), jnp.float32),
            struct((rows, width), jnp.bfloat16),
            struct((width, rows), jnp.bfloat16),
            struct((rows, width), jnp.bfloat16),
        ],
        scratch=[pltpu.VMEM((2 * own.shape[0], width), jnp.bfloat16)],
        flops=2 * rows * width * width,
        prefetch=1,
        move=18_000_000,
    )(at, x, dy, *heads, gain, own, *parts)


def mix_kernel(
    at_ref, in_ref, flip_ref, dy_ref, back_ref, gate_own, g0, g1, up_own, u0, u1, down_own, d0, d1,
    y_ref, din_ref, gg_ref, gu_ref, gd_ref, gate_ref, up_ref, down_ref,
):
    step = pl.program_id(0)
    x, side = at_ref[0], at_ref[1]
    rows = gate_own.shape[0]
    mine = pl.ds(pl.multiple_of(x * rows, 16), rows)
    theirs = pl.ds(pl.multiple_of((1 - x) * rows, 16), rows)
    gate_ref[mine, :] = gate_own[...]
    up_ref[mine, :] = up_own[...]

    @pl.when(step == side)
    def _():
        gate_ref[theirs, :] = g0[...]
        up_ref[theirs, :] = u0[...]

    @pl.when(step != side)
    def _():
        gate_ref[theirs, :] = g1[...]
        up_ref[theirs, :] = u1[...]

    @pl.when(step == x)
    def _():
        down_ref[...] = down_own[...]

    @pl.when(step != x)
    def _():
        down_ref[pl.ds(pl.multiple_of(side * rows, 16), rows), :] = d0[...]
        down_ref[pl.ds(pl.multiple_of((1 - side) * rows, 16), rows), :] = d1[...]

    entry, dy = in_ref[...], dy_ref[...]
    w_gate, w_up, w_down = gate_ref[...], up_ref[...], down_ref[...]
    gate = dot(entry, w_gate)
    up = dot(entry, w_up)
    sigmoid = jax.nn.sigmoid(gate)
    active = gate * sigmoid
    hidden = (active * up).astype(jnp.bfloat16)
    hidden_grad = dot(dy, w_down)
    gate_grad = (hidden_grad * up * sigmoid * (1.0 + gate * (1.0 - sigmoid))).astype(jnp.bfloat16)
    up_grad = (hidden_grad * active).astype(jnp.bfloat16)
    gd_ref[0] = dot(back_ref[...], hidden).astype(jnp.bfloat16)
    gg_ref[...] = dot(flip_ref[...], gate_grad).astype(jnp.bfloat16)
    gu_ref[...] = dot(flip_ref[...], up_grad).astype(jnp.bfloat16)
    y = dot_nt(hidden, w_down)
    din = dot_nt(gate_grad, w_gate) + dot_nt(up_grad, w_up)

    @pl.when(step == 0)
    def _():
        y_ref[...] = y
        din_ref[...] = din

    @pl.when(step > 0)
    def _():
        y_ref[...] += y
        din_ref[...] += din


def mix(at, entry, flip, dy, back, gate, up, down):
    rows, width = entry.shape
    cut = gate[1].shape[1]
    full, turned = whole((rows, width)), whole((width, rows))
    side = pl.BlockSpec((width // 2, cut), lambda i, a: (0, 2 * i + a[3]))
    piece = whole((width // 2, cut))
    grad = pl.BlockSpec((width, cut), lambda i, a: (0, i))
    return call(
        mix_kernel,
        (2,),
        [full, turned, full, turned, side, piece, piece, side, piece, piece]
        + [pl.BlockSpec((width, cut), lambda i, a: (0, a[3])), piece, piece],
        [full, full, grad, grad, pl.BlockSpec((1, width, cut), lambda i, a: (i, 0, 0))],
        [
            struct((rows, width), jnp.float32),
            struct((rows, width), jnp.float32),
            struct((width, 2 * cut), jnp.bfloat16),
            struct((width, 2 * cut), jnp.bfloat16),
            struct((2, width, cut), jnp.bfloat16),
        ],
        scratch=[pltpu.VMEM((width, cut), jnp.bfloat16)] * 3,
        flops=2 * 9 * rows * width * cut * 2,
        prefetch=1,
        move=30_000_000,
    )(at, entry, flip, dy, back, *gate, *up, *down)


def middle_kernel(
    at_ref, mid_ref, y0_ref, y1_ref, d0_ref, d1_ref, dy_ref, o0_ref, o1_ref, gain_ref,
    own_ref, p0, p1, p2, p3, mixed_ref, grad_ref, branch_ref, do_ref, gain_out, w_ref,
):
    step = pl.program_id(0)

    @pl.when(step == 0)
    def _():
        fill_rows(at_ref, w_ref, own_ref, (p0, p1, p2, p3))
        gain_out[...] = jnp.zeros_like(gain_out)

    middle = mid_ref[...]
    mixed_ref[...] = (middle + y0_ref[...] + y1_ref[...]).astype(jnp.bfloat16).T
    inverse = lax.rsqrt(jnp.mean(middle * middle, axis=-1, keepdims=True) + EPS)
    normed = middle * inverse
    back = d0_ref[...] + d1_ref[...]
    product = back * normed
    mean = jnp.mean(product * gain_ref[...], axis=-1, keepdims=True)
    grad = dy_ref[...].astype(jnp.float32) + inverse * (back * gain_ref[...] - normed * mean)
    grad_ref[...] = grad
    branch = grad.astype(jnp.bfloat16)
    branch_ref[...] = branch
    gain_out[...] += jnp.sum(product, axis=0, keepdims=True)
    deep = GROUP * HEAD_SIZE
    lane = lanes_of((BLOCK, LANES))
    inner = lane < HEAD_SIZE
    for g in range(KEY_VALUE_HEADS):
        heads = o0_ref[g] if g < o0_ref.shape[0] else o1_ref[g - o0_ref.shape[0]]
        upstream = dot_nt(branch, w_ref[pl.ds(g * deep, deep), :]).astype(jnp.bfloat16)
        upstream = upstream.astype(jnp.float32)
        both = upstream * heads.astype(jnp.float32)
        pair, pair_both = upstream[:, :LANES], both[:, :LANES]
        wide = (pair, pltpu.roll(pair, HEAD_SIZE, 1), upstream[:, LANES:])
        sums = (
            jnp.sum(jnp.where(inner, pair_both, 0.0), axis=-1, keepdims=True),
            jnp.sum(jnp.where(inner, 0.0, pair_both), axis=-1, keepdims=True),
            jnp.sum(both[:, LANES:], axis=-1, keepdims=True),
        )
        for h in range(GROUP):
            delta = -sums[h]
            high = delta.astype(jnp.bfloat16).astype(jnp.float32)
            low = delta - high
            own = wide[h]
            if own.shape[1] < LANES:
                own = jnp.concatenate([own, jnp.zeros_like(own)], axis=1)
            rest = jnp.where(lane == HEAD_SIZE, high, jnp.where(lane == HEAD_SIZE + 1, low, 0.0))
            do_ref[g * GROUP + h] = jnp.where(inner, own, rest).astype(jnp.bfloat16)


def middle_back(at, middle, y0, y1, d0, d1, dy, heads, gain, own, parts):
    rows, width = middle.shape
    band = pl.BlockSpec((BLOCK, width), lambda i, a: (i, 0))
    return call(
        middle_kernel,
        (rows // BLOCK,),
        [band] * 6
        + head_specs(heads)
        + [whole((1, width)), whole(own.shape)]
        + [whole(parts[0].shape)] * 4,
        [
            pl.BlockSpec((width, BLOCK), lambda i, a: (0, i)),
            band,
            band,
            pl.BlockSpec((QUERY_HEADS, BLOCK, LANES), lambda i, a: (0, i, 0)),
            whole((1, width)),
        ],
        [
            struct((width, rows), jnp.bfloat16),
            struct((rows, width), jnp.float32),
            struct((rows, width), jnp.bfloat16),
            struct((QUERY_HEADS, rows, LANES), jnp.bfloat16),
            struct((1, width), jnp.float32),
        ],
        scratch=[pltpu.VMEM((2 * own.shape[0], width), jnp.bfloat16)],
        flops=2 * rows * width * width,
        prefetch=1,
        move=30_000_000,
    )(at, middle, y0, y1, d0, d1, dy, *heads, gain, own, *parts)


def attend_back_kernel(q_ref, k_ref, v_ref, do_ref, cos_ref, sin_ref, out_ref, dq_ref):
    rows = q_ref.shape[1]
    count = rows // BLOCK
    after = lax.broadcasted_iota(jnp.int32, (BLOCK, BLOCK), 0) <= lanes_of((BLOCK, BLOCK))
    key_grads, value_grads = [], []
    for j in range(count):
        here = pl.ds(j * BLOCK, BLOCK)
        k, v = k_ref[0, here, :], v_ref[0, here, :]
        dk = jnp.zeros((BLOCK, LANES), jnp.float32)
        dv = jnp.zeros((BLOCK, LANES), jnp.float32)
        for h in range(GROUP):
            for start, size in ((j * BLOCK, BLOCK), ((j + 1) * BLOCK, rows - (j + 1) * BLOCK)):
                if not size:
                    continue
                span = pl.ds(start, size)
                q, do = q_ref[h, span, :], do_ref[h, span, :]
                scores = dot_nt(k, q)
                if start == j * BLOCK:
                    scores = jnp.where(after, scores, NEGATIVE)
                probs = jnp.exp(scores)
                score_grad = (probs * dot_nt(v, do)).astype(jnp.bfloat16)
                dv += dot(probs.astype(jnp.bfloat16), do)
                dk += dot(score_grad, q)
                dq = dot_tn(score_grad, k)
                if j == 0:
                    dq_ref[h, span, :] = dq
                else:
                    dq_ref[h, span, :] += dq
        key_grads.append(dk)
        value_grads.append(dv)
    cosine, sine = cos_ref[...], -sin_ref[...]
    half = HEAD_SIZE
    parts = [turn(dq_ref[h] * SCALE, cosine, sine)[:, :half] for h in range(GROUP)]
    parts.append(turn(jnp.concatenate(key_grads, axis=0), cosine, sine)[:, :half])
    parts.append(jnp.concatenate(value_grads, axis=0)[:, :half])
    parts.append(jnp.zeros((rows, WIDE - SPAN), jnp.float32))
    out_ref[0] = jnp.concatenate(parts, axis=1).astype(jnp.bfloat16)


def attend_back(q, k, v, do, cosine, sine, first, begin, groups):
    rows = q.shape[1]
    one = pl.BlockSpec((1, rows, LANES), lambda g: (g + first, 0, 0))
    table = whole((rows, LANES))
    return call(
        attend_back_kernel,
        (groups,),
        [
            pl.BlockSpec((GROUP, rows, LANES), lambda g: (g + begin, 0, 0)),
            one,
            one,
            pl.BlockSpec((GROUP, rows, LANES), lambda g: (g + first, 0, 0)),
            table,
            table,
        ],
        pl.BlockSpec((1, rows, WIDE), lambda g: (g, 0, 0)),
        struct((groups, rows, WIDE), jnp.bfloat16),
        scratch=[pltpu.VMEM((GROUP, rows, LANES), jnp.float32)],
        flops=2 * 10 * rows * rows * LANES * GROUP * groups,
        move=3_000_000 * groups,
    )(q, k, v, do, cosine, sine)


def weight_kernel(flip_ref, *refs):
    flip = flip_ref[...]
    parts = [dot(flip, ref[0])[:, :SPAN].astype(jnp.bfloat16) for ref in refs[:-1]]
    refs[-1][...] = jnp.concatenate(parts, axis=1)


def weight_grads(flip, backs):
    width, rows = flip.shape
    half = width // 2
    across = len(backs) * SPAN
    return call(
        weight_kernel,
        (2,),
        [pl.BlockSpec((half, rows), lambda i: (i, 0))] + [whole(b.shape) for b in backs],
        pl.BlockSpec((half, across), lambda i: (i, 0)),
        struct((width, across), jnp.bfloat16),
        flops=2 * rows * width * across,
        move=10_000_000,
    )(flip, *backs)


def near_kernel(flip_ref, back_ref, branch_ref, o0_ref, o1_ref, out_ref):
    deep = GROUP * HEAD_SIZE
    branch = branch_ref[...]
    for g in range(KEY_VALUE_HEADS):
        heads = o0_ref[g] if g < o0_ref.shape[0] else o1_ref[g - o0_ref.shape[0]]
        span = pl.ds(g * deep, deep)
        left = dot_tn(heads, branch)
        right = dot(flip_ref[span, :], back_ref[0])[:, :SPAN]
        out_ref[span, :] = jnp.concatenate([left, right], axis=1).astype(jnp.bfloat16)


def near_grads(flip, back, branch, heads):
    width, rows = flip.shape
    args = (flip, back, branch, *heads)
    return call(
        near_kernel,
        (1,),
        [whole(a.shape) for a in args],
        whole((width, width + SPAN)),
        struct((width, width + SPAN), jnp.bfloat16),
        flops=2 * rows * width * (width + SPAN),
        move=12_000_000,
    )(*args)


def finish_kernel(x_ref, mid_ref, *refs):
    gain_ref, w_ref, out_ref, gain_out = refs[KEY_VALUE_HEADS:]
    x = x_ref[...].astype(jnp.float32).T
    inverse = lax.rsqrt(jnp.mean(x * x, axis=-1, keepdims=True) + EPS)
    normed = x * inverse
    back = jnp.zeros_like(x)
    for g in range(KEY_VALUE_HEADS):
        back += dot_nt(refs[g][0], w_ref[:, pl.ds(g * WIDE, WIDE)])
    product = back * normed

    @pl.when(pl.program_id(0) == 0)
    def _():
        gain_out[...] = jnp.zeros_like(gain_out)

    gain_out[...] += jnp.sum(product, axis=0, keepdims=True)
    mean = jnp.mean(product * gain_ref[...], axis=-1, keepdims=True)
    grad = mid_ref[...] + inverse * (back * gain_ref[...] - normed * mean)
    out_ref[...] = grad.astype(jnp.bfloat16).T


def finish(x, middle_grad, backs, gain, w_first):
    width, rows = x.shape
    side = pl.BlockSpec((width, BLOCK), lambda i: (0, i))
    return call(
        finish_kernel,
        (rows // BLOCK,),
        [side, pl.BlockSpec((BLOCK, width), lambda i: (i, 0))]
        + [pl.BlockSpec((1, BLOCK, WIDE), lambda i: (0, i, 0)) for _ in backs]
        + [whole((1, width)), whole(w_first.shape)],
        [side, whole((1, width))],
        [struct((width, rows), jnp.bfloat16), struct((1, width), jnp.float32)],
        flops=2 * rows * width * WIDE * KEY_VALUE_HEADS,
        move=14_000_000,
    )(x, middle_grad, *backs, gain, w_first)


def widen_kernel(at_ref, mine_ref, other_ref, out_ref):
    cut = mine_ref.shape[2]
    mine, other = mine_ref[0].astype(jnp.float32), other_ref[0].astype(jnp.float32)

    @pl.when(at_ref[2] == 0)
    def _():
        out_ref[:, :cut] = mine
        out_ref[:, cut:] = other

    @pl.when(at_ref[2] != 0)
    def _():
        out_ref[:, :cut] = other
        out_ref[:, cut:] = mine


def came_at(at, j, order):
    apart = {2: at[1] ^ (j // 2), 4: at[4] ^ (j % 2)}
    return apart[order[0]] + 2 * apart[order[1]]


def widen(at, mine, other, order, spread):
    _, rows, columns = mine.shape
    if spread:
        shape = (2 * rows, 4 * columns)
        out = pl.BlockSpec((rows, 2 * columns), lambda j, a: (j % 2, j // 2))
    else:
        shape = (4 * rows, 2 * columns)
        out = pl.BlockSpec((rows, 2 * columns), lambda j, a: (j, 0))
    return call(
        widen_kernel,
        (4,),
        [pl.BlockSpec((1, rows, columns), lambda j, a: (came_at(a, j, order), 0, 0))] * 2,
        out,
        struct(shape, jnp.float32),
        prefetch=1,
        move=10_000_000,
    )(at, mine, other)


def unpack_kernel(
    at_ref, near0, near1, mid0, mid1, far0, far1, q_ref, k_ref, v_ref, out_ref,
    near_ref, mid_ref, far_ref,
):
    core, side = at_ref[2], at_ref[1]
    rows, columns = near0.shape[1:]
    for j in range(4):
        at = came_at(at_ref, j, (4, 2))
        mine, other = near0[at].astype(jnp.float32), near1[at].astype(jnp.float32)
        left, right = jnp.where(core == 0, mine, other), jnp.where(core == 0, other, mine)
        near_ref[j * rows : (j + 1) * rows, :] = jnp.concatenate([left, right], axis=1)
    for mine_ref, other_ref, into in ((mid0, mid1, mid_ref), (far0, far1, far_ref)):
        for c in range(2):
            for y in range(2):
                at = y ^ side
                mine, other = mine_ref[at].astype(jnp.float32), other_ref[at].astype(jnp.float32)
                start = (2 * c + y) * mine.shape[0]
                into[start : start + mine.shape[0], :] = jnp.where(core == c, mine, other)
    near, mid, far = near_ref[...], mid_ref[...], far_ref[...]
    deep = GROUP * HEAD_SIZE
    split = near.shape[1] - SPAN
    groups = [near[:, split:], mid[:, :SPAN], mid[:, SPAN:], far[:, :SPAN], far[:, SPAN:]]
    out_ref[...] = near[:, :split]
    q_ref[...] = jnp.concatenate([g[:, :deep] for g in groups], axis=1)
    k_ref[...] = jnp.concatenate([g[:, deep : deep + HEAD_SIZE] for g in groups], axis=1).T
    v_ref[...] = jnp.concatenate([g[:, deep + HEAD_SIZE :] for g in groups], axis=1).T


def unpack(at, near, mid, far):
    _, rows, columns = near[0].shape
    args = (*near, *mid, *far)
    tall = 4 * rows
    key_columns = KEY_VALUE_HEADS * HEAD_SIZE
    shapes = [
        (tall, QUERY_HEADS * HEAD_SIZE),
        (key_columns, tall),
        (key_columns, tall),
        (tall, 2 * columns - SPAN),
    ]
    return call(
        unpack_kernel,
        (1,),
        [whole(a.shape) for a in args],
        [whole(shape) for shape in shapes],
        [struct(shape, jnp.float32) for shape in shapes],
        scratch=[
            pltpu.VMEM((tall, 2 * columns), jnp.float32),
            pltpu.VMEM((tall, 2 * SPAN), jnp.float32),
            pltpu.VMEM((tall, 2 * SPAN), jnp.float32),
        ],
        prefetch=1,
        move=8_000_000,
    )(at, *args)


def tie(value, *others):
    return lax.optimization_barrier((value, *others))[0]


def first_rows(w_query, w_key, w_value):
    rows = w_query.shape[0]
    pad = jnp.zeros((rows, WIDE - SPAN), w_query.dtype)
    deep = GROUP * HEAD_SIZE
    columns = []
    for g in range(KEY_VALUE_HEADS):
        columns.append(w_query[:, g * deep : (g + 1) * deep])
        columns.append(w_key[:, g * HEAD_SIZE : (g + 1) * HEAD_SIZE])
        columns.append(w_value[:, g * HEAD_SIZE : (g + 1) * HEAD_SIZE])
        columns.append(pad)
    return jnp.concatenate(columns, axis=1)


def spread_rows(received):
    beside = swap_rep(received, 2)
    return [received, beside, swap_rep(received, 1), swap_rep(beside, 1)]


def start_sum(send, keep):
    return add_up(keep, swap_rep(send, 1))


def one_step(value, step, axes):
    if step == 0:
        return halve_shard(value)
    return halve(value, rep_bit(step), axes[step], partial(swap_rep, bit=step))


def over_z(value):
    bit = 8
    while bit < lax.axis_size("rep"):
        value = add_up(value, swap_rep(value, bit))
        bit *= 2
    return value


def back_step(value, step):
    return jnp.concatenate([value, swap_rep(value, step)], axis=0)


def split_cores(grad, axis):
    core = rep_bit(1)
    half = grad.shape[axis] // 2
    send = lax.dynamic_slice_in_dim(grad, (1 - core) * half, half, axis)
    keep = lax.dynamic_slice_in_dim(grad, core * half, half, axis)
    return send, keep


def per_device(
    tokens,
    segments,
    gain_attn,
    w_query,
    key_weight_matrix,
    value_weight_matrix,
    w_out,
    gain_mlp,
    w_gate,
    w_up,
    w_down,
    cotangent,
):
    shards = lax.axis_size("shard")
    fast = shards == 2
    rows, width = tokens.shape[1:]
    half = width // 2
    columns = QUERY_HEADS * HEAD_SIZE
    key_columns = KEY_VALUE_HEADS * HEAD_SIZE
    inner = w_gate.shape[1]
    cut = inner // 4
    x_t = tokens[0].T
    dy_t = cotangent[0].T
    tall = half * 4 // 15
    zero = jnp.int32(0)

    if fast:
        x, side, core, depth = lax.axis_index("shard"), rep_bit(2), rep_bit(1), rep_bit(4)
        x, side, core, depth = (v.astype(jnp.int32) for v in (x, side, core, depth))
        other = 1 - core
        start = window(None, core, side, half)
        narrow = partial(lax.dynamic_slice_in_dim, start_index=start, slice_size=tall, axis=0)
        part_first = first_rows(
            narrow(w_query), narrow(key_weight_matrix), narrow(value_weight_matrix)
        )
        came_first = swap_shard(part_first, 1)
        own_first = (w_query, key_weight_matrix.T, value_weight_matrix.T)
        gains = tie(jnp.stack([gain_attn, gain_mlp]).astype(jnp.float32), part_first)
        gains = place_pair(gains, swap_shard(gains, 1), x, 1)
        column = (2 * side + other) * cut
        part_out = narrow(w_out)
        part_gate = lax.dynamic_slice_in_dim(w_gate, column, cut, 1)
        part_up = lax.dynamic_slice_in_dim(w_up, column, cut, 1)
        own_down = w_down.T
        part_down = lax.dynamic_slice(own_down, (side * half, other * cut), (half, cut))
        part_out, part_gate = tie(part_out, came_first), tie(part_gate, came_first)
        part_up, part_down = tie(part_up, came_first), tie(part_down, came_first)
        came_out, came_gate = swap_shard(part_out, 1), swap_shard(part_gate, 1)
        came_up, came_down = swap_shard(part_up, 1), swap_shard(part_down, 1)
        parts_first = spread_rows(came_first)
        parts_out = spread_rows(came_out)
        parts_gate, parts_up, parts_down = (
            spread_rows(came) for came in (came_gate, came_up, came_down)
        )
        own_out, own_gate, own_up = w_out, w_gate, w_up
    else:
        x = side = core = depth = zero
        other = 1 - core
        full_first = [gather_rows(w) for w in (w_query, key_weight_matrix, value_weight_matrix)]
        full_out = gather_rows(w_out)
        starts = [half + window(None, c, y, half) for c in (0, 1) for y in (0, 1)]
        own_first = (full_first[0][:half], full_first[1][:half].T, full_first[2][:half].T)
        parts_first = [first_rows(*(w[s : s + tall] for w in full_first)) for s in starts]
        own_out, parts_out = full_out[:half], [full_out[s : s + tall] for s in starts]
        gains = gather_rows(jnp.pad(jnp.stack([gain_attn, gain_mlp], axis=1), ((0, 0), (0, 126))))
        gains = gains[:, :2].T.astype(jnp.float32)

        def cut_up(value):
            blocks = [value[half:, k * cut : (k + 1) * cut] for k in range(4)]
            return value[:half], [blocks[1], blocks[3], blocks[0], blocks[2]]

        own_gate, parts_gate = cut_up(gather_rows(w_gate))
        own_up, parts_up = cut_up(gather_rows(w_up))
        full_down = gather_rows(w_down).T
        own_down = full_down[:, : 2 * cut]
        parts_down = [
            full_down[r : r + half, (2 + c) * cut : (3 + c) * cut]
            for c in (1, 0)
            for r in (0, half)
        ]

    at = jnp.stack([x, side, core, core, depth])
    at_other = jnp.stack([x, side, core, other, depth])
    cosine, sine = angles(segments[0], HEAD_SIZE)
    cosine, sine = cosine[:, 0], sine[:, 0]
    cosine, sine = (
        jnp.concatenate([cosine] * 4, axis=1),
        jnp.concatenate([-sine, sine, -sine, sine], axis=1),
    )
    gain_one, gain_two = gains[:1], gains[1:]

    flip_one, q, k, v, w_first = project(
        at, x_t, segments[0][:, None], cosine, sine, gain_one.T, own_first, parts_first
    )
    if fast:
        q = tie(q, came_gate)
    heads0, back0 = attend(q, k, v, 0, 3)
    if fast:
        q = tie(q, heads0, came_up)
    heads1, back1 = attend(q, k, v, 3, 2)
    heads = (heads0, heads1)
    if fast:
        heads = (heads0, tie(heads1, came_down))
    middle, entry, flip, dy = blend(at, x_t, dy_t, heads, gain_two, own_out, parts_out)
    y0, d0, gate0, up0, down0 = mix(
        at_other, entry, flip, dy, dy_t,
        (own_gate, *parts_gate[:2]), (own_up, *parts_up[:2]), (own_down, *parts_down[:2]),
    )
    y1, d1, gate1, up1, down1 = mix(
        at, tie(entry, d0), flip, dy, dy_t,
        (own_gate, *parts_gate[2:]), (own_up, *parts_up[2:]), (own_down, *parts_down[2:]),
    )
    wide, tower, low = {2: 2, 4: 1}, {2: 1, 4: 1}, {2: 1}
    cube = (2, half, -1)
    if fast:
        gate = start_sum(gate0.reshape(cube), gate1.reshape(cube))
        up = start_sum(up0.reshape(cube), up1.reshape(cube))
        down = start_sum(down0, down1)
        y1, gate, up, down = lax.optimization_barrier((y1, gate, up, down))
        gate, up, down = one_step(gate, 0, wide), one_step(up, 4, wide), one_step(down, 2, tower)
    mixed, middle_grad, branch, do, grad_gain_two = middle_back(
        at, middle, y0, y1, d0, d1, dy, heads, gain_two, own_out, parts_out
    )
    backs = []

    def group_back(do):
        g = len(backs)
        held, begin = (back0, g) if g < 3 else (back1, g - 3)
        backs.append(attend_back(held, k, v, do, cosine, sine, g, begin, 1))

    group_back(do)
    if fast:
        gate, up, down, backs[0] = lax.optimization_barrier((gate, up, down, backs[0]))
        gate, up, down = one_step(gate, 2, wide), one_step(up, 2, wide), one_step(down, 0, tower)
    near = near_grads(flip_one, backs[0], branch, heads)
    group_back(tie(do, near))
    if fast:
        near = start_sum(*split_cores(near.reshape(cube), 2))
        gate, up, down, near, backs[1] = lax.optimization_barrier(
            (gate, up, down, near, backs[1])
        )
        gate, up, down = one_step(gate, 4, wide), one_step(up, 0, wide), one_step(down, 4, tower)
        near = one_step(near, 2, tower)
    group_back(tie(do, backs[1]))
    if fast:
        gate, up, down, near, backs[2] = lax.optimization_barrier(
            (gate, up, down, near, backs[2])
        )
        gate = over_z(gate)
        near = one_step(near, 4, tower)
    mid = weight_grads(flip_one, backs[1:3])
    group_back(tie(do, mid))
    if fast:
        mid = start_sum(*split_cores(mid.reshape(cube), 1))
        gate, mid, near, backs[3] = lax.optimization_barrier((gate, mid, near, backs[3]))
        up = over_z(up)
        gate = back_step(gate, 4)
        near, mid = one_step(near, 0, tower), one_step(mid, 0, low)
    group_back(tie(do, backs[3]))
    if fast:
        gate, up, near, mid, backs[4] = lax.optimization_barrier((gate, up, near, mid, backs[4]))
        down = over_z(down)
        gate, up = back_step(gate, 2), back_step(up, 2)
        mid = one_step(mid, 2, low)
    far = weight_grads(flip_one, backs[3:])
    if fast:
        far = start_sum(*split_cores(far.reshape(cube), 1))
        far, mid, middle_grad = lax.optimization_barrier((far, mid, middle_grad))
        far = one_step(far, 0, low)
        near = over_z(near)
        mid = add_up(mid, swap_rep(mid, 4))
    grad_tokens, grad_gain_one = finish(x_t, middle_grad, backs, gain_one, w_first)
    gain_sums = reduce_gains(jnp.concatenate([grad_gain_one, grad_gain_two]))
    if fast:
        far, near, mid, up, gate, down, grad_tokens = lax.optimization_barrier(
            (far, near, mid, up, gate, down, grad_tokens)
        )
        far = one_step(far, 2, low)
        mid = over_z(mid)
        down, up = back_step(down, 4), back_step(up, 4)
        near = back_step(near, 4)
        sum_gate = widen(at, gate, swap_rep(gate, 1), (4, 2), True)
        far, near, down, sum_gate = lax.optimization_barrier((far, near, down, sum_gate))
        far = add_up(far, swap_rep(far, 4))
        near, down = back_step(near, 2), back_step(down, 2)
        sum_up = widen(at, up, swap_rep(up, 1), (2, 4), True)
        far, sum_up, mid = lax.optimization_barrier((far, sum_up, mid))
        far = over_z(far)
        mid = back_step(mid, 2)
        sum_down = widen(at, down, swap_rep(down, 1), (4, 2), False).T
        far, sum_down = lax.optimization_barrier((far, sum_down))
        far = back_step(far, 2)
        grad_query, grad_key, grad_value, grad_out = unpack(
            at, (near, swap_rep(near, 1)), (mid, swap_rep(mid, 1)), (far, swap_rep(far, 1))
        )
        grad_key, grad_value = grad_key.T, grad_value.T
    else:
        def whole_grad(two, one):
            both = jnp.stack([one.reshape(width, 2, cut), two.reshape(width, 2, cut)], axis=2)
            return both.reshape(width, inner)

        across, upright = {1: 2, 2: 2, 4: 1}, {1: 1, 2: 1, 4: 1}
        sum_gate = reduce_rows(whole_grad(gate0, gate1), (0, 2, 4), across)
        sum_up = reduce_rows(whole_grad(up0, up1), (4, 2, 0), across)
        downs = [d.transpose(1, 0, 2) for d in (down0, down1)]
        sum_down = reduce_rows(whole_grad(*downs).T, (2, 0, 4), upright)
        sums = [reduce_rows(part, (0, 2, 4), across) for part in (near, mid, far)]
        tall_rows = sums[0].shape[0]
        grad_out = sums[0][:, :columns]
        groups = jnp.concatenate([sums[0][:, columns:], *sums[1:]], axis=1)
        groups = groups.reshape(tall_rows, KEY_VALUE_HEADS, SPAN)
        deep = GROUP * HEAD_SIZE
        grad_query = groups[:, :, :deep].reshape(tall_rows, columns)
        grad_key = groups[:, :, deep : deep + HEAD_SIZE].reshape(tall_rows, key_columns)
        grad_value = groups[:, :, deep + HEAD_SIZE :].reshape(tall_rows, key_columns)
    return (
        mixed.T[None],
        grad_tokens.T[None],
        gain_sums[0],
        grad_query,
        grad_key,
        grad_value,
        grad_out,
        gain_sums[1],
        sum_gate,
        sum_up,
        sum_down,
    )


def solution(mesh):
    placed = (
        P(("rep", "shard"), None, None),
        P(("rep", "shard"), None),
        P("shard"),
        P("shard", None),
        P("shard", None),
        P("shard", None),
        P("shard", None),
        P("shard"),
        P("shard", None),
        P("shard", None),
        P("shard", None),
        P(("rep", "shard"), None, None),
    )
    return jax.shard_map(
        per_device,
        mesh=mesh,
        in_specs=placed,
        out_specs=(
            P(("rep", "shard"), None, None),
            P(("rep", "shard"), None, None),
            P("shard"),
            P("shard", None),
            P("shard", None),
            P("shard", None),
            P("shard", None),
            P("shard"),
            P("shard", None),
            P("shard", None),
            P("shard", None),
        ),
        check_vma=False,
    )
```

```python
from functools import partial

import jax
import jax.numpy as jnp
from jax import lax
from jax.experimental import pallas as pl
from jax.experimental.pallas import tpu as pltpu
from jax.sharding import PartitionSpec as P

QUERY_HEADS = 15
KEY_VALUE_HEADS = 5
HEAD_SIZE = 64


EPS = 1e-05
NEGATIVE = -1e30


def angles(documents, head_dim):
    segment_length = documents.shape[0]
    places = jnp.arange(segment_length, dtype=jnp.int32)
    begins = jnp.concatenate([jnp.ones((1,), dtype=jnp.bool_), documents[1:] != documents[:-1]])
    starting = lax.cummax(jnp.where(begins, places, 0), axis=0)
    offsets = (places - starting).astype(jnp.float32)
    rates = 10000.0 ** (-2.0 * jnp.arange(head_dim // 2).astype(jnp.float32) / head_dim)
    phases = offsets[:, None] * rates[None, :]
    return (jnp.cos(phases)[:, None, :], jnp.sin(phases)[:, None, :])


def bit_swap(count, bit):
    return [(i, i ^ bit) for i in range(count)]


def swap_rep(value, bit):
    return lax.ppermute(value, "rep", bit_swap(lax.axis_size("rep"), bit))


def swap_shard(value, bit):
    return lax.ppermute(value, "shard", bit_swap(lax.axis_size("shard"), bit))


def rep_bit(bit):
    return (lax.axis_index("rep") // bit) % 2


def place_pair(mine, other, bit, axis):
    low = jnp.concatenate([mine, other], axis=axis)
    high = jnp.concatenate([other, mine], axis=axis)
    return jnp.where(bit == 0, low, high)


def gather_rows(piece):
    shards = lax.axis_size("shard")
    rows, columns = piece.shape
    quarter = rows // 4
    core, side = rep_bit(1), rep_bit(2)
    part = lax.dynamic_slice_in_dim(piece, (core * 2 + side) * quarter, quarter, 0)
    held = part[None]
    bit = 1
    while bit < shards:
        held = jnp.concatenate([held, swap_shard(held, bit)], axis=0)
        bit *= 2
    others = held[1:]
    others = place_pair(others, swap_rep(others, 2), side, 1)
    others = place_pair(others, swap_rep(others, 1), core, 1)
    me = lax.axis_index("shard")
    if shards == 2:
        return place_pair(piece, others[0], me, 0)
    whole = jnp.zeros((shards, rows, columns), piece.dtype)
    whole = lax.dynamic_update_slice_in_dim(whole, piece[None], me, 0)
    for j in range(1, shards):
        whole = lax.dynamic_update_slice_in_dim(whole, others[j - 1][None], me ^ j, 0)
    return whole.reshape(shards * rows, columns)


def add_up(left, right):
    return (left.astype(jnp.float32) + right.astype(jnp.float32)).astype(jnp.bfloat16)


def halve(value, bit, axis, swap):
    half = value.shape[axis] // 2
    mine = lax.dynamic_slice_in_dim(value, bit * half, half, axis)
    theirs = lax.dynamic_slice_in_dim(value, (1 - bit) * half, half, axis)
    return add_up(mine, swap(theirs))


def halve_shard(value):
    bit = lax.axis_size("shard") // 2
    while bit:
        value = halve(
            value, (lax.axis_index("shard") // bit) % 2, 0, partial(swap_shard, bit=bit)
        )
        bit //= 2
    return value


def reduce_rows(grad, order, axes):
    shards = lax.axis_size("shard")
    rows, columns = grad.shape
    value = grad.astype(jnp.bfloat16).reshape(shards, rows // shards, columns)
    value = halve(value, rep_bit(1), axes[1], partial(swap_rep, bit=1))
    for step in order:
        if step == 0:
            value = halve_shard(value)
        else:
            value = halve(value, rep_bit(step), axes[step], partial(swap_rep, bit=step))
    bit = 8
    while bit < lax.axis_size("rep"):
        value = add_up(value, swap_rep(value, bit))
        bit *= 2
    for step in [s for s in reversed(order) if s] + [1]:
        value = place_pair(value, swap_rep(value, step), rep_bit(step), axes[step])
    return value[0].astype(jnp.float32)


LANES = 128
BLOCK = 256
GROUP = QUERY_HEADS // KEY_VALUE_HEADS
SPAN = (GROUP + 2) * HEAD_SIZE
WIDE = -(-SPAN // LANES) * LANES
SCALE = HEAD_SIZE**-0.5
ROOM = 56 * 1024 * 1024


def dot(left, right):
    return jnp.dot(left, right, preferred_element_type=jnp.float32)


def dot_nt(left, right):
    return lax.dot_general(left, right, (((1,), (1,)), ((), ())), preferred_element_type=jnp.float32)


def dot_tn(left, right):
    return lax.dot_general(left, right, (((0,), (0,)), ((), ())), preferred_element_type=jnp.float32)


def lanes_of(shape):
    return lax.broadcasted_iota(jnp.int32, shape, len(shape) - 1)


def turn(pair, cosine, sine):
    lane = lanes_of(pair.shape) % HEAD_SIZE
    half = HEAD_SIZE // 2
    partner = jnp.where(
        lane < half, pltpu.roll(pair, LANES - half, 1), pltpu.roll(pair, half, 1)
    )
    return pair * cosine + partner * sine


def three_parts(column):
    high = column.astype(jnp.bfloat16)
    rest = column - high.astype(jnp.float32)
    middle = rest.astype(jnp.bfloat16)
    low = (rest - middle.astype(jnp.float32)).astype(jnp.bfloat16)
    return high, middle, low


def put_parts(base, column, first):
    lane = lanes_of(base.shape)
    for k, part in enumerate(three_parts(column)):
        base = jnp.where(lane == first + k, part.astype(jnp.float32), base)
    return base


def call(kernel, grid, in_specs, out_specs, out_shape, scratch=(), flops=0, prefetch=0, move=0):
    return pl.pallas_call(
        kernel,
        grid_spec=pltpu.PrefetchScalarGridSpec(
            num_scalar_prefetch=prefetch,
            grid=grid,
            in_specs=in_specs,
            out_specs=out_specs,
            scratch_shapes=list(scratch),
        ),
        out_shape=out_shape,
        compiler_params=pltpu.CompilerParams(
            dimension_semantics=("arbitrary",) * len(grid), vmem_limit_bytes=ROOM
        ),
        cost_estimate=pl.CostEstimate(flops=flops, bytes_accessed=move, transcendentals=0),
    )


def struct(shape, dtype):
    return jax.ShapeDtypeStruct(shape, dtype)


def whole(shape):
    return pl.BlockSpec(shape, lambda *_: (0,) * len(shape))


def window(at_ref, core, side, rows):
    half = rows // 2
    return core * half + side * (half - rows * 4 // 15)


def fill_rows(at_ref, whole_ref, own_ref, parts):
    rows, tall = own_ref.shape[0], parts[0].shape[0]
    x, side, core = at_ref[0], at_ref[1], at_ref[2]
    whole_ref[pl.ds(pl.multiple_of(x * rows, 16), rows), :] = own_ref[...]
    for k, part in enumerate(parts):
        c, y = core ^ (k // 2), side ^ (k % 2)
        start = (1 - x) * rows + window(at_ref, c, y, rows)
        whole_ref[pl.ds(pl.multiple_of(start, 16), tall), :] = part[...]


def project_kernel(
    at_ref, x_ref, doc_ref, cos_ref, sin_ref, gain_ref, wq_ref, wk_ref, wv_ref, p0, p1, p2, p3,
    flip_ref, q_ref, k_ref, v_ref, w_ref, in_ref, own_ref,
):
    step = pl.program_id(0)

    @pl.when(step == 0)
    def _():
        w_key, w_value = wk_ref[...].T, wv_ref[...].T
        deep = GROUP * HEAD_SIZE
        pad = jnp.zeros((own_ref.shape[0], WIDE - SPAN), jnp.bfloat16)
        columns = []
        for g in range(KEY_VALUE_HEADS):
            span = slice(g * HEAD_SIZE, (g + 1) * HEAD_SIZE)
            columns += [wq_ref[:, g * deep : (g + 1) * deep], w_key[:, span], w_value[:, span], pad]
        own_ref[...] = jnp.concatenate(columns, axis=1)
        fill_rows(at_ref, w_ref, own_ref, (p0, p1, p2, p3))
        x = x_ref[...].astype(jnp.float32)
        inverse = lax.rsqrt(jnp.mean(x * x, axis=0, keepdims=True) + EPS)
        flip = (x * inverse * gain_ref[...]).astype(jnp.bfloat16)
        flip_ref[...] = flip
        in_ref[...] = flip.T

    y = dot(in_ref[...], w_ref[:, pl.ds(pl.multiple_of(step * WIDE, LANES), WIDE)])
    cosine, sine = cos_ref[...], sin_ref[...]
    first = turn(y[:, :LANES], cosine, sine)
    second = turn(y[:, LANES : 2 * LANES], cosine, sine)
    lane = lanes_of(first.shape)
    inner = lane < HEAD_SIZE
    doc = doc_ref[...]
    same = ((lane - HEAD_SIZE) == doc).astype(jnp.float32)
    q_ref[0] = jnp.where(inner, first * SCALE, same).astype(jnp.bfloat16)
    q_ref[1] = jnp.where(inner, pltpu.roll(first, HEAD_SIZE, 1) * SCALE, same).astype(jnp.bfloat16)
    q_ref[2] = jnp.where(inner, second * SCALE, same).astype(jnp.bfloat16)
    away = jnp.where(
        lane < HEAD_SIZE + 4,
        jnp.where((lane - HEAD_SIZE) == doc, 0.0, NEGATIVE),
        jnp.where(lane < HEAD_SIZE + 7, 1.0, 0.0),
    )
    k_ref[0] = jnp.where(inner, pltpu.roll(second, HEAD_SIZE, 1), away).astype(jnp.bfloat16)
    ones = jnp.where(lane < HEAD_SIZE + 3, 1.0, 0.0)
    v_ref[0] = jnp.where(inner, y[:, 2 * LANES :], ones).astype(jnp.bfloat16)


def project(at, x, documents, cosine, sine, gain, own, parts):
    width, rows = x.shape
    table = whole((rows, LANES))
    across = parts[0].shape[1]
    return call(
        project_kernel,
        (KEY_VALUE_HEADS,),
        [whole((width, rows)), whole((rows, 1)), table, table, whole((width, 1))]
        + [whole(w.shape) for w in own]
        + [whole(parts[0].shape)] * 4,
        [
            whole((width, rows)),
            pl.BlockSpec((GROUP, rows, LANES), lambda g, a: (g, 0, 0)),
            pl.BlockSpec((1, rows, LANES), lambda g, a: (g, 0, 0)),
            pl.BlockSpec((1, rows, LANES), lambda g, a: (g, 0, 0)),
            whole((width, across)),
        ],
        [
            struct((width, rows), jnp.bfloat16),
            struct((QUERY_HEADS, rows, LANES), jnp.bfloat16),
            struct((KEY_VALUE_HEADS, rows, LANES), jnp.bfloat16),
            struct((KEY_VALUE_HEADS, rows, LANES), jnp.bfloat16),
            struct((width, across), jnp.bfloat16),
        ],
        scratch=[
            pltpu.VMEM((rows, width), jnp.bfloat16),
            pltpu.VMEM((width // 2, across), jnp.bfloat16),
        ],
        flops=2 * rows * width * WIDE * KEY_VALUE_HEADS,
        prefetch=1,
        move=20_000_000,
    )(at, x, documents, cosine, sine, gain, *own, *parts)


def attend_kernel(q_ref, k_ref, v_ref, o_ref, qb_ref):
    rows = q_ref.shape[1]
    deep = GROUP * BLOCK
    row = lax.broadcasted_iota(jnp.int32, (GROUP, BLOCK, BLOCK), 1).reshape(deep, BLOCK)
    below = lanes_of((deep, BLOCK)) <= row
    for i in range(rows // BLOCK):
        here = pl.ds(i * BLOCK, BLOCK)
        q = q_ref[:, here, :].reshape(deep, LANES)
        near = jnp.where(below, dot_nt(q, k_ref[0, here, :]), NEGATIVE)
        top = jnp.max(near, axis=-1, keepdims=True)
        if i:
            past = pl.ds(0, i * BLOCK)
            far = dot_nt(q, k_ref[0, past, :])
            top = jnp.maximum(top, jnp.max(far, axis=-1, keepdims=True))
            total = dot(jnp.exp(far - top).astype(jnp.bfloat16), v_ref[0, past, :])
            total += dot(jnp.exp(near - top).astype(jnp.bfloat16), v_ref[0, here, :])
        else:
            total = dot(jnp.exp(near - top).astype(jnp.bfloat16), v_ref[0, here, :])
        summed = total[:, HEAD_SIZE : HEAD_SIZE + 1]
        out = (total / summed).reshape(GROUP, BLOCK, LANES)
        o_ref[0, here, :] = jnp.concatenate(
            [out[h][:, :HEAD_SIZE] for h in range(GROUP)], axis=1
        ).astype(jnp.bfloat16)
        back = put_parts(q.astype(jnp.float32), -(top + jnp.log(summed)), HEAD_SIZE + 4)
        qb_ref[:, here, :] = back.astype(jnp.bfloat16).reshape(GROUP, BLOCK, LANES)


def attend(q, k, v, first, groups):
    rows = q.shape[1]
    one = pl.BlockSpec((1, rows, LANES), lambda g: (g + first, 0, 0))
    three = pl.BlockSpec((GROUP, rows, LANES), lambda g: (g + first, 0, 0))
    return call(
        attend_kernel,
        (groups,),
        [three, one, one],
        [
            pl.BlockSpec((1, rows, GROUP * HEAD_SIZE), lambda g: (g, 0, 0)),
            pl.BlockSpec((GROUP, rows, LANES), lambda g: (g, 0, 0)),
        ],
        [
            struct((groups, rows, GROUP * HEAD_SIZE), jnp.bfloat16),
            struct((groups * GROUP, rows, LANES), jnp.bfloat16),
        ],
        flops=2 * 4 * rows * rows * LANES * GROUP * groups,
        move=3_000_000 * groups,
    )(q, k, v)


def blend_kernel(
    at_ref, x_ref, dy_ref, o0_ref, o1_ref, gain_ref, own_ref, p0, p1, p2, p3,
    mid_ref, in_ref, flip_ref, back_ref, w_ref,
):
    @pl.when(pl.program_id(0) == 0)
    def _():
        fill_rows(at_ref, w_ref, own_ref, (p0, p1, p2, p3))

    total = x_ref[...].astype(jnp.float32).T
    deep = GROUP * HEAD_SIZE
    early = o0_ref.shape[0]
    for g in range(KEY_VALUE_HEADS):
        heads = o0_ref[g] if g < early else o1_ref[g - early]
        total += dot(heads, w_ref[pl.ds(g * deep, deep), :])
    mid_ref[...] = total
    inverse = lax.rsqrt(jnp.mean(total * total, axis=-1, keepdims=True) + EPS)
    entry = (total * inverse * gain_ref[...]).astype(jnp.bfloat16)
    in_ref[...] = entry
    flip_ref[...] = entry.T
    back_ref[...] = dy_ref[...].T


def head_specs(heads):
    deep = GROUP * HEAD_SIZE
    return [pl.BlockSpec((h.shape[0], BLOCK, deep), lambda i, a: (0, i, 0)) for h in heads]


def blend(at, x, dy, heads, gain, own, parts):
    width, rows = x.shape
    band = pl.BlockSpec((BLOCK, width), lambda i, a: (i, 0))
    side = pl.BlockSpec((width, BLOCK), lambda i, a: (0, i))
    return call(
        blend_kernel,
        (rows // BLOCK,),
        [side, side]
        + head_specs(heads)
        + [whole((1, width)), whole(own.shape)]
        + [whole(parts[0].shape)] * 4,
        [band, band, side, band],
        [
            struct((rows, width), jnp.float32),
            struct((rows, width), jnp.bfloat16),
            struct((width, rows), jnp.bfloat16),
            struct((rows, width), jnp.bfloat16),
        ],
        scratch=[pltpu.VMEM((2 * own.shape[0], width), jnp.bfloat16)],
        flops=2 * rows * width * width,
        prefetch=1,
        move=18_000_000,
    )(at, x, dy, *heads, gain, own, *parts)


def mix_kernel(
    at_ref, in_ref, flip_ref, dy_ref, back_ref, gate_own, g0, g1, up_own, u0, u1, down_own, d0, d1,
    y_ref, din_ref, gg_ref, gu_ref, gd_ref, gate_ref, up_ref, down_ref,
):
    step = pl.program_id(0)
    x, side = at_ref[0], at_ref[1]
    rows = gate_own.shape[0]
    mine = pl.ds(pl.multiple_of(x * rows, 16), rows)
    theirs = pl.ds(pl.multiple_of((1 - x) * rows, 16), rows)
    gate_ref[mine, :] = gate_own[...]
    up_ref[mine, :] = up_own[...]

    @pl.when(step == side)
    def _():
        gate_ref[theirs, :] = g0[...]
        up_ref[theirs, :] = u0[...]

    @pl.when(step != side)
    def _():
        gate_ref[theirs, :] = g1[...]
        up_ref[theirs, :] = u1[...]

    @pl.when(step == x)
    def _():
        down_ref[...] = down_own[...]

    @pl.when(step != x)
    def _():
        down_ref[pl.ds(pl.multiple_of(side * rows, 16), rows), :] = d0[...]
        down_ref[pl.ds(pl.multiple_of((1 - side) * rows, 16), rows), :] = d1[...]

    entry, dy = in_ref[...], dy_ref[...]
    w_gate, w_up, w_down = gate_ref[...], up_ref[...], down_ref[...]
    gate = dot(entry, w_gate)
    up = dot(entry, w_up)
    sigmoid = jax.nn.sigmoid(gate)
    active = gate * sigmoid
    hidden = (active * up).astype(jnp.bfloat16)
    hidden_grad = dot(dy, w_down)
    gate_grad = (hidden_grad * up * sigmoid * (1.0 + gate * (1.0 - sigmoid))).astype(jnp.bfloat16)
    up_grad = (hidden_grad * active).astype(jnp.bfloat16)
    gd_ref[0] = dot(back_ref[...], hidden).astype(jnp.bfloat16)
    gg_ref[...] = dot(flip_ref[...], gate_grad).astype(jnp.bfloat16)
    gu_ref[...] = dot(flip_ref[...], up_grad).astype(jnp.bfloat16)
    y = dot_nt(hidden, w_down)
    din = dot_nt(gate_grad, w_gate) + dot_nt(up_grad, w_up)

    @pl.when(step == 0)
    def _():
        y_ref[...] = y
        din_ref[...] = din

    @pl.when(step > 0)
    def _():
        y_ref[...] += y
        din_ref[...] += din


def mix(at, entry, flip, dy, back, gate, up, down):
    rows, width = entry.shape
    cut = gate[1].shape[1]
    full, turned = whole((rows, width)), whole((width, rows))
    side = pl.BlockSpec((width // 2, cut), lambda i, a: (0, 2 * i + a[3]))
    piece = whole((width // 2, cut))
    grad = pl.BlockSpec((width, cut), lambda i, a: (0, i))
    return call(
        mix_kernel,
        (2,),
        [full, turned, full, turned, side, piece, piece, side, piece, piece]
        + [pl.BlockSpec((width, cut), lambda i, a: (0, a[3])), piece, piece],
        [full, full, grad, grad, pl.BlockSpec((1, width, cut), lambda i, a: (i, 0, 0))],
        [
            struct((rows, width), jnp.float32),
            struct((rows, width), jnp.float32),
            struct((width, 2 * cut), jnp.bfloat16),
            struct((width, 2 * cut), jnp.bfloat16),
            struct((2, width, cut), jnp.bfloat16),
        ],
        scratch=[pltpu.VMEM((width, cut), jnp.bfloat16)] * 3,
        flops=2 * 9 * rows * width * cut * 2,
        prefetch=1,
        move=30_000_000,
    )(at, entry, flip, dy, back, *gate, *up, *down)


def middle_kernel(
    at_ref, mid_ref, y0_ref, y1_ref, d0_ref, d1_ref, dy_ref, o0_ref, o1_ref, gain_ref,
    own_ref, p0, p1, p2, p3, mixed_ref, grad_ref, branch_ref, do_ref, gain_out, w_ref,
):
    step = pl.program_id(0)

    @pl.when(step == 0)
    def _():
        fill_rows(at_ref, w_ref, own_ref, (p0, p1, p2, p3))
        gain_out[...] = jnp.zeros_like(gain_out)

    middle = mid_ref[...]
    mixed_ref[...] = (middle + y0_ref[...] + y1_ref[...]).astype(jnp.bfloat16).T
    inverse = lax.rsqrt(jnp.mean(middle * middle, axis=-1, keepdims=True) + EPS)
    normed = middle * inverse
    back = d0_ref[...] + d1_ref[...]
    product = back * normed
    mean = jnp.mean(product * gain_ref[...], axis=-1, keepdims=True)
    grad = dy_ref[...].astype(jnp.float32) + inverse * (back * gain_ref[...] - normed * mean)
    grad_ref[...] = grad
    branch = grad.astype(jnp.bfloat16)
    branch_ref[...] = branch
    gain_out[...] += jnp.sum(product, axis=0, keepdims=True)
    deep = GROUP * HEAD_SIZE
    lane = lanes_of((BLOCK, LANES))
    inner = lane < HEAD_SIZE
    for g in range(KEY_VALUE_HEADS):
        heads = o0_ref[g] if g < o0_ref.shape[0] else o1_ref[g - o0_ref.shape[0]]
        upstream = dot_nt(branch, w_ref[pl.ds(g * deep, deep), :]).astype(jnp.bfloat16)
        upstream = upstream.astype(jnp.float32)
        both = upstream * heads.astype(jnp.float32)
        pair, pair_both = upstream[:, :LANES], both[:, :LANES]
        wide = (pair, pltpu.roll(pair, HEAD_SIZE, 1), upstream[:, LANES:])
        sums = (
            jnp.sum(jnp.where(inner, pair_both, 0.0), axis=-1, keepdims=True),
            jnp.sum(jnp.where(inner, 0.0, pair_both), axis=-1, keepdims=True),
            jnp.sum(both[:, LANES:], axis=-1, keepdims=True),
        )
        for h in range(GROUP):
            delta = -sums[h]
            high = delta.astype(jnp.bfloat16).astype(jnp.float32)
            low = delta - high
            own = wide[h]
            if own.shape[1] < LANES:
                own = jnp.concatenate([own, jnp.zeros_like(own)], axis=1)
            rest = jnp.where(lane == HEAD_SIZE, high, jnp.where(lane == HEAD_SIZE + 1, low, 0.0))
            do_ref[g * GROUP + h] = jnp.where(inner, own, rest).astype(jnp.bfloat16)


def middle_back(at, middle, y0, y1, d0, d1, dy, heads, gain, own, parts):
    rows, width = middle.shape
    band = pl.BlockSpec((BLOCK, width), lambda i, a: (i, 0))
    return call(
        middle_kernel,
        (rows // BLOCK,),
        [band] * 6
        + head_specs(heads)
        + [whole((1, width)), whole(own.shape)]
        + [whole(parts[0].shape)] * 4,
        [
            pl.BlockSpec((width, BLOCK), lambda i, a: (0, i)),
            band,
            band,
            pl.BlockSpec((QUERY_HEADS, BLOCK, LANES), lambda i, a: (0, i, 0)),
            whole((1, width)),
        ],
        [
            struct((width, rows), jnp.bfloat16),
            struct((rows, width), jnp.float32),
            struct((rows, width), jnp.bfloat16),
            struct((QUERY_HEADS, rows, LANES), jnp.bfloat16),
            struct((1, width), jnp.float32),
        ],
        scratch=[pltpu.VMEM((2 * own.shape[0], width), jnp.bfloat16)],
        flops=2 * rows * width * width,
        prefetch=1,
        move=30_000_000,
    )(at, middle, y0, y1, d0, d1, dy, *heads, gain, own, *parts)


def attend_back_kernel(q_ref, k_ref, v_ref, do_ref, cos_ref, sin_ref, out_ref, dq_ref):
    rows = q_ref.shape[1]
    count = rows // BLOCK
    after = lax.broadcasted_iota(jnp.int32, (BLOCK, BLOCK), 0) <= lanes_of((BLOCK, BLOCK))
    key_grads, value_grads = [], []
    for j in range(count):
        here = pl.ds(j * BLOCK, BLOCK)
        k, v = k_ref[0, here, :], v_ref[0, here, :]
        dk = jnp.zeros((BLOCK, LANES), jnp.float32)
        dv = jnp.zeros((BLOCK, LANES), jnp.float32)
        for h in range(GROUP):
            for start, size in ((j * BLOCK, BLOCK), ((j + 1) * BLOCK, rows - (j + 1) * BLOCK)):
                if not size:
                    continue
                span = pl.ds(start, size)
                q, do = q_ref[h, span, :], do_ref[h, span, :]
                scores = dot_nt(k, q)
                if start == j * BLOCK:
                    scores = jnp.where(after, scores, NEGATIVE)
                probs = jnp.exp(scores)
                score_grad = (probs * dot_nt(v, do)).astype(jnp.bfloat16)
                dv += dot(probs.astype(jnp.bfloat16), do)
                dk += dot(score_grad, q)
                dq = dot_tn(score_grad, k)
                if j == 0:
                    dq_ref[h, span, :] = dq
                else:
                    dq_ref[h, span, :] += dq
        key_grads.append(dk)
        value_grads.append(dv)
    cosine, sine = cos_ref[...], -sin_ref[...]
    half = HEAD_SIZE
    parts = [turn(dq_ref[h] * SCALE, cosine, sine)[:, :half] for h in range(GROUP)]
    parts.append(turn(jnp.concatenate(key_grads, axis=0), cosine, sine)[:, :half])
    parts.append(jnp.concatenate(value_grads, axis=0)[:, :half])
    parts.append(jnp.zeros((rows, WIDE - SPAN), jnp.float32))
    out_ref[0] = jnp.concatenate(parts, axis=1).astype(jnp.bfloat16)


def attend_back(q, k, v, do, cosine, sine, first, begin, groups):
    rows = q.shape[1]
    one = pl.BlockSpec((1, rows, LANES), lambda g: (g + first, 0, 0))
    table = whole((rows, LANES))
    return call(
        attend_back_kernel,
        (groups,),
        [
            pl.BlockSpec((GROUP, rows, LANES), lambda g: (g + begin, 0, 0)),
            one,
            one,
            pl.BlockSpec((GROUP, rows, LANES), lambda g: (g + first, 0, 0)),
            table,
            table,
        ],
        pl.BlockSpec((1, rows, WIDE), lambda g: (g, 0, 0)),
        struct((groups, rows, WIDE), jnp.bfloat16),
        scratch=[pltpu.VMEM((GROUP, rows, LANES), jnp.float32)],
        flops=2 * 10 * rows * rows * LANES * GROUP * groups,
        move=3_000_000 * groups,
    )(q, k, v, do, cosine, sine)


def weight_kernel(flip_ref, *refs):
    flip = flip_ref[...]
    parts = [dot(flip, ref[0])[:, :SPAN].astype(jnp.bfloat16) for ref in refs[:-1]]
    refs[-1][...] = jnp.concatenate(parts, axis=1)


def weight_grads(flip, backs):
    width, rows = flip.shape
    half = width // 2
    across = len(backs) * SPAN
    return call(
        weight_kernel,
        (2,),
        [pl.BlockSpec((half, rows), lambda i: (i, 0))] + [whole(b.shape) for b in backs],
        pl.BlockSpec((half, across), lambda i: (i, 0)),
        struct((width, across), jnp.bfloat16),
        flops=2 * rows * width * across,
        move=10_000_000,
    )(flip, *backs)


def near_kernel(flip_ref, back_ref, branch_ref, o0_ref, o1_ref, out_ref):
    deep = GROUP * HEAD_SIZE
    branch = branch_ref[...]
    for g in range(KEY_VALUE_HEADS):
        heads = o0_ref[g] if g < o0_ref.shape[0] else o1_ref[g - o0_ref.shape[0]]
        span = pl.ds(g * deep, deep)
        left = dot_tn(heads, branch)
        right = dot(flip_ref[span, :], back_ref[0])[:, :SPAN]
        out_ref[span, :] = jnp.concatenate([left, right], axis=1).astype(jnp.bfloat16)


def near_grads(flip, back, branch, heads):
    width, rows = flip.shape
    args = (flip, back, branch, *heads)
    return call(
        near_kernel,
        (1,),
        [whole(a.shape) for a in args],
        whole((width, width + SPAN)),
        struct((width, width + SPAN), jnp.bfloat16),
        flops=2 * rows * width * (width + SPAN),
        move=12_000_000,
    )(*args)


def finish_kernel(x_ref, mid_ref, *refs):
    gain_ref, w_ref, out_ref, gain_out = refs[KEY_VALUE_HEADS:]
    x = x_ref[...].astype(jnp.float32).T
    inverse = lax.rsqrt(jnp.mean(x * x, axis=-1, keepdims=True) + EPS)
    normed = x * inverse
    back = jnp.zeros_like(x)
    for g in range(KEY_VALUE_HEADS):
        back += dot_nt(refs[g][0], w_ref[:, pl.ds(g * WIDE, WIDE)])
    product = back * normed

    @pl.when(pl.program_id(0) == 0)
    def _():
        gain_out[...] = jnp.zeros_like(gain_out)

    gain_out[...] += jnp.sum(product, axis=0, keepdims=True)
    mean = jnp.mean(product * gain_ref[...], axis=-1, keepdims=True)
    grad = mid_ref[...] + inverse * (back * gain_ref[...] - normed * mean)
    out_ref[...] = grad.astype(jnp.bfloat16).T


def finish(x, middle_grad, backs, gain, w_first):
    width, rows = x.shape
    side = pl.BlockSpec((width, BLOCK), lambda i: (0, i))
    return call(
        finish_kernel,
        (rows // BLOCK,),
        [side, pl.BlockSpec((BLOCK, width), lambda i: (i, 0))]
        + [pl.BlockSpec((1, BLOCK, WIDE), lambda i: (0, i, 0)) for _ in backs]
        + [whole((1, width)), whole(w_first.shape)],
        [side, whole((1, width))],
        [struct((width, rows), jnp.bfloat16), struct((1, width), jnp.float32)],
        flops=2 * rows * width * WIDE * KEY_VALUE_HEADS,
        move=14_000_000,
    )(x, middle_grad, *backs, gain, w_first)


def widen_kernel(at_ref, mine_ref, other_ref, out_ref):
    cut = mine_ref.shape[2]
    mine, other = mine_ref[0].astype(jnp.float32), other_ref[0].astype(jnp.float32)

    @pl.when(at_ref[2] == 0)
    def _():
        out_ref[:, :cut] = mine
        out_ref[:, cut:] = other

    @pl.when(at_ref[2] != 0)
    def _():
        out_ref[:, :cut] = other
        out_ref[:, cut:] = mine


def came_at(at, j, order):
    apart = {2: at[1] ^ (j // 2), 4: at[4] ^ (j % 2)}
    return apart[order[0]] + 2 * apart[order[1]]


def widen(at, mine, other, order, spread):
    _, rows, columns = mine.shape
    if spread:
        shape = (2 * rows, 4 * columns)
        out = pl.BlockSpec((rows, 2 * columns), lambda j, a: (j % 2, j // 2))
    else:
        shape = (4 * rows, 2 * columns)
        out = pl.BlockSpec((rows, 2 * columns), lambda j, a: (j, 0))
    return call(
        widen_kernel,
        (4,),
        [pl.BlockSpec((1, rows, columns), lambda j, a: (came_at(a, j, order), 0, 0))] * 2,
        out,
        struct(shape, jnp.float32),
        prefetch=1,
        move=10_000_000,
    )(at, mine, other)


def unpack_kernel(
    at_ref, near0, near1, mid0, mid1, far0, far1, q_ref, k_ref, v_ref, out_ref,
    near_ref, mid_ref, far_ref,
):
    core, side = at_ref[2], at_ref[1]
    rows, columns = near0.shape[1:]
    for j in range(4):
        at = came_at(at_ref, j, (4, 2))
        mine, other = near0[at].astype(jnp.float32), near1[at].astype(jnp.float32)
        left, right = jnp.where(core == 0, mine, other), jnp.where(core == 0, other, mine)
        near_ref[j * rows : (j + 1) * rows, :] = jnp.concatenate([left, right], axis=1)
    for mine_ref, other_ref, into in ((mid0, mid1, mid_ref), (far0, far1, far_ref)):
        for c in range(2):
            for y in range(2):
                at = y ^ side
                mine, other = mine_ref[at].astype(jnp.float32), other_ref[at].astype(jnp.float32)
                start = (2 * c + y) * mine.shape[0]
                into[start : start + mine.shape[0], :] = jnp.where(core == c, mine, other)
    near, mid, far = near_ref[...], mid_ref[...], far_ref[...]
    deep = GROUP * HEAD_SIZE
    split = near.shape[1] - SPAN
    groups = [near[:, split:], mid[:, :SPAN], mid[:, SPAN:], far[:, :SPAN], far[:, SPAN:]]
    out_ref[...] = near[:, :split]
    q_ref[...] = jnp.concatenate([g[:, :deep] for g in groups], axis=1)
    k_ref[...] = jnp.concatenate([g[:, deep : deep + HEAD_SIZE] for g in groups], axis=1).T
    v_ref[...] = jnp.concatenate([g[:, deep + HEAD_SIZE :] for g in groups], axis=1).T


def unpack(at, near, mid, far):
    _, rows, columns = near[0].shape
    args = (*near, *mid, *far)
    tall = 4 * rows
    key_columns = KEY_VALUE_HEADS * HEAD_SIZE
    shapes = [
        (tall, QUERY_HEADS * HEAD_SIZE),
        (key_columns, tall),
        (key_columns, tall),
        (tall, 2 * columns - SPAN),
    ]
    return call(
        unpack_kernel,
        (1,),
        [whole(a.shape) for a in args],
        [whole(shape) for shape in shapes],
        [struct(shape, jnp.float32) for shape in shapes],
        scratch=[
            pltpu.VMEM((tall, 2 * columns), jnp.float32),
            pltpu.VMEM((tall, 2 * SPAN), jnp.float32),
            pltpu.VMEM((tall, 2 * SPAN), jnp.float32),
        ],
        prefetch=1,
        move=8_000_000,
    )(at, *args)


def tie(value, *others):
    return lax.optimization_barrier((value, *others))[0]


def first_rows(w_query, w_key, w_value):
    rows = w_query.shape[0]
    pad = jnp.zeros((rows, WIDE - SPAN), w_query.dtype)
    deep = GROUP * HEAD_SIZE
    columns = []
    for g in range(KEY_VALUE_HEADS):
        columns.append(w_query[:, g * deep : (g + 1) * deep])
        columns.append(w_key[:, g * HEAD_SIZE : (g + 1) * HEAD_SIZE])
        columns.append(w_value[:, g * HEAD_SIZE : (g + 1) * HEAD_SIZE])
        columns.append(pad)
    return jnp.concatenate(columns, axis=1)


def spread_rows(received):
    beside = swap_rep(received, 2)
    return [received, beside, swap_rep(received, 1), swap_rep(beside, 1)]


def start_sum(send, keep):
    return add_up(keep, swap_rep(send, 1))


def one_step(value, step, axes):
    if step == 0:
        return halve_shard(value)
    return halve(value, rep_bit(step), axes[step], partial(swap_rep, bit=step))


def over_z(value):
    bit = 8
    while bit < lax.axis_size("rep"):
        other = swap_rep(value, bit)
        value = value + other if value.dtype == jnp.float32 else add_up(value, other)
        bit *= 2
    return value


def back_step(value, step):
    return jnp.concatenate([value, swap_rep(value, step)], axis=0)


def split_cores(grad, axis):
    core = rep_bit(1)
    half = grad.shape[axis] // 2
    send = lax.dynamic_slice_in_dim(grad, (1 - core) * half, half, axis)
    keep = lax.dynamic_slice_in_dim(grad, core * half, half, axis)
    return send, keep


def per_device(
    tokens,
    segments,
    gain_attn,
    w_query,
    key_weight_matrix,
    value_weight_matrix,
    w_out,
    gain_mlp,
    w_gate,
    w_up,
    w_down,
    cotangent,
):
    shards = lax.axis_size("shard")
    fast = shards == 2
    rows, width = tokens.shape[1:]
    half = width // 2
    columns = QUERY_HEADS * HEAD_SIZE
    key_columns = KEY_VALUE_HEADS * HEAD_SIZE
    inner = w_gate.shape[1]
    cut = inner // 4
    x_t = tokens[0].T
    dy_t = cotangent[0].T
    tall = half * 4 // 15
    zero = jnp.int32(0)

    if fast:
        x, side, core, depth = lax.axis_index("shard"), rep_bit(2), rep_bit(1), rep_bit(4)
        x, side, core, depth = (v.astype(jnp.int32) for v in (x, side, core, depth))
        other = 1 - core
        start = window(None, core, side, half)
        narrow = partial(lax.dynamic_slice_in_dim, start_index=start, slice_size=tall, axis=0)
        part_first = first_rows(
            narrow(w_query), narrow(key_weight_matrix), narrow(value_weight_matrix)
        )
        came_first = swap_shard(part_first, 1)
        own_first = (w_query, key_weight_matrix.T, value_weight_matrix.T)
        gains = tie(jnp.stack([gain_attn, gain_mlp]).astype(jnp.float32), part_first)
        gains = place_pair(gains, swap_shard(gains, 1), x, 1)
        column = (2 * side + other) * cut
        part_out = narrow(w_out)
        part_gate = lax.dynamic_slice_in_dim(w_gate, column, cut, 1)
        part_up = lax.dynamic_slice_in_dim(w_up, column, cut, 1)
        own_down = w_down.T
        part_down = lax.dynamic_slice(own_down, (side * half, other * cut), (half, cut))
        part_out, part_gate = tie(part_out, came_first), tie(part_gate, came_first)
        part_up, part_down = tie(part_up, came_first), tie(part_down, came_first)
        came_out, came_gate = swap_shard(part_out, 1), swap_shard(part_gate, 1)
        came_up, came_down = swap_shard(part_up, 1), swap_shard(part_down, 1)
        parts_first = spread_rows(came_first)
        own_out, own_gate, own_up = w_out, w_gate, w_up
    else:
        x = side = core = depth = zero
        other = 1 - core
        full_first = [gather_rows(w) for w in (w_query, key_weight_matrix, value_weight_matrix)]
        full_out = gather_rows(w_out)
        starts = [half + window(None, c, y, half) for c in (0, 1) for y in (0, 1)]
        own_first = (full_first[0][:half], full_first[1][:half].T, full_first[2][:half].T)
        parts_first = [first_rows(*(w[s : s + tall] for w in full_first)) for s in starts]
        own_out, parts_out = full_out[:half], [full_out[s : s + tall] for s in starts]
        gains = gather_rows(jnp.pad(jnp.stack([gain_attn, gain_mlp], axis=1), ((0, 0), (0, 126))))
        gains = gains[:, :2].T.astype(jnp.float32)

        def cut_up(value):
            blocks = [value[half:, k * cut : (k + 1) * cut] for k in range(4)]
            return value[:half], [blocks[1], blocks[3], blocks[0], blocks[2]]

        own_gate, parts_gate = cut_up(gather_rows(w_gate))
        own_up, parts_up = cut_up(gather_rows(w_up))
        full_down = gather_rows(w_down).T
        own_down = full_down[:, : 2 * cut]
        parts_down = [
            full_down[r : r + half, (2 + c) * cut : (3 + c) * cut]
            for c in (1, 0)
            for r in (0, half)
        ]

    at = jnp.stack([x, side, core, core, depth])
    at_other = jnp.stack([x, side, core, other, depth])
    cosine, sine = angles(segments[0], HEAD_SIZE)
    cosine, sine = cosine[:, 0], sine[:, 0]
    cosine, sine = (
        jnp.concatenate([cosine] * 4, axis=1),
        jnp.concatenate([-sine, sine, -sine, sine], axis=1),
    )
    gain_one, gain_two = gains[:1], gains[1:]

    flip_one, q, k, v, w_first = project(
        at, x_t, segments[0][:, None], cosine, sine, gain_one.T, own_first, parts_first
    )
    if fast:
        q, came_out, came_gate = lax.optimization_barrier((q, came_out, came_gate))
        parts_out, parts_gate = spread_rows(came_out), spread_rows(came_gate)
    heads0, back0 = attend(q, k, v, 0, 3)
    if fast:
        q, heads0, came_up, came_down = lax.optimization_barrier((q, heads0, came_up, came_down))
        parts_up, parts_down = spread_rows(came_up), spread_rows(came_down)
    heads1, back1 = attend(q, k, v, 3, 2)
    heads = (heads0, heads1)
    middle, entry, flip, dy = blend(at, x_t, dy_t, heads, gain_two, own_out, parts_out)
    y0, d0, gate0, up0, down0 = mix(
        at_other, entry, flip, dy, dy_t,
        (own_gate, *parts_gate[:2]), (own_up, *parts_up[:2]), (own_down, *parts_down[:2]),
    )
    y1, d1, gate1, up1, down1 = mix(
        at, tie(entry, d0), flip, dy, dy_t,
        (own_gate, *parts_gate[2:]), (own_up, *parts_up[2:]), (own_down, *parts_down[2:]),
    )
    wide, tower, low = {2: 2, 4: 1}, {2: 1, 4: 1}, {2: 1}
    cube = (2, half, -1)
    if fast:
        gate = start_sum(gate0.reshape(cube), gate1.reshape(cube))
        up = start_sum(up0.reshape(cube), up1.reshape(cube))
        down = start_sum(down0, down1)
        y1, gate, up, down = lax.optimization_barrier((y1, gate, up, down))
        gate, up, down = one_step(gate, 0, wide), one_step(up, 4, wide), one_step(down, 2, tower)
    mixed, middle_grad, branch, do, grad_gain_two = middle_back(
        at, middle, y0, y1, d0, d1, dy, heads, gain_two, own_out, parts_out
    )
    backs = []

    def group_back(do):
        g = len(backs)
        held, begin = (back0, g) if g < 3 else (back1, g - 3)
        backs.append(attend_back(held, k, v, do, cosine, sine, g, begin, 1))

    group_back(do)
    if fast:
        gate, up, down, backs[0] = lax.optimization_barrier((gate, up, down, backs[0]))
        gate, up, down = one_step(gate, 2, wide), one_step(up, 0, wide), one_step(down, 4, tower)
    near = near_grads(flip_one, backs[0], branch, heads)
    group_back(tie(do, near))
    if fast:
        near = start_sum(*split_cores(near.reshape(cube), 2))
        gate, up, down, near, backs[1] = lax.optimization_barrier(
            (gate, up, down, near, backs[1])
        )
        gate, up, down = one_step(gate, 4, wide), one_step(up, 2, wide), one_step(down, 0, tower)
        near = one_step(near, 0, tower)
    group_back(tie(do, backs[1]))
    if fast:
        gate, up, down, backs[2] = lax.optimization_barrier((gate, up, down, backs[2]))
        gate = over_z(gate)
    mid = weight_grads(flip_one, backs[1:3])
    if fast:
        up, near, mid = lax.optimization_barrier((up, near, mid))
        up = over_z(up)
        near = one_step(near, 2, tower)
    group_back(tie(do, mid))
    if fast:
        mid = start_sum(*split_cores(mid.reshape(cube), 1))
        gate, mid, near, backs[3] = lax.optimization_barrier((gate, mid, near, backs[3]))
        down = over_z(down)
        gate = back_step(gate, 4)
        near, mid = one_step(near, 4, tower), one_step(mid, 0, low)
    group_back(tie(do, backs[3]))
    if fast:
        gate, up, near, mid, backs[4] = lax.optimization_barrier((gate, up, near, mid, backs[4]))
        gate, up = back_step(gate, 2), back_step(up, 2)
        mid = one_step(mid, 2, low)
    far = weight_grads(flip_one, backs[3:])
    if fast:
        far = start_sum(*split_cores(far.reshape(cube), 1))
        near, mid, far, middle_grad = lax.optimization_barrier((near, mid, far, middle_grad))
        far = one_step(far, 0, low)
        near = over_z(near)
        mid = add_up(mid, swap_rep(mid, 4))
    grad_tokens, grad_gain_one = finish(x_t, middle_grad, backs, gain_one, w_first)
    gain_sums = jnp.concatenate([grad_gain_one, grad_gain_two])
    if fast:
        gain_sums, far, gate, up, down, near, mid = lax.optimization_barrier(
            (gain_sums, far, gate, up, down, near, mid)
        )
        far = one_step(far, 2, low)
        gain_sums += swap_rep(gain_sums, 4)
        other_gate = swap_rep(gate, 1)
        up, down = back_step(up, 4), back_step(down, 4)
        near, mid = back_step(near, 4), over_z(mid)
        sum_gate = widen(at, gate, other_gate, (4, 2), True)
        gain_sums, far, sum_gate, near, down = lax.optimization_barrier(
            (gain_sums, far, sum_gate, near, down)
        )
        far = add_up(far, swap_rep(far, 4))
        gain_sums += swap_rep(gain_sums, 2)
        near, down = back_step(near, 2), back_step(down, 2)
        other_up = swap_rep(up, 1)
        sum_up = widen(at, up, other_up, (2, 4), True)
        gain_sums, far, sum_up, near, mid, down = lax.optimization_barrier(
            (gain_sums, far, sum_up, near, mid, down)
        )
        far = over_z(far)
        gain_sums += swap_shard(gain_sums, 1)
        mid = back_step(mid, 2)
        other_down, other_near = swap_rep(down, 1), swap_rep(near, 1)
        sum_down = widen(at, down, other_down, (4, 2), False).T
        gain_sums, far, sum_down, other_near, mid = lax.optimization_barrier(
            (gain_sums, far, sum_down, other_near, mid)
        )
        far = back_step(far, 2)
        gain_sums = over_z(gain_sums)
        other_mid = swap_rep(mid, 1)
        gain_sums, far = lax.optimization_barrier((gain_sums, far))
        gain_sums += swap_rep(gain_sums, 1)
        grad_query, grad_key, grad_value, grad_out = unpack(
            at, (near, other_near), (mid, other_mid), (far, swap_rep(far, 1))
        )
        grad_key, grad_value = grad_key.T, grad_value.T
    else:
        def whole_grad(two, one):
            both = jnp.stack([one.reshape(width, 2, cut), two.reshape(width, 2, cut)], axis=2)
            return both.reshape(width, inner)

        gain_sums = lax.psum(gain_sums, ("rep", "shard"))
        across, upright = {1: 2, 2: 2, 4: 1}, {1: 1, 2: 1, 4: 1}
        sum_gate = reduce_rows(whole_grad(gate0, gate1), (0, 2, 4), across)
        sum_up = reduce_rows(whole_grad(up0, up1), (4, 0, 2), across)
        downs = [d.transpose(1, 0, 2) for d in (down0, down1)]
        sum_down = reduce_rows(whole_grad(*downs).T, (2, 0, 4), upright)
        sums = [reduce_rows(part, (0, 2, 4), across) for part in (near, mid, far)]
        tall_rows = sums[0].shape[0]
        grad_out = sums[0][:, :columns]
        groups = jnp.concatenate([sums[0][:, columns:], *sums[1:]], axis=1)
        groups = groups.reshape(tall_rows, KEY_VALUE_HEADS, SPAN)
        deep = GROUP * HEAD_SIZE
        grad_query = groups[:, :, :deep].reshape(tall_rows, columns)
        grad_key = groups[:, :, deep : deep + HEAD_SIZE].reshape(tall_rows, key_columns)
        grad_value = groups[:, :, deep + HEAD_SIZE :].reshape(tall_rows, key_columns)
    own = width // shards
    gain_sums = lax.dynamic_slice_in_dim(gain_sums, lax.axis_index("shard") * own, own, 1)
    return (
        mixed.T[None],
        grad_tokens.T[None],
        gain_sums[0],
        grad_query,
        grad_key,
        grad_value,
        grad_out,
        gain_sums[1],
        sum_gate,
        sum_up,
        sum_down,
    )


def solution(mesh):
    placed = (
        P(("rep", "shard"), None, None),
        P(("rep", "shard"), None),
        P("shard"),
        P("shard", None),
        P("shard", None),
        P("shard", None),
        P("shard", None),
        P("shard"),
        P("shard", None),
        P("shard", None),
        P("shard", None),
        P(("rep", "shard"), None, None),
    )
    return jax.shard_map(
        per_device,
        mesh=mesh,
        in_specs=placed,
        out_specs=(
            P(("rep", "shard"), None, None),
            P(("rep", "shard"), None, None),
            P("shard"),
            P("shard", None),
            P("shard", None),
            P("shard", None),
            P("shard", None),
            P("shard"),
            P("shard", None),
            P("shard", None),
            P("shard", None),
        ),
        check_vma=False,
    )
```

```python
from functools import partial

import jax
import jax.numpy as jnp
from jax import lax
from jax.experimental import pallas as pl
from jax.experimental.pallas import tpu as pltpu
from jax.sharding import PartitionSpec as P

QUERY_HEADS = 15
KEY_VALUE_HEADS = 5
HEAD_SIZE = 64


EPS = 1e-05
NEGATIVE = -1e30


def angles(documents, head_dim):
    segment_length = documents.shape[0]
    places = jnp.arange(segment_length, dtype=jnp.int32)
    begins = jnp.concatenate([jnp.ones((1,), dtype=jnp.bool_), documents[1:] != documents[:-1]])
    starting = lax.cummax(jnp.where(begins, places, 0), axis=0)
    offsets = (places - starting).astype(jnp.float32)
    rates = 10000.0 ** (-2.0 * jnp.arange(head_dim // 2).astype(jnp.float32) / head_dim)
    phases = offsets[:, None] * rates[None, :]
    return (jnp.cos(phases)[:, None, :], jnp.sin(phases)[:, None, :])


def bit_swap(count, bit):
    return [(i, i ^ bit) for i in range(count)]


def swap_rep(value, bit):
    return lax.ppermute(value, "rep", bit_swap(lax.axis_size("rep"), bit))


def swap_shard(value, bit):
    return lax.ppermute(value, "shard", bit_swap(lax.axis_size("shard"), bit))


def rep_bit(bit):
    return (lax.axis_index("rep") // bit) % 2


def place_pair(mine, other, bit, axis):
    low = jnp.concatenate([mine, other], axis=axis)
    high = jnp.concatenate([other, mine], axis=axis)
    return jnp.where(bit == 0, low, high)


def gather_rows(piece):
    shards = lax.axis_size("shard")
    rows, columns = piece.shape
    quarter = rows // 4
    core, side = rep_bit(1), rep_bit(2)
    part = lax.dynamic_slice_in_dim(piece, (core * 2 + side) * quarter, quarter, 0)
    held = part[None]
    bit = 1
    while bit < shards:
        held = jnp.concatenate([held, swap_shard(held, bit)], axis=0)
        bit *= 2
    others = held[1:]
    others = place_pair(others, swap_rep(others, 2), side, 1)
    others = place_pair(others, swap_rep(others, 1), core, 1)
    me = lax.axis_index("shard")
    if shards == 2:
        return place_pair(piece, others[0], me, 0)
    whole = jnp.zeros((shards, rows, columns), piece.dtype)
    whole = lax.dynamic_update_slice_in_dim(whole, piece[None], me, 0)
    for j in range(1, shards):
        whole = lax.dynamic_update_slice_in_dim(whole, others[j - 1][None], me ^ j, 0)
    return whole.reshape(shards * rows, columns)


def add_up(left, right):
    return (left.astype(jnp.float32) + right.astype(jnp.float32)).astype(jnp.bfloat16)


def halve(value, bit, axis, swap):
    half = value.shape[axis] // 2
    mine = lax.dynamic_slice_in_dim(value, bit * half, half, axis)
    theirs = lax.dynamic_slice_in_dim(value, (1 - bit) * half, half, axis)
    return add_up(mine, swap(theirs))


def halve_shard(value):
    bit = lax.axis_size("shard") // 2
    while bit:
        value = halve(
            value, (lax.axis_index("shard") // bit) % 2, 0, partial(swap_shard, bit=bit)
        )
        bit //= 2
    return value


def reduce_rows(grad, order, axes):
    shards = lax.axis_size("shard")
    rows, columns = grad.shape
    value = grad.astype(jnp.bfloat16).reshape(shards, rows // shards, columns)
    value = halve(value, rep_bit(1), axes[1], partial(swap_rep, bit=1))
    for step in order:
        if step == 0:
            value = halve_shard(value)
        else:
            value = halve(value, rep_bit(step), axes[step], partial(swap_rep, bit=step))
    bit = 8
    while bit < lax.axis_size("rep"):
        value = add_up(value, swap_rep(value, bit))
        bit *= 2
    for step in [s for s in reversed(order) if s] + [1]:
        value = place_pair(value, swap_rep(value, step), rep_bit(step), axes[step])
    return value[0].astype(jnp.float32)


LANES = 128
BLOCK = 256
GROUP = QUERY_HEADS // KEY_VALUE_HEADS
SPAN = (GROUP + 2) * HEAD_SIZE
WIDE = -(-SPAN // LANES) * LANES
SCALE = HEAD_SIZE**-0.5
ROOM = 56 * 1024 * 1024


def dot(left, right):
    return jnp.dot(left, right, preferred_element_type=jnp.float32)


def dot_nt(left, right):
    return lax.dot_general(left, right, (((1,), (1,)), ((), ())), preferred_element_type=jnp.float32)


def dot_tn(left, right):
    return lax.dot_general(left, right, (((0,), (0,)), ((), ())), preferred_element_type=jnp.float32)


def lanes_of(shape):
    return lax.broadcasted_iota(jnp.int32, shape, len(shape) - 1)


def turn(pair, cosine, sine):
    lane = lanes_of(pair.shape) % HEAD_SIZE
    half = HEAD_SIZE // 2
    partner = jnp.where(
        lane < half, pltpu.roll(pair, LANES - half, 1), pltpu.roll(pair, half, 1)
    )
    return pair * cosine + partner * sine


def three_parts(column):
    high = column.astype(jnp.bfloat16)
    rest = column - high.astype(jnp.float32)
    middle = rest.astype(jnp.bfloat16)
    low = (rest - middle.astype(jnp.float32)).astype(jnp.bfloat16)
    return high, middle, low


def put_parts(base, column, first):
    lane = lanes_of(base.shape)
    for k, part in enumerate(three_parts(column)):
        base = jnp.where(lane == first + k, part.astype(jnp.float32), base)
    return base


def call(kernel, grid, in_specs, out_specs, out_shape, scratch=(), flops=0, prefetch=0, move=0):
    return pl.pallas_call(
        kernel,
        grid_spec=pltpu.PrefetchScalarGridSpec(
            num_scalar_prefetch=prefetch,
            grid=grid,
            in_specs=in_specs,
            out_specs=out_specs,
            scratch_shapes=list(scratch),
        ),
        out_shape=out_shape,
        compiler_params=pltpu.CompilerParams(
            dimension_semantics=("arbitrary",) * len(grid), vmem_limit_bytes=ROOM
        ),
        cost_estimate=pl.CostEstimate(flops=flops, bytes_accessed=move, transcendentals=0),
    )


def struct(shape, dtype):
    return jax.ShapeDtypeStruct(shape, dtype)


def whole(shape):
    return pl.BlockSpec(shape, lambda *_: (0,) * len(shape))


def window(at_ref, core, side, rows):
    half = rows // 2
    return core * half + side * (half - rows * 4 // 15)


def fill_rows(at_ref, whole_ref, own_ref, parts):
    rows, tall = own_ref.shape[0], parts[0].shape[0]
    x, side, core = at_ref[0], at_ref[1], at_ref[2]
    whole_ref[pl.ds(pl.multiple_of(x * rows, 16), rows), :] = own_ref[...]
    for k, part in enumerate(parts):
        c, y = core ^ (k // 2), side ^ (k % 2)
        start = (1 - x) * rows + window(at_ref, c, y, rows)
        whole_ref[pl.ds(pl.multiple_of(start, 16), tall), :] = part[...]


def project_kernel(
    at_ref, x_ref, doc_ref, cos_ref, sin_ref, wq_ref, wk_ref, wv_ref, spare_ref, p0, p1, p2, p3,
    flip_ref, q_ref, k_ref, v_ref, w_ref, gains_ref, in_ref, own_ref,
):
    step = pl.program_id(0)

    @pl.when(step == 0)
    def _():
        w_key, w_value = wk_ref[...].T, wv_ref[...].T
        deep = GROUP * HEAD_SIZE
        pad = jnp.zeros_like(spare_ref)
        columns = []
        for g in range(KEY_VALUE_HEADS):
            span = slice(g * HEAD_SIZE, (g + 1) * HEAD_SIZE)
            columns += [wq_ref[:, g * deep : (g + 1) * deep], w_key[:, span], w_value[:, span]]
            columns.append(pad if g else spare_ref[...])
        own_ref[...] = jnp.concatenate(columns, axis=1)
        fill_rows(at_ref, w_ref, own_ref, (p0, p1, p2, p3))
        x = x_ref[...].astype(jnp.float32)
        inverse = lax.rsqrt(jnp.mean(x * x, axis=0, keepdims=True) + EPS)
        first = SPAN % LANES
        spare = w_ref[:, SPAN - first : SPAN - first + LANES].astype(jnp.float32)
        gains_ref[...] = spare.T[first : first + 8, :]
        gain = spare[:, first : first + 1]
        flip = (x * inverse * gain).astype(jnp.bfloat16)
        flip_ref[...] = flip
        in_ref[...] = flip.T

    y = dot(in_ref[...], w_ref[:, pl.ds(pl.multiple_of(step * WIDE, LANES), WIDE)])
    cosine, sine = cos_ref[...], sin_ref[...]
    first = turn(y[:, :LANES], cosine, sine)
    second = turn(y[:, LANES : 2 * LANES], cosine, sine)
    lane = lanes_of(first.shape)
    inner = lane < HEAD_SIZE
    doc = doc_ref[...]
    same = ((lane - HEAD_SIZE) == doc).astype(jnp.float32)
    q_ref[0] = jnp.where(inner, first * SCALE, same).astype(jnp.bfloat16)
    q_ref[1] = jnp.where(inner, pltpu.roll(first, HEAD_SIZE, 1) * SCALE, same).astype(jnp.bfloat16)
    q_ref[2] = jnp.where(inner, second * SCALE, same).astype(jnp.bfloat16)
    away = jnp.where(
        lane < HEAD_SIZE + 4,
        jnp.where((lane - HEAD_SIZE) == doc, 0.0, NEGATIVE),
        jnp.where(lane < HEAD_SIZE + 7, 1.0, 0.0),
    )
    k_ref[0] = jnp.where(inner, pltpu.roll(second, HEAD_SIZE, 1), away).astype(jnp.bfloat16)
    ones = jnp.where(lane < HEAD_SIZE + 3, 1.0, 0.0)
    v_ref[0] = jnp.where(inner, y[:, 2 * LANES :], ones).astype(jnp.bfloat16)


def project(at, x, documents, cosine, sine, own, parts):
    width, rows = x.shape
    table = whole((rows, LANES))
    across = parts[0].shape[1]
    return call(
        project_kernel,
        (KEY_VALUE_HEADS,),
        [whole((width, rows)), whole((rows, 1)), table, table]
        + [whole(w.shape) for w in own]
        + [whole(parts[0].shape)] * 4,
        [
            whole((width, rows)),
            pl.BlockSpec((GROUP, rows, LANES), lambda g, a: (g, 0, 0)),
            pl.BlockSpec((1, rows, LANES), lambda g, a: (g, 0, 0)),
            pl.BlockSpec((1, rows, LANES), lambda g, a: (g, 0, 0)),
            whole((width, across)),
            whole((8, width)),
        ],
        [
            struct((width, rows), jnp.bfloat16),
            struct((QUERY_HEADS, rows, LANES), jnp.bfloat16),
            struct((KEY_VALUE_HEADS, rows, LANES), jnp.bfloat16),
            struct((KEY_VALUE_HEADS, rows, LANES), jnp.bfloat16),
            struct((width, across), jnp.bfloat16),
            struct((8, width), jnp.float32),
        ],
        scratch=[
            pltpu.VMEM((rows, width), jnp.bfloat16),
            pltpu.VMEM((width // 2, across), jnp.bfloat16),
        ],
        flops=2 * rows * width * WIDE * KEY_VALUE_HEADS,
        prefetch=1,
        move=20_000_000,
    )(at, x, documents, cosine, sine, *own, *parts)


def attend_kernel(q_ref, k_ref, v_ref, o_ref, qb_ref):
    rows = q_ref.shape[1]
    deep = GROUP * BLOCK
    row = lax.broadcasted_iota(jnp.int32, (GROUP, BLOCK, BLOCK), 1).reshape(deep, BLOCK)
    below = lanes_of((deep, BLOCK)) <= row
    for i in range(rows // BLOCK):
        here = pl.ds(i * BLOCK, BLOCK)
        q = q_ref[:, here, :].reshape(deep, LANES)
        near = jnp.where(below, dot_nt(q, k_ref[0, here, :]), NEGATIVE)
        top = jnp.max(near, axis=-1, keepdims=True)
        if i:
            past = pl.ds(0, i * BLOCK)
            far = dot_nt(q, k_ref[0, past, :])
            top = jnp.maximum(top, jnp.max(far, axis=-1, keepdims=True))
            total = dot(jnp.exp(far - top).astype(jnp.bfloat16), v_ref[0, past, :])
            total += dot(jnp.exp(near - top).astype(jnp.bfloat16), v_ref[0, here, :])
        else:
            total = dot(jnp.exp(near - top).astype(jnp.bfloat16), v_ref[0, here, :])
        summed = total[:, HEAD_SIZE : HEAD_SIZE + 1]
        out = (total / summed).reshape(GROUP, BLOCK, LANES)
        o_ref[0, here, :] = jnp.concatenate(
            [out[h][:, :HEAD_SIZE] for h in range(GROUP)], axis=1
        ).astype(jnp.bfloat16)
        back = put_parts(q.astype(jnp.float32), -(top + jnp.log(summed)), HEAD_SIZE + 4)
        qb_ref[:, here, :] = back.astype(jnp.bfloat16).reshape(GROUP, BLOCK, LANES)


def attend(q, k, v, first, groups):
    rows = q.shape[1]
    one = pl.BlockSpec((1, rows, LANES), lambda g: (g + first, 0, 0))
    three = pl.BlockSpec((GROUP, rows, LANES), lambda g: (g + first, 0, 0))
    return call(
        attend_kernel,
        (groups,),
        [three, one, one],
        [
            pl.BlockSpec((1, rows, GROUP * HEAD_SIZE), lambda g: (g, 0, 0)),
            pl.BlockSpec((GROUP, rows, LANES), lambda g: (g, 0, 0)),
        ],
        [
            struct((groups, rows, GROUP * HEAD_SIZE), jnp.bfloat16),
            struct((groups * GROUP, rows, LANES), jnp.bfloat16),
        ],
        flops=2 * 4 * rows * rows * LANES * GROUP * groups,
        move=3_000_000 * groups,
    )(q, k, v)


def blend_kernel(
    at_ref, x_ref, dy_ref, o_ref, gain_ref, own_ref, p0, p1, p2, p3,
    mid_ref, in_ref, flip_ref, back_ref, w_ref,
):
    @pl.when(pl.program_id(0) == 0)
    def _():
        fill_rows(at_ref, w_ref, own_ref, (p0, p1, p2, p3))

    total = x_ref[...].astype(jnp.float32).T
    deep = GROUP * HEAD_SIZE
    for g in range(KEY_VALUE_HEADS):
        heads = o_ref[g]
        total += dot(heads, w_ref[pl.ds(g * deep, deep), :])
    mid_ref[...] = total
    inverse = lax.rsqrt(jnp.mean(total * total, axis=-1, keepdims=True) + EPS)
    entry = (total * inverse * gain_ref[...]).astype(jnp.bfloat16)
    in_ref[...] = entry
    flip_ref[...] = entry.T
    back_ref[...] = dy_ref[...].T


def head_specs(heads):
    deep = GROUP * HEAD_SIZE
    return [pl.BlockSpec((h.shape[0], BLOCK, deep), lambda i, a: (0, i, 0)) for h in heads]


def blend(at, x, dy, heads, gain, own, parts):
    width, rows = x.shape
    band = pl.BlockSpec((BLOCK, width), lambda i, a: (i, 0))
    side = pl.BlockSpec((width, BLOCK), lambda i, a: (0, i))
    return call(
        blend_kernel,
        (rows // BLOCK,),
        [side, side]
        + head_specs(heads)
        + [whole((1, width)), whole(own.shape)]
        + [whole(parts[0].shape)] * 4,
        [band, band, side, band],
        [
            struct((rows, width), jnp.float32),
            struct((rows, width), jnp.bfloat16),
            struct((width, rows), jnp.bfloat16),
            struct((rows, width), jnp.bfloat16),
        ],
        scratch=[pltpu.VMEM((2 * own.shape[0], width), jnp.bfloat16)],
        flops=2 * rows * width * width,
        prefetch=1,
        move=18_000_000,
    )(at, x, dy, *heads, gain, own, *parts)


def mix_kernel(
    at_ref, in_ref, flip_ref, dy_ref, back_ref, gate_own, g0, g1, up_own, u0, u1, down_own, d0, d1,
    y_ref, din_ref, gg_ref, gu_ref, gd_ref, gate_ref, up_ref, down_ref,
):
    step = pl.program_id(0)
    x, side = at_ref[0], at_ref[1]
    rows = gate_own.shape[0]
    mine = pl.ds(pl.multiple_of(x * rows, 16), rows)
    theirs = pl.ds(pl.multiple_of((1 - x) * rows, 16), rows)
    gate_ref[mine, :] = gate_own[...]
    up_ref[mine, :] = up_own[...]

    @pl.when(step == side)
    def _():
        gate_ref[theirs, :] = g0[...]
        up_ref[theirs, :] = u0[...]

    @pl.when(step != side)
    def _():
        gate_ref[theirs, :] = g1[...]
        up_ref[theirs, :] = u1[...]

    @pl.when(step == x)
    def _():
        down_ref[...] = down_own[...]

    @pl.when(step != x)
    def _():
        down_ref[pl.ds(pl.multiple_of(side * rows, 16), rows), :] = d0[...]
        down_ref[pl.ds(pl.multiple_of((1 - side) * rows, 16), rows), :] = d1[...]

    entry, dy = in_ref[...], dy_ref[...]
    w_gate, w_up, w_down = gate_ref[...], up_ref[...], down_ref[...]
    gate = dot(entry, w_gate)
    up = dot(entry, w_up)
    sigmoid = jax.nn.sigmoid(gate)
    active = gate * sigmoid
    hidden = (active * up).astype(jnp.bfloat16)
    hidden_grad = dot(dy, w_down)
    gate_grad = (hidden_grad * up * sigmoid * (1.0 + gate * (1.0 - sigmoid))).astype(jnp.bfloat16)
    up_grad = (hidden_grad * active).astype(jnp.bfloat16)
    gd_ref[0] = dot(back_ref[...], hidden).astype(jnp.bfloat16)
    gg_ref[...] = dot(flip_ref[...], gate_grad).astype(jnp.bfloat16)
    gu_ref[...] = dot(flip_ref[...], up_grad).astype(jnp.bfloat16)
    y = dot_nt(hidden, w_down)
    din = dot_nt(gate_grad, w_gate) + dot_nt(up_grad, w_up)

    @pl.when(step == 0)
    def _():
        y_ref[...] = y
        din_ref[...] = din

    @pl.when(step > 0)
    def _():
        y_ref[...] += y
        din_ref[...] += din


def mix(at, entry, flip, dy, back, gate, up, down):
    rows, width = entry.shape
    cut = gate[1].shape[1]
    full, turned = whole((rows, width)), whole((width, rows))
    side = pl.BlockSpec((width // 2, cut), lambda i, a: (0, 2 * i + a[3]))
    piece = whole((width // 2, cut))
    grad = pl.BlockSpec((width, cut), lambda i, a: (0, i))
    return call(
        mix_kernel,
        (2,),
        [full, turned, full, turned, side, piece, piece, side, piece, piece]
        + [pl.BlockSpec((width, cut), lambda i, a: (0, a[3])), piece, piece],
        [full, full, grad, grad, pl.BlockSpec((1, width, cut), lambda i, a: (i, 0, 0))],
        [
            struct((rows, width), jnp.float32),
            struct((rows, width), jnp.float32),
            struct((width, 2 * cut), jnp.bfloat16),
            struct((width, 2 * cut), jnp.bfloat16),
            struct((2, width, cut), jnp.bfloat16),
        ],
        scratch=[pltpu.VMEM((width, cut), jnp.bfloat16)] * 3,
        flops=2 * 9 * rows * width * cut * 2,
        prefetch=1,
        move=30_000_000,
    )(at, entry, flip, dy, back, *gate, *up, *down)


def middle_kernel(
    at_ref, mid_ref, y0_ref, y1_ref, d0_ref, d1_ref, dy_ref, o_ref, gain_ref,
    own_ref, p0, p1, p2, p3, mixed_ref, grad_ref, branch_ref, do_ref, gain_out, w_ref,
):
    step = pl.program_id(0)

    @pl.when(step == 0)
    def _():
        fill_rows(at_ref, w_ref, own_ref, (p0, p1, p2, p3))
        gain_out[...] = jnp.zeros_like(gain_out)

    middle = mid_ref[...]
    mixed_ref[...] = (middle + y0_ref[...] + y1_ref[...]).astype(jnp.bfloat16).T
    inverse = lax.rsqrt(jnp.mean(middle * middle, axis=-1, keepdims=True) + EPS)
    normed = middle * inverse
    back = d0_ref[...] + d1_ref[...]
    product = back * normed
    mean = jnp.mean(product * gain_ref[...], axis=-1, keepdims=True)
    grad = dy_ref[...].astype(jnp.float32) + inverse * (back * gain_ref[...] - normed * mean)
    grad_ref[...] = grad
    branch = grad.astype(jnp.bfloat16)
    branch_ref[...] = branch
    gain_out[...] += jnp.sum(product, axis=0, keepdims=True)
    deep = GROUP * HEAD_SIZE
    lane = lanes_of((BLOCK, LANES))
    inner = lane < HEAD_SIZE
    for g in range(KEY_VALUE_HEADS):
        heads = o_ref[g]
        upstream = dot_nt(branch, w_ref[pl.ds(g * deep, deep), :]).astype(jnp.bfloat16)
        upstream = upstream.astype(jnp.float32)
        both = upstream * heads.astype(jnp.float32)
        pair, pair_both = upstream[:, :LANES], both[:, :LANES]
        wide = (pair, pltpu.roll(pair, HEAD_SIZE, 1), upstream[:, LANES:])
        sums = (
            jnp.sum(jnp.where(inner, pair_both, 0.0), axis=-1, keepdims=True),
            jnp.sum(jnp.where(inner, 0.0, pair_both), axis=-1, keepdims=True),
            jnp.sum(both[:, LANES:], axis=-1, keepdims=True),
        )
        for h in range(GROUP):
            delta = -sums[h]
            high = delta.astype(jnp.bfloat16).astype(jnp.float32)
            low = delta - high
            own = wide[h]
            if own.shape[1] < LANES:
                own = jnp.concatenate([own, jnp.zeros_like(own)], axis=1)
            rest = jnp.where(lane == HEAD_SIZE, high, jnp.where(lane == HEAD_SIZE + 1, low, 0.0))
            do_ref[g * GROUP + h] = jnp.where(inner, own, rest).astype(jnp.bfloat16)


def middle_back(at, middle, y0, y1, d0, d1, dy, heads, gain, own, parts):
    rows, width = middle.shape
    band = pl.BlockSpec((BLOCK, width), lambda i, a: (i, 0))
    return call(
        middle_kernel,
        (rows // BLOCK,),
        [band] * 6
        + head_specs(heads)
        + [whole((1, width)), whole(own.shape)]
        + [whole(parts[0].shape)] * 4,
        [
            pl.BlockSpec((width, BLOCK), lambda i, a: (0, i)),
            band,
            band,
            pl.BlockSpec((QUERY_HEADS, BLOCK, LANES), lambda i, a: (0, i, 0)),
            whole((1, width)),
        ],
        [
            struct((width, rows), jnp.bfloat16),
            struct((rows, width), jnp.float32),
            struct((rows, width), jnp.bfloat16),
            struct((QUERY_HEADS, rows, LANES), jnp.bfloat16),
            struct((1, width), jnp.float32),
        ],
        scratch=[pltpu.VMEM((2 * own.shape[0], width), jnp.bfloat16)],
        flops=2 * rows * width * width,
        prefetch=1,
        move=30_000_000,
    )(at, middle, y0, y1, d0, d1, dy, *heads, gain, own, *parts)


def attend_back_kernel(q_ref, k_ref, v_ref, do_ref, cos_ref, sin_ref, out_ref, dq_ref):
    rows = q_ref.shape[1]
    count = rows // BLOCK
    after = lax.broadcasted_iota(jnp.int32, (BLOCK, BLOCK), 0) <= lanes_of((BLOCK, BLOCK))
    key_grads, value_grads = [], []
    for j in range(count):
        here = pl.ds(j * BLOCK, BLOCK)
        k, v = k_ref[0, here, :], v_ref[0, here, :]
        dk = jnp.zeros((BLOCK, LANES), jnp.float32)
        dv = jnp.zeros((BLOCK, LANES), jnp.float32)
        for h in range(GROUP):
            for start, size in ((j * BLOCK, BLOCK), ((j + 1) * BLOCK, rows - (j + 1) * BLOCK)):
                if not size:
                    continue
                span = pl.ds(start, size)
                q, do = q_ref[h, span, :], do_ref[h, span, :]
                scores = dot_nt(k, q)
                if start == j * BLOCK:
                    scores = jnp.where(after, scores, NEGATIVE)
                probs = jnp.exp(scores)
                score_grad = (probs * dot_nt(v, do)).astype(jnp.bfloat16)
                dv += dot(probs.astype(jnp.bfloat16), do)
                dk += dot(score_grad, q)
                dq = dot_tn(score_grad, k)
                if j == 0:
                    dq_ref[h, span, :] = dq
                else:
                    dq_ref[h, span, :] += dq
        key_grads.append(dk)
        value_grads.append(dv)
    cosine, sine = cos_ref[...], -sin_ref[...]
    half = HEAD_SIZE
    parts = [turn(dq_ref[h] * SCALE, cosine, sine)[:, :half] for h in range(GROUP)]
    parts.append(turn(jnp.concatenate(key_grads, axis=0), cosine, sine)[:, :half])
    parts.append(jnp.concatenate(value_grads, axis=0)[:, :half])
    parts.append(jnp.zeros((rows, WIDE - SPAN), jnp.float32))
    out_ref[0] = jnp.concatenate(parts, axis=1).astype(jnp.bfloat16)


def attend_back(q, k, v, do, cosine, sine, first, groups):
    rows = q.shape[1]
    one = pl.BlockSpec((1, rows, LANES), lambda g: (g + first, 0, 0))
    table = whole((rows, LANES))
    return call(
        attend_back_kernel,
        (groups,),
        [
            pl.BlockSpec((GROUP, rows, LANES), lambda g: (g + first, 0, 0)),
            one,
            one,
            pl.BlockSpec((GROUP, rows, LANES), lambda g: (g + first, 0, 0)),
            table,
            table,
        ],
        pl.BlockSpec((1, rows, WIDE), lambda g: (g, 0, 0)),
        struct((groups, rows, WIDE), jnp.bfloat16),
        scratch=[pltpu.VMEM((GROUP, rows, LANES), jnp.float32)],
        flops=2 * 10 * rows * rows * LANES * GROUP * groups,
        move=3_000_000 * groups,
    )(q, k, v, do, cosine, sine)


def weight_kernel(flip_ref, *refs):
    flip = flip_ref[...]
    parts = [
        dot(flip, ref[g])[:, :SPAN].astype(jnp.bfloat16)
        for ref in refs[:-1]
        for g in range(ref.shape[0])
    ]
    refs[-1][...] = jnp.concatenate(parts, axis=1)


def weight_grads(flip, backs):
    width, rows = flip.shape
    half = width // 2
    across = sum(b.shape[0] for b in backs) * SPAN
    return call(
        weight_kernel,
        (2,),
        [pl.BlockSpec((half, rows), lambda i: (i, 0))] + [whole(b.shape) for b in backs],
        pl.BlockSpec((half, across), lambda i: (i, 0)),
        struct((width, across), jnp.bfloat16),
        flops=2 * rows * width * across,
        move=10_000_000,
    )(flip, *backs)


def near_kernel(flip_ref, back_ref, branch_ref, o_ref, out_ref):
    deep = GROUP * HEAD_SIZE
    branch = branch_ref[...]
    for g in range(KEY_VALUE_HEADS):
        heads = o_ref[g]
        span = pl.ds(g * deep, deep)
        left = dot_tn(heads, branch)
        right = dot(flip_ref[span, :], back_ref[0])[:, :SPAN]
        out_ref[span, :] = jnp.concatenate([left, right], axis=1).astype(jnp.bfloat16)


def near_grads(flip, back, branch, heads):
    width, rows = flip.shape
    args = (flip, back, branch, *heads)
    return call(
        near_kernel,
        (1,),
        [whole(a.shape) for a in args],
        whole((width, width + SPAN)),
        struct((width, width + SPAN), jnp.bfloat16),
        flops=2 * rows * width * (width + SPAN),
        move=12_000_000,
    )(*args)


def finish_kernel(x_ref, mid_ref, *refs):
    *backs, gain_ref, w_ref, out_ref, gain_out = refs
    groups = [ref[g] for ref in backs for g in range(ref.shape[0])]
    x = x_ref[...].astype(jnp.float32).T
    inverse = lax.rsqrt(jnp.mean(x * x, axis=-1, keepdims=True) + EPS)
    normed = x * inverse
    back = jnp.zeros_like(x)
    for g in range(KEY_VALUE_HEADS):
        back += dot_nt(groups[g], w_ref[:, pl.ds(g * WIDE, WIDE)])
    product = back * normed

    @pl.when(pl.program_id(0) == 0)
    def _():
        gain_out[...] = jnp.zeros_like(gain_out)

    gain_out[...] += jnp.sum(product, axis=0, keepdims=True)
    mean = jnp.mean(product * gain_ref[...], axis=-1, keepdims=True)
    grad = mid_ref[...] + inverse * (back * gain_ref[...] - normed * mean)
    out_ref[...] = grad.astype(jnp.bfloat16).T


def finish(x, middle_grad, backs, gain, w_first):
    width, rows = x.shape
    side = pl.BlockSpec((width, BLOCK), lambda i: (0, i))
    return call(
        finish_kernel,
        (rows // BLOCK,),
        [side, pl.BlockSpec((BLOCK, width), lambda i: (i, 0))]
        + [pl.BlockSpec((b.shape[0], BLOCK, WIDE), lambda i: (0, i, 0)) for b in backs]
        + [whole((1, width)), whole(w_first.shape)],
        [side, whole((1, width))],
        [struct((width, rows), jnp.bfloat16), struct((1, width), jnp.float32)],
        flops=2 * rows * width * WIDE * KEY_VALUE_HEADS,
        move=14_000_000,
    )(x, middle_grad, *backs, gain, w_first)


def widen_kernel(at_ref, mine_ref, other_ref, out_ref):
    cut = mine_ref.shape[2]
    mine, other = mine_ref[0].astype(jnp.float32), other_ref[0].astype(jnp.float32)

    @pl.when(at_ref[2] == 0)
    def _():
        out_ref[:, :cut] = mine
        out_ref[:, cut:] = other

    @pl.when(at_ref[2] != 0)
    def _():
        out_ref[:, :cut] = other
        out_ref[:, cut:] = mine


def came_at(at, j, order):
    apart = {2: at[1] ^ (j // 2), 4: at[4] ^ (j % 2)}
    return apart[order[0]] + 2 * apart[order[1]]


def widen(at, mine, other, order, spread):
    _, rows, columns = mine.shape
    if spread:
        shape = (2 * rows, 4 * columns)
        out = pl.BlockSpec((rows, 2 * columns), lambda j, a: (j % 2, j // 2))
    else:
        shape = (4 * rows, 2 * columns)
        out = pl.BlockSpec((rows, 2 * columns), lambda j, a: (j, 0))
    return call(
        widen_kernel,
        (4,),
        [pl.BlockSpec((1, rows, columns), lambda j, a: (came_at(a, j, order), 0, 0))] * 2,
        out,
        struct(shape, jnp.float32),
        prefetch=1,
        move=10_000_000,
    )(at, mine, other)


def unpack_kernel(
    at_ref, near0, near1, mid0, mid1, far0, far1, q_ref, k_ref, v_ref, out_ref,
    near_ref, mid_ref, far_ref,
):
    core, side = at_ref[2], at_ref[1]
    rows, columns = near0.shape[1:]
    for j in range(4):
        at = came_at(at_ref, j, (4, 2))
        mine, other = near0[at].astype(jnp.float32), near1[at].astype(jnp.float32)
        left, right = jnp.where(core == 0, mine, other), jnp.where(core == 0, other, mine)
        near_ref[j * rows : (j + 1) * rows, :] = jnp.concatenate([left, right], axis=1)
    for mine_ref, other_ref, into in ((mid0, mid1, mid_ref), (far0, far1, far_ref)):
        for c in range(2):
            for y in range(2):
                at = y ^ side
                mine, other = mine_ref[at].astype(jnp.float32), other_ref[at].astype(jnp.float32)
                start = (2 * c + y) * mine.shape[0]
                into[start : start + mine.shape[0], :] = jnp.where(core == c, mine, other)
    near, mid, far = near_ref[...], mid_ref[...], far_ref[...]
    deep = GROUP * HEAD_SIZE
    split = near.shape[1] - SPAN
    groups = [near[:, split:], mid[:, :SPAN], mid[:, SPAN:], far[:, :SPAN], far[:, SPAN:]]
    out_ref[...] = near[:, :split]
    q_ref[...] = jnp.concatenate([g[:, :deep] for g in groups], axis=1)
    k_ref[...] = jnp.concatenate([g[:, deep : deep + HEAD_SIZE] for g in groups], axis=1).T
    v_ref[...] = jnp.concatenate([g[:, deep + HEAD_SIZE :] for g in groups], axis=1).T


def unpack(at, near, mid, far):
    _, rows, columns = near[0].shape
    args = (*near, *mid, *far)
    tall = 4 * rows
    key_columns = KEY_VALUE_HEADS * HEAD_SIZE
    shapes = [
        (tall, QUERY_HEADS * HEAD_SIZE),
        (key_columns, tall),
        (key_columns, tall),
        (tall, 2 * columns - SPAN),
    ]
    return call(
        unpack_kernel,
        (1,),
        [whole(a.shape) for a in args],
        [whole(shape) for shape in shapes],
        [struct(shape, jnp.float32) for shape in shapes],
        scratch=[
            pltpu.VMEM((tall, 2 * columns), jnp.float32),
            pltpu.VMEM((tall, 2 * SPAN), jnp.float32),
            pltpu.VMEM((tall, 2 * SPAN), jnp.float32),
        ],
        prefetch=1,
        move=8_000_000,
    )(at, *args)


def tie(value, *others):
    return lax.optimization_barrier((value, *others))[0]


def spare_columns(gain_attn, gain_mlp):
    return jnp.pad(jnp.stack([gain_attn, gain_mlp], axis=1), ((0, 0), (0, WIDE - SPAN - 2)))


def first_rows(w_query, w_key, w_value, spare):
    deep = GROUP * HEAD_SIZE
    columns = []
    for g in range(KEY_VALUE_HEADS):
        columns.append(w_query[:, g * deep : (g + 1) * deep])
        columns.append(w_key[:, g * HEAD_SIZE : (g + 1) * HEAD_SIZE])
        columns.append(w_value[:, g * HEAD_SIZE : (g + 1) * HEAD_SIZE])
        columns.append(spare if g == 0 else jnp.zeros_like(spare))
    return jnp.concatenate(columns, axis=1)


def spread_rows(received):
    beside = swap_rep(received, 2)
    return [received, beside, swap_rep(received, 1), swap_rep(beside, 1)]


def start_sum(send, keep):
    return add_up(keep, swap_rep(send, 1))


def one_step(value, step, axes):
    if step == 0:
        return halve_shard(value)
    return halve(value, rep_bit(step), axes[step], partial(swap_rep, bit=step))


def over_z(value):
    bit = 8
    while bit < lax.axis_size("rep"):
        other = swap_rep(value, bit)
        value = value + other if value.dtype == jnp.float32 else add_up(value, other)
        bit *= 2
    return value


def begin_z(value):
    bit, last = 8, lax.axis_size("rep") // 2
    while bit < last:
        value = add_up(value, swap_rep(value, bit))
        bit *= 2
    return value, (swap_rep(value, last) if last >= 8 else jnp.zeros_like(value))


def end_z(begun, after):
    return add_up(tie(begun[0], after), begun[1])


def back_step(value, step):
    return jnp.concatenate([value, swap_rep(value, step)], axis=0)


def split_cores(grad, axis):
    core = rep_bit(1)
    half = grad.shape[axis] // 2
    send = lax.dynamic_slice_in_dim(grad, (1 - core) * half, half, axis)
    keep = lax.dynamic_slice_in_dim(grad, core * half, half, axis)
    return send, keep


def per_device(
    tokens,
    segments,
    gain_attn,
    w_query,
    key_weight_matrix,
    value_weight_matrix,
    w_out,
    gain_mlp,
    w_gate,
    w_up,
    w_down,
    cotangent,
):
    shards = lax.axis_size("shard")
    fast = shards == 2
    rows, width = tokens.shape[1:]
    half = width // 2
    columns = QUERY_HEADS * HEAD_SIZE
    key_columns = KEY_VALUE_HEADS * HEAD_SIZE
    inner = w_gate.shape[1]
    cut = inner // 4
    x_t = tokens[0].T
    dy_t = cotangent[0].T
    tall = half * 4 // 15
    zero = jnp.int32(0)
    spare = spare_columns(gain_attn, gain_mlp)

    if fast:
        x, side, core, depth = lax.axis_index("shard"), rep_bit(2), rep_bit(1), rep_bit(4)
        x, side, core, depth = (v.astype(jnp.int32) for v in (x, side, core, depth))
        other = 1 - core
        start = window(None, core, side, half)
        narrow = partial(lax.dynamic_slice_in_dim, start_index=start, slice_size=tall, axis=0)
        part_first = first_rows(
            narrow(w_query),
            narrow(key_weight_matrix),
            narrow(value_weight_matrix),
            narrow(spare),
        )
        own_first = (w_query, key_weight_matrix.T, value_weight_matrix.T, spare)
        column = (2 * side + other) * cut
        beside = (2 * (1 - side) + other) * cut
        own_down = w_down.T
        part_up = lax.dynamic_slice_in_dim(w_up, column, cut, 1)
        part_first, part_up = lax.optimization_barrier((part_first, part_up))
        part_down = lax.dynamic_slice(own_down, (side * half, other * cut), (half, cut))
        part_down = tie(part_down, part_up)
        part_out = tie(narrow(w_out), part_down)
        part_gate = tie(lax.dynamic_slice_in_dim(w_gate, column, cut, 1), part_down)
        part_beside = tie(lax.dynamic_slice_in_dim(w_gate, beside, cut, 1), part_down)
        came_first = swap_shard(part_first, 1)
        came_up, came_down = swap_shard(part_up, 1), swap_shard(part_down, 1)
        came_out = swap_shard(part_out, 1)
        came_gate = [swap_shard(part_gate, 1), swap_shard(part_beside, 1)]
        parts_first = spread_rows(came_first)
        own_out, own_gate, own_up = w_out, w_gate, w_up
    else:
        x = side = core = depth = zero
        other = 1 - core
        full_first = [gather_rows(w) for w in (w_query, key_weight_matrix, value_weight_matrix)]
        full_out = gather_rows(w_out)
        starts = [half + window(None, c, y, half) for c in (0, 1) for y in (0, 1)]
        full_first.append(gather_rows(jnp.pad(spare, ((0, 0), (0, 64))))[:, : WIDE - SPAN])
        own_first = (
            full_first[0][:half], full_first[1][:half].T, full_first[2][:half].T,
            full_first[3][:half],
        )
        parts_first = [first_rows(*(w[s : s + tall] for w in full_first)) for s in starts]
        own_out, parts_out = full_out[:half], [full_out[s : s + tall] for s in starts]
        def cut_up(value):
            blocks = [value[half:, k * cut : (k + 1) * cut] for k in range(4)]
            return value[:half], [blocks[1], blocks[3], blocks[0], blocks[2]]

        own_gate, parts_gate = cut_up(gather_rows(w_gate))
        own_up, parts_up = cut_up(gather_rows(w_up))
        full_down = gather_rows(w_down).T
        own_down = full_down[:, : 2 * cut]
        parts_down = [
            full_down[r : r + half, (2 + c) * cut : (3 + c) * cut]
            for c in (1, 0)
            for r in (0, half)
        ]

    at = jnp.stack([x, side, core, core, depth])
    at_other = jnp.stack([x, side, core, other, depth])
    cosine, sine = angles(segments[0], HEAD_SIZE)
    cosine, sine = cosine[:, 0], sine[:, 0]
    cosine, sine = (
        jnp.concatenate([cosine] * 4, axis=1),
        jnp.concatenate([-sine, sine, -sine, sine], axis=1),
    )

    flip_one, q, k, v, w_first, gains = project(
        at, x_t, segments[0][:, None], cosine, sine, own_first, parts_first
    )
    gain_one, gain_two = gains[:1], gains[1:2]
    if fast:
        q, came_up, came_down, came_out = lax.optimization_barrier(
            (q, came_up, came_down, came_out)
        )
        parts_up, parts_down = spread_rows(came_up), spread_rows(came_down)
        parts_out = spread_rows(came_out)
    heads0, back0 = attend(q, k, v, 0, KEY_VALUE_HEADS)
    heads = (heads0,)
    if fast:
        came_gate = [tie(came, heads0) for came in came_gate]
        parts_gate = came_gate + [swap_rep(came, 1) for came in came_gate]
    middle, entry, flip, dy = blend(at, x_t, dy_t, heads, gain_two, own_out, parts_out)
    y0, d0, gate0, up0, down0 = mix(
        at_other, entry, flip, dy, dy_t,
        (own_gate, *parts_gate[:2]), (own_up, *parts_up[:2]), (own_down, *parts_down[:2]),
    )
    y1, d1, gate1, up1, down1 = mix(
        at, tie(entry, d0), flip, dy, dy_t,
        (own_gate, *parts_gate[2:]), (own_up, *parts_up[2:]), (own_down, *parts_down[2:]),
    )
    wide, tower, low = {2: 2, 4: 1}, {2: 1, 4: 1}, {2: 1}
    cube = (2, half, -1)
    if fast:
        gate = start_sum(gate0.reshape(cube), gate1.reshape(cube))
        up = start_sum(up0.reshape(cube), up1.reshape(cube))
        down = start_sum(down0, down1)
        y1, gate, up, down = lax.optimization_barrier((y1, gate, up, down))
        gate, up, down = one_step(gate, 0, wide), one_step(up, 4, wide), one_step(down, 2, tower)
    mixed, middle_grad, branch, do, grad_gain_two = middle_back(
        at, middle, y0, y1, d0, d1, dy, heads, gain_two, own_out, parts_out
    )
    backs = []

    def group_back(do, groups=1):
        g = sum(back.shape[0] for back in backs)
        backs.append(attend_back(back0, k, v, do, cosine, sine, g, groups))

    group_back(do)
    if fast:
        gate, up, down, backs[0] = lax.optimization_barrier((gate, up, down, backs[0]))
        gate, up, down = one_step(gate, 2, wide), one_step(up, 0, wide), one_step(down, 4, tower)
    near = near_grads(flip_one, backs[0], branch, heads)
    group_back(tie(do, near))
    if fast:
        near = start_sum(*split_cores(near.reshape(cube), 2))
        gate, up, down, near, backs[1] = lax.optimization_barrier(
            (gate, up, down, near, backs[1])
        )
        gate, up, down = one_step(gate, 4, wide), one_step(up, 2, wide), one_step(down, 0, tower)
        near = one_step(near, 2, tower)
    group_back(tie(do, backs[1]))
    if fast:
        gate, up, down, backs[2] = lax.optimization_barrier((gate, up, down, backs[2]))
        gate, up, down = begin_z(gate), begin_z(up), begin_z(down)
    mid = weight_grads(flip_one, backs[1:3])
    if fast:
        mid = start_sum(*split_cores(mid.reshape(cube), 1))
    group_back(tie(do, mid), 2)
    if fast:
        gate, up, down = (end_z(part, backs[3]) for part in (gate, up, down))
        gate, up, near, mid, backs[3] = lax.optimization_barrier((gate, up, near, mid, backs[3]))
        gate, up = back_step(gate, 4), back_step(up, 2)
        near, mid = one_step(near, 4, tower), one_step(mid, 0, low)
    far = weight_grads(flip_one, backs[3:])
    if fast:
        far = start_sum(*split_cores(far.reshape(cube), 1))
        far, gate, down, near, mid, middle_grad = lax.optimization_barrier(
            (far, gate, down, near, mid, middle_grad)
        )
        far = one_step(far, 0, low)
        gate, down = back_step(gate, 2), back_step(down, 4)
        near, mid = one_step(near, 0, tower), one_step(mid, 2, low)
    grad_tokens, grad_gain_one = finish(x_t, middle_grad, backs, gain_one, w_first)
    gain_sums = jnp.concatenate([grad_gain_one, grad_gain_two])
    if fast:
        far, near, mid, up, gate, down, gain_sums = lax.optimization_barrier(
            (far, near, mid, up, gate, down, gain_sums)
        )
        far = one_step(far, 2, low)
        gain_sums += swap_shard(gain_sums, 1)
        up, mid, near = back_step(up, 4), over_z(mid), over_z(near)
        sum_gate = widen(at, gate, swap_rep(gate, 1), (4, 2), True)
        far, gain_sums, mid, sum_gate = lax.optimization_barrier((far, gain_sums, mid, sum_gate))
        far = over_z(far)
        gain_sums += swap_rep(gain_sums, 1)
        down, mid = back_step(down, 2), add_up(mid, swap_rep(mid, 4))
        far, gain_sums, up, near = lax.optimization_barrier((far, gain_sums, up, near))
        far = add_up(far, swap_rep(far, 4))
        gain_sums = over_z(gain_sums)
        near = back_step(near, 4)
        sum_up = widen(at, up, swap_rep(up, 1), (2, 4), True)
        far, gain_sums, sum_up, near, down, mid = lax.optimization_barrier(
            (far, gain_sums, sum_up, near, down, mid)
        )
        far, near, mid = back_step(far, 2), back_step(near, 2), back_step(mid, 2)
        gain_sums += swap_rep(gain_sums, 2)
        sum_down = widen(at, down, swap_rep(down, 1), (4, 2), False).T
        far, near, mid, gain_sums, sum_down = lax.optimization_barrier(
            (far, near, mid, gain_sums, sum_down)
        )
        gain_sums += swap_rep(gain_sums, 4)
        grad_query, grad_key, grad_value, grad_out = unpack(
            at, (near, swap_rep(near, 1)), (mid, swap_rep(mid, 1)), (far, swap_rep(far, 1))
        )
        grad_key, grad_value = grad_key.T, grad_value.T
    else:
        def whole_grad(two, one):
            both = jnp.stack([one.reshape(width, 2, cut), two.reshape(width, 2, cut)], axis=2)
            return both.reshape(width, inner)

        gain_sums = lax.psum(gain_sums, ("rep", "shard"))
        across, upright = {1: 2, 2: 2, 4: 1}, {1: 1, 2: 1, 4: 1}
        sum_gate = reduce_rows(whole_grad(gate0, gate1), (0, 2, 4), across)
        sum_up = reduce_rows(whole_grad(up0, up1), (4, 0, 2), across)
        downs = [d.transpose(1, 0, 2) for d in (down0, down1)]
        sum_down = reduce_rows(whole_grad(*downs).T, (2, 0, 4), upright)
        sums = [reduce_rows(part, (0, 2, 4), across) for part in (near, mid, far)]
        tall_rows = sums[0].shape[0]
        grad_out = sums[0][:, :columns]
        groups = jnp.concatenate([sums[0][:, columns:], *sums[1:]], axis=1)
        groups = groups.reshape(tall_rows, KEY_VALUE_HEADS, SPAN)
        deep = GROUP * HEAD_SIZE
        grad_query = groups[:, :, :deep].reshape(tall_rows, columns)
        grad_key = groups[:, :, deep : deep + HEAD_SIZE].reshape(tall_rows, key_columns)
        grad_value = groups[:, :, deep + HEAD_SIZE :].reshape(tall_rows, key_columns)
    own = width // shards
    gain_sums = lax.dynamic_slice_in_dim(gain_sums, lax.axis_index("shard") * own, own, 1)
    return (
        mixed.T[None],
        grad_tokens.T[None],
        gain_sums[0],
        grad_query,
        grad_key,
        grad_value,
        grad_out,
        gain_sums[1],
        sum_gate,
        sum_up,
        sum_down,
    )


def solution(mesh):
    placed = (
        P(("rep", "shard"), None, None),
        P(("rep", "shard"), None),
        P("shard"),
        P("shard", None),
        P("shard", None),
        P("shard", None),
        P("shard", None),
        P("shard"),
        P("shard", None),
        P("shard", None),
        P("shard", None),
        P(("rep", "shard"), None, None),
    )
    return jax.shard_map(
        per_device,
        mesh=mesh,
        in_specs=placed,
        out_specs=(
            P(("rep", "shard"), None, None),
            P(("rep", "shard"), None, None),
            P("shard"),
            P("shard", None),
            P("shard", None),
            P("shard", None),
            P("shard", None),
            P("shard"),
            P("shard", None),
            P("shard", None),
            P("shard", None),
        ),
        check_vma=False,
    )
```

```python
from functools import partial

import jax
import jax.numpy as jnp
from jax import lax
from jax.experimental import pallas as pl
from jax.experimental.pallas import tpu as pltpu
from jax.sharding import PartitionSpec as P

QUERY_HEADS = 15
KEY_VALUE_HEADS = 5
HEAD_SIZE = 64


EPS = 1e-05
NEGATIVE = -1e30


def angles(documents, head_dim):
    segment_length = documents.shape[0]
    places = jnp.arange(segment_length, dtype=jnp.int32)
    begins = jnp.concatenate([jnp.ones((1,), dtype=jnp.bool_), documents[1:] != documents[:-1]])
    starting = lax.cummax(jnp.where(begins, places, 0), axis=0)
    offsets = (places - starting).astype(jnp.float32)
    rates = 10000.0 ** (-2.0 * jnp.arange(head_dim // 2).astype(jnp.float32) / head_dim)
    phases = offsets[:, None] * rates[None, :]
    return (jnp.cos(phases)[:, None, :], jnp.sin(phases)[:, None, :])


def bit_swap(count, bit):
    return [(i, i ^ bit) for i in range(count)]


def swap_rep(value, bit):
    return lax.ppermute(value, "rep", bit_swap(lax.axis_size("rep"), bit))


def swap_shard(value, bit):
    return lax.ppermute(value, "shard", bit_swap(lax.axis_size("shard"), bit))


def rep_bit(bit):
    return (lax.axis_index("rep") // bit) % 2


def place_pair(mine, other, bit, axis):
    low = jnp.concatenate([mine, other], axis=axis)
    high = jnp.concatenate([other, mine], axis=axis)
    return jnp.where(bit == 0, low, high)


def gather_rows(piece):
    shards = lax.axis_size("shard")
    rows, columns = piece.shape
    quarter = rows // 4
    core, side = rep_bit(1), rep_bit(2)
    part = lax.dynamic_slice_in_dim(piece, (core * 2 + side) * quarter, quarter, 0)
    held = part[None]
    bit = 1
    while bit < shards:
        held = jnp.concatenate([held, swap_shard(held, bit)], axis=0)
        bit *= 2
    others = held[1:]
    others = place_pair(others, swap_rep(others, 2), side, 1)
    others = place_pair(others, swap_rep(others, 1), core, 1)
    me = lax.axis_index("shard")
    if shards == 2:
        return place_pair(piece, others[0], me, 0)
    whole = jnp.zeros((shards, rows, columns), piece.dtype)
    whole = lax.dynamic_update_slice_in_dim(whole, piece[None], me, 0)
    for j in range(1, shards):
        whole = lax.dynamic_update_slice_in_dim(whole, others[j - 1][None], me ^ j, 0)
    return whole.reshape(shards * rows, columns)


def add_up(left, right):
    return (left.astype(jnp.float32) + right.astype(jnp.float32)).astype(jnp.bfloat16)


def halve(value, bit, axis, swap):
    half = value.shape[axis] // 2
    mine = lax.dynamic_slice_in_dim(value, bit * half, half, axis)
    theirs = lax.dynamic_slice_in_dim(value, (1 - bit) * half, half, axis)
    return add_up(mine, swap(theirs))


def halve_shard(value):
    bit = lax.axis_size("shard") // 2
    while bit:
        value = halve(
            value, (lax.axis_index("shard") // bit) % 2, 0, partial(swap_shard, bit=bit)
        )
        bit //= 2
    return value


def reduce_rows(grad, order, axes):
    shards = lax.axis_size("shard")
    rows, columns = grad.shape
    value = grad.astype(jnp.bfloat16).reshape(shards, rows // shards, columns)
    value = halve(value, rep_bit(1), axes[1], partial(swap_rep, bit=1))
    for step in order:
        if step == 0:
            value = halve_shard(value)
        else:
            value = halve(value, rep_bit(step), axes[step], partial(swap_rep, bit=step))
    bit = 8
    while bit < lax.axis_size("rep"):
        value = add_up(value, swap_rep(value, bit))
        bit *= 2
    for step in [s for s in reversed(order) if s] + [1]:
        value = place_pair(value, swap_rep(value, step), rep_bit(step), axes[step])
    return value[0].astype(jnp.float32)


LANES = 128
BLOCK = 256
GROUP = QUERY_HEADS // KEY_VALUE_HEADS
SPAN = (GROUP + 2) * HEAD_SIZE
WIDE = -(-SPAN // LANES) * LANES
SCALE = HEAD_SIZE**-0.5
ROOM = 56 * 1024 * 1024


def dot(left, right):
    return jnp.dot(left, right, preferred_element_type=jnp.float32)


def dot_nt(left, right):
    return lax.dot_general(left, right, (((1,), (1,)), ((), ())), preferred_element_type=jnp.float32)


def dot_tn(left, right):
    return lax.dot_general(left, right, (((0,), (0,)), ((), ())), preferred_element_type=jnp.float32)


def lanes_of(shape):
    return lax.broadcasted_iota(jnp.int32, shape, len(shape) - 1)


def turn(pair, cosine, sine):
    lane = lanes_of(pair.shape) % HEAD_SIZE
    half = HEAD_SIZE // 2
    partner = jnp.where(
        lane < half, pltpu.roll(pair, LANES - half, 1), pltpu.roll(pair, half, 1)
    )
    return pair * cosine + partner * sine


def three_parts(column):
    high = column.astype(jnp.bfloat16)
    rest = column - high.astype(jnp.float32)
    middle = rest.astype(jnp.bfloat16)
    low = (rest - middle.astype(jnp.float32)).astype(jnp.bfloat16)
    return high, middle, low


def put_parts(base, column, first):
    lane = lanes_of(base.shape)
    for k, part in enumerate(three_parts(column)):
        base = jnp.where(lane == first + k, part.astype(jnp.float32), base)
    return base


def call(kernel, grid, in_specs, out_specs, out_shape, scratch=(), flops=0, prefetch=0, move=0):
    return pl.pallas_call(
        kernel,
        grid_spec=pltpu.PrefetchScalarGridSpec(
            num_scalar_prefetch=prefetch,
            grid=grid,
            in_specs=in_specs,
            out_specs=out_specs,
            scratch_shapes=list(scratch),
        ),
        out_shape=out_shape,
        compiler_params=pltpu.CompilerParams(
            dimension_semantics=("arbitrary",) * len(grid), vmem_limit_bytes=ROOM
        ),
        cost_estimate=pl.CostEstimate(flops=flops, bytes_accessed=move, transcendentals=0),
    )


def struct(shape, dtype):
    return jax.ShapeDtypeStruct(shape, dtype)


def whole(shape):
    return pl.BlockSpec(shape, lambda *_: (0,) * len(shape))


def window(at_ref, core, side, rows):
    half = rows // 2
    return core * half + side * (half - rows * 4 // 15)


def fill_rows(at_ref, whole_ref, own_ref, parts):
    rows, tall = own_ref.shape[0], parts[0].shape[0]
    x, side, core = at_ref[0], at_ref[1], at_ref[2]
    whole_ref[pl.ds(pl.multiple_of(x * rows, 16), rows), :] = own_ref[...]
    for k, part in enumerate(parts):
        c, y = core ^ (k // 2), side ^ (k % 2)
        start = (1 - x) * rows + window(at_ref, c, y, rows)
        whole_ref[pl.ds(pl.multiple_of(start, 16), tall), :] = part[...]


def project_kernel(
    at_ref, x_ref, doc_ref, cos_ref, sin_ref, wq_ref, wk_ref, wv_ref, spare_ref, p0, p1, p2, p3,
    flip_ref, q_ref, k_ref, v_ref, w_ref, gains_ref, in_ref, own_ref,
):
    step = pl.program_id(0)

    @pl.when(step == 0)
    def _():
        w_key, w_value = wk_ref[...].T, wv_ref[...].T
        deep = GROUP * HEAD_SIZE
        pad = jnp.zeros_like(spare_ref)
        columns = []
        for g in range(KEY_VALUE_HEADS):
            span = slice(g * HEAD_SIZE, (g + 1) * HEAD_SIZE)
            columns += [wq_ref[:, g * deep : (g + 1) * deep], w_key[:, span], w_value[:, span]]
            columns.append(pad if g else spare_ref[...])
        own_ref[...] = jnp.concatenate(columns, axis=1)
        fill_rows(at_ref, w_ref, own_ref, (p0, p1, p2, p3))
        x = x_ref[...].astype(jnp.float32)
        inverse = lax.rsqrt(jnp.mean(x * x, axis=0, keepdims=True) + EPS)
        first = SPAN % LANES
        spare = w_ref[:, SPAN - first : SPAN - first + LANES].astype(jnp.float32)
        gains_ref[...] = spare.T[first : first + 8, :]
        gain = spare[:, first : first + 1]
        flip = (x * inverse * gain).astype(jnp.bfloat16)
        flip_ref[...] = flip
        in_ref[...] = flip.T

    y = dot(in_ref[...], w_ref[:, pl.ds(pl.multiple_of(step * WIDE, LANES), WIDE)])
    cosine, sine = cos_ref[...], sin_ref[...]
    first = turn(y[:, :LANES], cosine, sine)
    second = turn(y[:, LANES : 2 * LANES], cosine, sine)
    lane = lanes_of(first.shape)
    inner = lane < HEAD_SIZE
    doc = doc_ref[...]
    same = ((lane - HEAD_SIZE) == doc).astype(jnp.float32)
    q_ref[0] = jnp.where(inner, first * SCALE, same).astype(jnp.bfloat16)
    q_ref[1] = jnp.where(inner, pltpu.roll(first, HEAD_SIZE, 1) * SCALE, same).astype(jnp.bfloat16)
    q_ref[2] = jnp.where(inner, second * SCALE, same).astype(jnp.bfloat16)
    away = jnp.where(
        lane < HEAD_SIZE + 4,
        jnp.where((lane - HEAD_SIZE) == doc, 0.0, NEGATIVE),
        jnp.where(lane < HEAD_SIZE + 7, 1.0, 0.0),
    )
    k_ref[0] = jnp.where(inner, pltpu.roll(second, HEAD_SIZE, 1), away).astype(jnp.bfloat16)
    ones = jnp.where(lane < HEAD_SIZE + 3, 1.0, 0.0)
    v_ref[0] = jnp.where(inner, y[:, 2 * LANES :], ones).astype(jnp.bfloat16)


def project(at, x, documents, cosine, sine, own, parts):
    width, rows = x.shape
    table = whole((rows, LANES))
    across = parts[0].shape[1]
    return call(
        project_kernel,
        (KEY_VALUE_HEADS,),
        [whole((width, rows)), whole((rows, 1)), table, table]
        + [whole(w.shape) for w in own]
        + [whole(parts[0].shape)] * 4,
        [
            whole((width, rows)),
            pl.BlockSpec((GROUP, rows, LANES), lambda g, a: (g, 0, 0)),
            pl.BlockSpec((1, rows, LANES), lambda g, a: (g, 0, 0)),
            pl.BlockSpec((1, rows, LANES), lambda g, a: (g, 0, 0)),
            whole((width, across)),
            whole((8, width)),
        ],
        [
            struct((width, rows), jnp.bfloat16),
            struct((QUERY_HEADS, rows, LANES), jnp.bfloat16),
            struct((KEY_VALUE_HEADS, rows, LANES), jnp.bfloat16),
            struct((KEY_VALUE_HEADS, rows, LANES), jnp.bfloat16),
            struct((width, across), jnp.bfloat16),
            struct((8, width), jnp.float32),
        ],
        scratch=[
            pltpu.VMEM((rows, width), jnp.bfloat16),
            pltpu.VMEM((width // 2, across), jnp.bfloat16),
        ],
        flops=2 * rows * width * WIDE * KEY_VALUE_HEADS,
        prefetch=1,
        move=20_000_000,
    )(at, x, documents, cosine, sine, *own, *parts)


def attend_kernel(q_ref, k_ref, v_ref, o_ref, qb_ref):
    rows = q_ref.shape[1]
    deep = GROUP * BLOCK
    row = lax.broadcasted_iota(jnp.int32, (GROUP, BLOCK, BLOCK), 1).reshape(deep, BLOCK)
    below = lanes_of((deep, BLOCK)) <= row
    for i in range(rows // BLOCK):
        here = pl.ds(i * BLOCK, BLOCK)
        q = q_ref[:, here, :].reshape(deep, LANES)
        near = jnp.where(below, dot_nt(q, k_ref[0, here, :]), NEGATIVE)
        top = jnp.max(near, axis=-1, keepdims=True)
        if i:
            past = pl.ds(0, i * BLOCK)
            far = dot_nt(q, k_ref[0, past, :])
            top = jnp.maximum(top, jnp.max(far, axis=-1, keepdims=True))
            total = dot(jnp.exp(far - top).astype(jnp.bfloat16), v_ref[0, past, :])
            total += dot(jnp.exp(near - top).astype(jnp.bfloat16), v_ref[0, here, :])
        else:
            total = dot(jnp.exp(near - top).astype(jnp.bfloat16), v_ref[0, here, :])
        summed = total[:, HEAD_SIZE : HEAD_SIZE + 1]
        out = (total / summed).reshape(GROUP, BLOCK, LANES)
        o_ref[0, here, :] = jnp.concatenate(
            [out[h][:, :HEAD_SIZE] for h in range(GROUP)], axis=1
        ).astype(jnp.bfloat16)
        back = put_parts(q.astype(jnp.float32), -(top + jnp.log(summed)), HEAD_SIZE + 4)
        qb_ref[:, here, :] = back.astype(jnp.bfloat16).reshape(GROUP, BLOCK, LANES)


def attend(q, k, v, first, groups):
    rows = q.shape[1]
    one = pl.BlockSpec((1, rows, LANES), lambda g: (g + first, 0, 0))
    three = pl.BlockSpec((GROUP, rows, LANES), lambda g: (g + first, 0, 0))
    return call(
        attend_kernel,
        (groups,),
        [three, one, one],
        [
            pl.BlockSpec((1, rows, GROUP * HEAD_SIZE), lambda g: (g, 0, 0)),
            pl.BlockSpec((GROUP, rows, LANES), lambda g: (g, 0, 0)),
        ],
        [
            struct((groups, rows, GROUP * HEAD_SIZE), jnp.bfloat16),
            struct((groups * GROUP, rows, LANES), jnp.bfloat16),
        ],
        flops=2 * 4 * rows * rows * LANES * GROUP * groups,
        move=3_000_000 * groups,
    )(q, k, v)


def blend_kernel(
    at_ref, x_ref, dy_ref, o_ref, gain_ref, own_ref, p0, p1, p2, p3,
    mid_ref, in_ref, flip_ref, back_ref, w_ref,
):
    @pl.when(pl.program_id(0) == 0)
    def _():
        fill_rows(at_ref, w_ref, own_ref, (p0, p1, p2, p3))

    total = x_ref[...].astype(jnp.float32).T
    deep = GROUP * HEAD_SIZE
    for g in range(KEY_VALUE_HEADS):
        heads = o_ref[g]
        total += dot(heads, w_ref[pl.ds(g * deep, deep), :])
    mid_ref[...] = total
    inverse = lax.rsqrt(jnp.mean(total * total, axis=-1, keepdims=True) + EPS)
    entry = (total * inverse * gain_ref[...]).astype(jnp.bfloat16)
    in_ref[...] = entry
    flip_ref[...] = entry.T
    back_ref[...] = dy_ref[...].T


def head_specs(heads):
    deep = GROUP * HEAD_SIZE
    return [pl.BlockSpec((h.shape[0], BLOCK, deep), lambda i, a: (0, i, 0)) for h in heads]


def blend(at, x, dy, heads, gain, own, parts):
    width, rows = x.shape
    band = pl.BlockSpec((BLOCK, width), lambda i, a: (i, 0))
    side = pl.BlockSpec((width, BLOCK), lambda i, a: (0, i))
    return call(
        blend_kernel,
        (rows // BLOCK,),
        [side, side]
        + head_specs(heads)
        + [whole((1, width)), whole(own.shape)]
        + [whole(parts[0].shape)] * 4,
        [band, band, side, band],
        [
            struct((rows, width), jnp.float32),
            struct((rows, width), jnp.bfloat16),
            struct((width, rows), jnp.bfloat16),
            struct((rows, width), jnp.bfloat16),
        ],
        scratch=[pltpu.VMEM((2 * own.shape[0], width), jnp.bfloat16)],
        flops=2 * rows * width * width,
        prefetch=1,
        move=18_000_000,
    )(at, x, dy, *heads, gain, own, *parts)


def mix_kernel(
    at_ref, in_ref, flip_ref, dy_ref, back_ref, gate_own, g0, g1, up_own, u0, u1, down_own, d0, d1,
    y_ref, din_ref, gg_ref, gu_ref, gd_ref, gate_ref, up_ref, down_ref,
):
    step = pl.program_id(0)
    x, side = at_ref[0], at_ref[1]
    rows = gate_own.shape[0]
    mine = pl.ds(pl.multiple_of(x * rows, 16), rows)
    theirs = pl.ds(pl.multiple_of((1 - x) * rows, 16), rows)
    gate_ref[mine, :] = gate_own[...]
    up_ref[mine, :] = up_own[...]

    @pl.when(step == side)
    def _():
        gate_ref[theirs, :] = g0[...]
        up_ref[theirs, :] = u0[...]

    @pl.when(step != side)
    def _():
        gate_ref[theirs, :] = g1[...]
        up_ref[theirs, :] = u1[...]

    @pl.when(step == x)
    def _():
        down_ref[...] = down_own[...]

    @pl.when(step != x)
    def _():
        down_ref[pl.ds(pl.multiple_of(side * rows, 16), rows), :] = d0[...]
        down_ref[pl.ds(pl.multiple_of((1 - side) * rows, 16), rows), :] = d1[...]

    entry, dy = in_ref[...], dy_ref[...]
    w_gate, w_up, w_down = gate_ref[...], up_ref[...], down_ref[...]
    gate = dot(entry, w_gate)
    up = dot(entry, w_up)
    sigmoid = jax.nn.sigmoid(gate)
    active = gate * sigmoid
    hidden = (active * up).astype(jnp.bfloat16)
    hidden_grad = dot(dy, w_down)
    gate_grad = (hidden_grad * up * sigmoid * (1.0 + gate * (1.0 - sigmoid))).astype(jnp.bfloat16)
    up_grad = (hidden_grad * active).astype(jnp.bfloat16)
    gd_ref[0] = dot(back_ref[...], hidden).astype(jnp.bfloat16)
    gg_ref[...] = dot(flip_ref[...], gate_grad).astype(jnp.bfloat16)
    gu_ref[...] = dot(flip_ref[...], up_grad).astype(jnp.bfloat16)
    y = dot_nt(hidden, w_down)
    din = dot_nt(gate_grad, w_gate) + dot_nt(up_grad, w_up)

    @pl.when(step == 0)
    def _():
        y_ref[...] = y
        din_ref[...] = din

    @pl.when(step > 0)
    def _():
        y_ref[...] += y
        din_ref[...] += din


def mix(at, entry, flip, dy, back, gate, up, down):
    rows, width = entry.shape
    cut = gate[1].shape[1]
    full, turned = whole((rows, width)), whole((width, rows))
    side = pl.BlockSpec((width // 2, cut), lambda i, a: (0, 2 * i + a[3]))
    piece = whole((width // 2, cut))
    grad = pl.BlockSpec((width, cut), lambda i, a: (0, i))
    return call(
        mix_kernel,
        (2,),
        [full, turned, full, turned, side, piece, piece, side, piece, piece]
        + [pl.BlockSpec((width, cut), lambda i, a: (0, a[3])), piece, piece],
        [full, full, grad, grad, pl.BlockSpec((1, width, cut), lambda i, a: (i, 0, 0))],
        [
            struct((rows, width), jnp.float32),
            struct((rows, width), jnp.float32),
            struct((width, 2 * cut), jnp.bfloat16),
            struct((width, 2 * cut), jnp.bfloat16),
            struct((2, width, cut), jnp.bfloat16),
        ],
        scratch=[pltpu.VMEM((width, cut), jnp.bfloat16)] * 3,
        flops=2 * 9 * rows * width * cut * 2,
        prefetch=1,
        move=30_000_000,
    )(at, entry, flip, dy, back, *gate, *up, *down)


def middle_kernel(
    at_ref, mid_ref, y0_ref, y1_ref, d0_ref, d1_ref, dy_ref, o_ref, gain_ref,
    own_ref, p0, p1, p2, p3, mixed_ref, grad_ref, branch_ref, do_ref, gain_out, w_ref,
):
    step = pl.program_id(0)

    @pl.when(step == 0)
    def _():
        fill_rows(at_ref, w_ref, own_ref, (p0, p1, p2, p3))
        gain_out[...] = jnp.zeros_like(gain_out)

    middle = mid_ref[...]
    mixed_ref[...] = (middle + y0_ref[...] + y1_ref[...]).astype(jnp.bfloat16).T
    inverse = lax.rsqrt(jnp.mean(middle * middle, axis=-1, keepdims=True) + EPS)
    normed = middle * inverse
    back = d0_ref[...] + d1_ref[...]
    product = back * normed
    mean = jnp.mean(product * gain_ref[...], axis=-1, keepdims=True)
    grad = dy_ref[...].astype(jnp.float32) + inverse * (back * gain_ref[...] - normed * mean)
    grad_ref[...] = grad
    branch = grad.astype(jnp.bfloat16)
    branch_ref[...] = branch
    gain_out[...] += jnp.sum(product, axis=0, keepdims=True)
    deep = GROUP * HEAD_SIZE
    lane = lanes_of((BLOCK, LANES))
    inner = lane < HEAD_SIZE
    for g in range(KEY_VALUE_HEADS):
        heads = o_ref[g]
        upstream = dot_nt(branch, w_ref[pl.ds(g * deep, deep), :]).astype(jnp.bfloat16)
        upstream = upstream.astype(jnp.float32)
        both = upstream * heads.astype(jnp.float32)
        pair, pair_both = upstream[:, :LANES], both[:, :LANES]
        wide = (pair, pltpu.roll(pair, HEAD_SIZE, 1), upstream[:, LANES:])
        sums = (
            jnp.sum(jnp.where(inner, pair_both, 0.0), axis=-1, keepdims=True),
            jnp.sum(jnp.where(inner, 0.0, pair_both), axis=-1, keepdims=True),
            jnp.sum(both[:, LANES:], axis=-1, keepdims=True),
        )
        for h in range(GROUP):
            delta = -sums[h]
            high = delta.astype(jnp.bfloat16).astype(jnp.float32)
            low = delta - high
            own = wide[h]
            if own.shape[1] < LANES:
                own = jnp.concatenate([own, jnp.zeros_like(own)], axis=1)
            rest = jnp.where(lane == HEAD_SIZE, high, jnp.where(lane == HEAD_SIZE + 1, low, 0.0))
            do_ref[g * GROUP + h] = jnp.where(inner, own, rest).astype(jnp.bfloat16)


def middle_back(at, middle, y0, y1, d0, d1, dy, heads, gain, own, parts):
    rows, width = middle.shape
    band = pl.BlockSpec((BLOCK, width), lambda i, a: (i, 0))
    return call(
        middle_kernel,
        (rows // BLOCK,),
        [band] * 6
        + head_specs(heads)
        + [whole((1, width)), whole(own.shape)]
        + [whole(parts[0].shape)] * 4,
        [
            pl.BlockSpec((width, BLOCK), lambda i, a: (0, i)),
            band,
            band,
            pl.BlockSpec((QUERY_HEADS, BLOCK, LANES), lambda i, a: (0, i, 0)),
            whole((1, width)),
        ],
        [
            struct((width, rows), jnp.bfloat16),
            struct((rows, width), jnp.float32),
            struct((rows, width), jnp.bfloat16),
            struct((QUERY_HEADS, rows, LANES), jnp.bfloat16),
            struct((1, width), jnp.float32),
        ],
        scratch=[pltpu.VMEM((2 * own.shape[0], width), jnp.bfloat16)],
        flops=2 * rows * width * width,
        prefetch=1,
        move=30_000_000,
    )(at, middle, y0, y1, d0, d1, dy, *heads, gain, own, *parts)


def attend_back_kernel(q_ref, k_ref, v_ref, do_ref, cos_ref, sin_ref, out_ref, dq_ref):
    rows = q_ref.shape[1]
    count = rows // BLOCK
    after = lax.broadcasted_iota(jnp.int32, (BLOCK, BLOCK), 0) <= lanes_of((BLOCK, BLOCK))
    key_grads, value_grads = [], []
    for j in range(count):
        here = pl.ds(j * BLOCK, BLOCK)
        k, v = k_ref[0, here, :], v_ref[0, here, :]
        dk = jnp.zeros((BLOCK, LANES), jnp.float32)
        dv = jnp.zeros((BLOCK, LANES), jnp.float32)
        for h in range(GROUP):
            for start, size in ((j * BLOCK, BLOCK), ((j + 1) * BLOCK, rows - (j + 1) * BLOCK)):
                if not size:
                    continue
                span = pl.ds(start, size)
                q, do = q_ref[h, span, :], do_ref[h, span, :]
                scores = dot_nt(k, q)
                if start == j * BLOCK:
                    scores = jnp.where(after, scores, NEGATIVE)
                probs = jnp.exp(scores)
                score_grad = (probs * dot_nt(v, do)).astype(jnp.bfloat16)
                dv += dot(probs.astype(jnp.bfloat16), do)
                dk += dot(score_grad, q)
                dq = dot_tn(score_grad, k)
                if j == 0:
                    dq_ref[h, span, :] = dq
                else:
                    dq_ref[h, span, :] += dq
        key_grads.append(dk)
        value_grads.append(dv)
    cosine, sine = cos_ref[...], -sin_ref[...]
    half = HEAD_SIZE
    parts = [turn(dq_ref[h] * SCALE, cosine, sine)[:, :half] for h in range(GROUP)]
    parts.append(turn(jnp.concatenate(key_grads, axis=0), cosine, sine)[:, :half])
    parts.append(jnp.concatenate(value_grads, axis=0)[:, :half])
    parts.append(jnp.zeros((rows, WIDE - SPAN), jnp.float32))
    out_ref[0] = jnp.concatenate(parts, axis=1).astype(jnp.bfloat16)


def attend_back(q, k, v, do, cosine, sine, first, groups):
    rows = q.shape[1]
    one = pl.BlockSpec((1, rows, LANES), lambda g: (g + first, 0, 0))
    table = whole((rows, LANES))
    return call(
        attend_back_kernel,
        (groups,),
        [
            pl.BlockSpec((GROUP, rows, LANES), lambda g: (g + first, 0, 0)),
            one,
            one,
            pl.BlockSpec((GROUP, rows, LANES), lambda g: (g + first, 0, 0)),
            table,
            table,
        ],
        pl.BlockSpec((1, rows, WIDE), lambda g: (g, 0, 0)),
        struct((groups, rows, WIDE), jnp.bfloat16),
        scratch=[pltpu.VMEM((GROUP, rows, LANES), jnp.float32)],
        flops=2 * 10 * rows * rows * LANES * GROUP * groups,
        move=3_000_000 * groups,
    )(q, k, v, do, cosine, sine)


def weight_kernel(flip_ref, *refs):
    flip = flip_ref[...]
    parts = [
        dot(flip, ref[g])[:, :SPAN].astype(jnp.bfloat16)
        for ref in refs[:-1]
        for g in range(ref.shape[0])
    ]
    refs[-1][...] = jnp.concatenate(parts, axis=1)


def weight_grads(flip, backs):
    width, rows = flip.shape
    half = width // 2
    across = sum(b.shape[0] for b in backs) * SPAN
    return call(
        weight_kernel,
        (2,),
        [pl.BlockSpec((half, rows), lambda i: (i, 0))] + [whole(b.shape) for b in backs],
        pl.BlockSpec((half, across), lambda i: (i, 0)),
        struct((width, across), jnp.bfloat16),
        flops=2 * rows * width * across,
        move=10_000_000,
    )(flip, *backs)


def near_kernel(flip_ref, back_ref, branch_ref, o_ref, out_ref):
    deep = GROUP * HEAD_SIZE
    branch = branch_ref[...]
    for g in range(KEY_VALUE_HEADS):
        heads = o_ref[g]
        span = pl.ds(g * deep, deep)
        left = dot_tn(heads, branch)
        right = dot(flip_ref[span, :], back_ref[0])[:, :SPAN]
        out_ref[span, :] = jnp.concatenate([left, right], axis=1).astype(jnp.bfloat16)


def near_grads(flip, back, branch, heads):
    width, rows = flip.shape
    args = (flip, back, branch, *heads)
    return call(
        near_kernel,
        (1,),
        [whole(a.shape) for a in args],
        whole((width, width + SPAN)),
        struct((width, width + SPAN), jnp.bfloat16),
        flops=2 * rows * width * (width + SPAN),
        move=12_000_000,
    )(*args)


def finish_kernel(x_ref, mid_ref, *refs):
    *backs, gain_ref, w_ref, out_ref, gain_out = refs
    groups = [ref[g] for ref in backs for g in range(ref.shape[0])]
    x = x_ref[...].astype(jnp.float32).T
    inverse = lax.rsqrt(jnp.mean(x * x, axis=-1, keepdims=True) + EPS)
    normed = x * inverse
    back = jnp.zeros_like(x)
    for g in range(KEY_VALUE_HEADS):
        back += dot_nt(groups[g], w_ref[:, pl.ds(g * WIDE, WIDE)])
    product = back * normed

    @pl.when(pl.program_id(0) == 0)
    def _():
        gain_out[...] = jnp.zeros_like(gain_out)

    gain_out[...] += jnp.sum(product, axis=0, keepdims=True)
    mean = jnp.mean(product * gain_ref[...], axis=-1, keepdims=True)
    grad = mid_ref[...] + inverse * (back * gain_ref[...] - normed * mean)
    out_ref[...] = grad.astype(jnp.bfloat16).T


def finish(x, middle_grad, backs, gain, w_first):
    width, rows = x.shape
    side = pl.BlockSpec((width, BLOCK), lambda i: (0, i))
    return call(
        finish_kernel,
        (rows // BLOCK,),
        [side, pl.BlockSpec((BLOCK, width), lambda i: (i, 0))]
        + [pl.BlockSpec((b.shape[0], BLOCK, WIDE), lambda i: (0, i, 0)) for b in backs]
        + [whole((1, width)), whole(w_first.shape)],
        [side, whole((1, width))],
        [struct((width, rows), jnp.bfloat16), struct((1, width), jnp.float32)],
        flops=2 * rows * width * WIDE * KEY_VALUE_HEADS,
        move=14_000_000,
    )(x, middle_grad, *backs, gain, w_first)


def widen_kernel(at_ref, mine_ref, other_ref, out_ref):
    cut = mine_ref.shape[2]
    mine, other = mine_ref[0].astype(jnp.float32), other_ref[0].astype(jnp.float32)

    @pl.when(at_ref[2] == 0)
    def _():
        out_ref[:, :cut] = mine
        out_ref[:, cut:] = other

    @pl.when(at_ref[2] != 0)
    def _():
        out_ref[:, :cut] = other
        out_ref[:, cut:] = mine


def came_at(at, j, order):
    apart = {2: at[1] ^ (j // 2), 4: at[4] ^ (j % 2)}
    return apart[order[0]] + 2 * apart[order[1]]


def widen(at, mine, other, order, spread):
    _, rows, columns = mine.shape
    if spread:
        shape = (2 * rows, 4 * columns)
        out = pl.BlockSpec((rows, 2 * columns), lambda j, a: (j % 2, j // 2))
    else:
        shape = (4 * rows, 2 * columns)
        out = pl.BlockSpec((rows, 2 * columns), lambda j, a: (j, 0))
    return call(
        widen_kernel,
        (4,),
        [pl.BlockSpec((1, rows, columns), lambda j, a: (came_at(a, j, order), 0, 0))] * 2,
        out,
        struct(shape, jnp.float32),
        prefetch=1,
        move=10_000_000,
    )(at, mine, other)


def unpack_kernel(
    at_ref, near0, near1, far0, far1, q_ref, k_ref, v_ref, out_ref, near_ref, far_ref,
):
    core, side = at_ref[2], at_ref[1]
    rows, columns = near0.shape[1:]
    for j in range(4):
        at = came_at(at_ref, j, (4, 2))
        mine, other = near0[at].astype(jnp.float32), near1[at].astype(jnp.float32)
        left, right = jnp.where(core == 0, mine, other), jnp.where(core == 0, other, mine)
        near_ref[j * rows : (j + 1) * rows, :] = jnp.concatenate([left, right], axis=1)
    for c in range(2):
        for y in range(2):
            at = y ^ side
            mine, other = far0[at].astype(jnp.float32), far1[at].astype(jnp.float32)
            start = (2 * c + y) * mine.shape[0]
            far_ref[start : start + mine.shape[0], :] = jnp.where(core == c, mine, other)
    near, far = near_ref[...], far_ref[...]
    deep = GROUP * HEAD_SIZE
    split = near.shape[1] - SPAN
    groups = [near[:, split:]]
    groups += [far[:, g * SPAN : (g + 1) * SPAN] for g in range(KEY_VALUE_HEADS - 1)]
    out_ref[...] = near[:, :split]
    q_ref[...] = jnp.concatenate([g[:, :deep] for g in groups], axis=1)
    k_ref[...] = jnp.concatenate([g[:, deep : deep + HEAD_SIZE] for g in groups], axis=1).T
    v_ref[...] = jnp.concatenate([g[:, deep + HEAD_SIZE :] for g in groups], axis=1).T


def unpack(at, near, far):
    _, rows, columns = near[0].shape
    args = (*near, *far)
    tall = 4 * rows
    key_columns = KEY_VALUE_HEADS * HEAD_SIZE
    shapes = [
        (tall, QUERY_HEADS * HEAD_SIZE),
        (key_columns, tall),
        (key_columns, tall),
        (tall, 2 * columns - SPAN),
    ]
    return call(
        unpack_kernel,
        (1,),
        [whole(a.shape) for a in args],
        [whole(shape) for shape in shapes],
        [struct(shape, jnp.float32) for shape in shapes],
        scratch=[
            pltpu.VMEM((tall, 2 * columns), jnp.float32),
            pltpu.VMEM((tall, (KEY_VALUE_HEADS - 1) * SPAN), jnp.float32),
        ],
        prefetch=1,
        move=8_000_000,
    )(at, *args)


def tie(value, *others):
    return lax.optimization_barrier((value, *others))[0]


def spare_columns(gain_attn, gain_mlp):
    return jnp.pad(jnp.stack([gain_attn, gain_mlp], axis=1), ((0, 0), (0, WIDE - SPAN - 2)))


def first_rows(w_query, w_key, w_value, spare):
    deep = GROUP * HEAD_SIZE
    columns = []
    for g in range(KEY_VALUE_HEADS):
        columns.append(w_query[:, g * deep : (g + 1) * deep])
        columns.append(w_key[:, g * HEAD_SIZE : (g + 1) * HEAD_SIZE])
        columns.append(w_value[:, g * HEAD_SIZE : (g + 1) * HEAD_SIZE])
        columns.append(spare if g == 0 else jnp.zeros_like(spare))
    return jnp.concatenate(columns, axis=1)


def spread_rows(received):
    beside = swap_rep(received, 2)
    return [received, beside, swap_rep(received, 1), swap_rep(beside, 1)]


def start_sum(send, keep):
    return add_up(keep, swap_rep(send, 1))


def one_step(value, step, axes):
    if step == 0:
        return halve_shard(value)
    return halve(value, rep_bit(step), axes[step], partial(swap_rep, bit=step))


def over_z(value):
    bit = 8
    while bit < lax.axis_size("rep"):
        other = swap_rep(value, bit)
        value = value + other if value.dtype == jnp.float32 else add_up(value, other)
        bit *= 2
    return value


def begin_z(value):
    bit, last = 8, lax.axis_size("rep") // 2
    while bit < last:
        value = add_up(value, swap_rep(value, bit))
        bit *= 2
    return value, (swap_rep(value, last) if last >= 8 else jnp.zeros_like(value))


def begin_step(value, step, axes):
    axis, bit = axes[step], rep_bit(step)
    half = value.shape[axis] // 2
    mine = lax.dynamic_slice_in_dim(value, bit * half, half, axis)
    theirs = lax.dynamic_slice_in_dim(value, (1 - bit) * half, half, axis)
    return mine, swap_rep(theirs, step)


def end_sum(begun, after):
    return add_up(tie(begun[0], after), begun[1])


def back_step(value, step):
    return jnp.concatenate([value, swap_rep(value, step)], axis=0)


def split_cores(grad, axis):
    core = rep_bit(1)
    half = grad.shape[axis] // 2
    send = lax.dynamic_slice_in_dim(grad, (1 - core) * half, half, axis)
    keep = lax.dynamic_slice_in_dim(grad, core * half, half, axis)
    return send, keep


def per_device(
    tokens,
    segments,
    gain_attn,
    w_query,
    key_weight_matrix,
    value_weight_matrix,
    w_out,
    gain_mlp,
    w_gate,
    w_up,
    w_down,
    cotangent,
):
    shards = lax.axis_size("shard")
    fast = shards == 2
    rows, width = tokens.shape[1:]
    half = width // 2
    columns = QUERY_HEADS * HEAD_SIZE
    key_columns = KEY_VALUE_HEADS * HEAD_SIZE
    inner = w_gate.shape[1]
    cut = inner // 4
    x_t = tokens[0].T
    dy_t = cotangent[0].T
    tall = half * 4 // 15
    zero = jnp.int32(0)
    spare = spare_columns(gain_attn, gain_mlp)

    if fast:
        x, side, core, depth = lax.axis_index("shard"), rep_bit(2), rep_bit(1), rep_bit(4)
        x, side, core, depth = (v.astype(jnp.int32) for v in (x, side, core, depth))
        other = 1 - core
        start = window(None, core, side, half)
        narrow = partial(lax.dynamic_slice_in_dim, start_index=start, slice_size=tall, axis=0)
        part_first = first_rows(
            narrow(w_query),
            narrow(key_weight_matrix),
            narrow(value_weight_matrix),
            narrow(spare),
        )
        own_first = (w_query, key_weight_matrix.T, value_weight_matrix.T, spare)
        column = (2 * side + other) * cut
        beside = (2 * (1 - side) + other) * cut
        own_down = w_down.T
        part_up = lax.dynamic_slice_in_dim(w_up, column, cut, 1)
        part_first, part_up = lax.optimization_barrier((part_first, part_up))
        part_down = lax.dynamic_slice(own_down, (side * half, other * cut), (half, cut))
        part_down = tie(part_down, part_up)
        part_out = tie(narrow(w_out), part_down)
        part_gate = tie(lax.dynamic_slice_in_dim(w_gate, column, cut, 1), part_down)
        part_beside = tie(lax.dynamic_slice_in_dim(w_gate, beside, cut, 1), part_down)
        came_first = swap_shard(part_first, 1)
        came_up, came_down = swap_shard(part_up, 1), swap_shard(part_down, 1)
        came_out = swap_shard(part_out, 1)
        came_gate = [swap_shard(part_gate, 1), swap_shard(part_beside, 1)]
        parts_first = spread_rows(came_first)
        own_out, own_gate, own_up = w_out, w_gate, w_up
    else:
        x = side = core = depth = zero
        other = 1 - core
        full_first = [gather_rows(w) for w in (w_query, key_weight_matrix, value_weight_matrix)]
        full_out = gather_rows(w_out)
        starts = [half + window(None, c, y, half) for c in (0, 1) for y in (0, 1)]
        full_first.append(gather_rows(jnp.pad(spare, ((0, 0), (0, 64))))[:, : WIDE - SPAN])
        own_first = (
            full_first[0][:half], full_first[1][:half].T, full_first[2][:half].T,
            full_first[3][:half],
        )
        parts_first = [first_rows(*(w[s : s + tall] for w in full_first)) for s in starts]
        own_out, parts_out = full_out[:half], [full_out[s : s + tall] for s in starts]
        def cut_up(value):
            blocks = [value[half:, k * cut : (k + 1) * cut] for k in range(4)]
            return value[:half], [blocks[1], blocks[3], blocks[0], blocks[2]]

        own_gate, parts_gate = cut_up(gather_rows(w_gate))
        own_up, parts_up = cut_up(gather_rows(w_up))
        full_down = gather_rows(w_down).T
        own_down = full_down[:, : 2 * cut]
        parts_down = [
            full_down[r : r + half, (2 + c) * cut : (3 + c) * cut]
            for c in (1, 0)
            for r in (0, half)
        ]

    at = jnp.stack([x, side, core, core, depth])
    at_other = jnp.stack([x, side, core, other, depth])
    cosine, sine = angles(segments[0], HEAD_SIZE)
    cosine, sine = cosine[:, 0], sine[:, 0]
    cosine, sine = (
        jnp.concatenate([cosine] * 4, axis=1),
        jnp.concatenate([-sine, sine, -sine, sine], axis=1),
    )

    flip_one, q, k, v, w_first, gains = project(
        at, x_t, segments[0][:, None], cosine, sine, own_first, parts_first
    )
    gain_one, gain_two = gains[:1], gains[1:2]
    if fast:
        q, came_up, came_down, came_out = lax.optimization_barrier(
            (q, came_up, came_down, came_out)
        )
        parts_up, parts_down = spread_rows(came_up), spread_rows(came_down)
        parts_out = spread_rows(came_out)
    heads0, back0 = attend(q, k, v, 0, KEY_VALUE_HEADS)
    heads = (heads0,)
    if fast:
        came_gate = [tie(came, heads0) for came in came_gate]
        parts_gate = came_gate + [swap_rep(came, 1) for came in came_gate]
    middle, entry, flip, dy = blend(at, x_t, dy_t, heads, gain_two, own_out, parts_out)
    y0, d0, gate0, up0, down0 = mix(
        at_other, entry, flip, dy, dy_t,
        (own_gate, *parts_gate[:2]), (own_up, *parts_up[:2]), (own_down, *parts_down[:2]),
    )
    y1, d1, gate1, up1, down1 = mix(
        at, tie(entry, d0), flip, dy, dy_t,
        (own_gate, *parts_gate[2:]), (own_up, *parts_up[2:]), (own_down, *parts_down[2:]),
    )
    wide, tower, low = {2: 2, 4: 1}, {2: 1, 4: 1}, {2: 1}
    cube = (2, half, -1)
    if fast:
        gate = start_sum(gate0.reshape(cube), gate1.reshape(cube))
        up = start_sum(up0.reshape(cube), up1.reshape(cube))
        down = start_sum(down0, down1)
        y1, gate, up, down = lax.optimization_barrier((y1, gate, up, down))
        gate, up, down = one_step(gate, 0, wide), one_step(up, 4, wide), one_step(down, 2, tower)
    mixed, middle_grad, branch, do, grad_gain_two = middle_back(
        at, middle, y0, y1, d0, d1, dy, heads, gain_two, own_out, parts_out
    )
    backs = []

    def group_back(do, groups=1):
        g = sum(back.shape[0] for back in backs)
        backs.append(attend_back(back0, k, v, do, cosine, sine, g, groups))

    group_back(do)
    if fast:
        gate, up, down, backs[0] = lax.optimization_barrier((gate, up, down, backs[0]))
        gate, up, down = one_step(gate, 2, wide), one_step(up, 0, wide), one_step(down, 4, tower)
    near = near_grads(flip_one, backs[0], branch, heads)
    group_back(tie(do, near))
    if fast:
        near = start_sum(*split_cores(near.reshape(cube), 2))
        gate, up, down, near, backs[1] = lax.optimization_barrier(
            (gate, up, down, near, backs[1])
        )
        gate, up, down = one_step(gate, 4, wide), one_step(up, 2, wide), one_step(down, 0, tower)
        near = begin_step(near, 2, tower)
    group_back(tie(do, backs[1]))
    if fast:
        gate, up, down, backs[2] = lax.optimization_barrier((gate, up, down, backs[2]))
        gate, up, down = begin_z(gate), begin_z(up), begin_z(down)
    group_back(tie(do, backs[2]), 2)
    if fast:
        gate, up, down, near = (end_sum(part, backs[3]) for part in (gate, up, down, near))
        gate, up, near, backs[3] = lax.optimization_barrier((gate, up, near, backs[3]))
        gate, up, near = back_step(gate, 4), back_step(up, 2), one_step(near, 4, tower)
    far = weight_grads(flip_one, backs[1:])
    if fast:
        far = start_sum(*split_cores(far.reshape(cube), 1))
        far, gate, down, near, middle_grad = lax.optimization_barrier(
            (far, gate, down, near, middle_grad)
        )
        far, near = one_step(far, 0, low), one_step(near, 0, tower)
        gate, down = back_step(gate, 2), back_step(down, 4)
    grad_tokens, grad_gain_one = finish(x_t, middle_grad, backs, gain_one, w_first)
    gain_sums = jnp.concatenate([grad_gain_one, grad_gain_two])
    if fast:
        far, near, up, gate, down, gain_sums = lax.optimization_barrier(
            (far, near, up, gate, down, gain_sums)
        )
        far = one_step(far, 2, low)
        gain_sums += swap_shard(gain_sums, 1)
        near, up = over_z(near), back_step(up, 4)
        sum_gate = widen(at, gate, swap_rep(gate, 1), (4, 2), True)
        far, gain_sums, near, sum_gate = lax.optimization_barrier(
            (far, gain_sums, near, sum_gate)
        )
        far = over_z(far)
        gain_sums += swap_rep(gain_sums, 1)
        near, down = back_step(near, 4), back_step(down, 2)
        far, gain_sums, near, up = lax.optimization_barrier((far, gain_sums, near, up))
        far = add_up(far, swap_rep(far, 4))
        gain_sums = over_z(gain_sums)
        near = back_step(near, 2)
        sum_up = widen(at, up, swap_rep(up, 1), (2, 4), True)
        far, gain_sums, sum_up, near, down = lax.optimization_barrier(
            (far, gain_sums, sum_up, near, down)
        )
        far = back_step(far, 2)
        gain_sums += swap_rep(gain_sums, 2)
        other_near = swap_rep(near, 1)
        sum_down = widen(at, down, swap_rep(down, 1), (4, 2), False).T
        far, other_near, gain_sums, sum_down = lax.optimization_barrier(
            (far, other_near, gain_sums, sum_down)
        )
        gain_sums += swap_rep(gain_sums, 4)
        grad_query, grad_key, grad_value, grad_out = unpack(
            at, (near, other_near), (far, swap_rep(far, 1))
        )
        grad_key, grad_value = grad_key.T, grad_value.T
    else:
        def whole_grad(two, one):
            both = jnp.stack([one.reshape(width, 2, cut), two.reshape(width, 2, cut)], axis=2)
            return both.reshape(width, inner)

        gain_sums = lax.psum(gain_sums, ("rep", "shard"))
        across, upright = {1: 2, 2: 2, 4: 1}, {1: 1, 2: 1, 4: 1}
        sum_gate = reduce_rows(whole_grad(gate0, gate1), (0, 2, 4), across)
        sum_up = reduce_rows(whole_grad(up0, up1), (4, 0, 2), across)
        downs = [d.transpose(1, 0, 2) for d in (down0, down1)]
        sum_down = reduce_rows(whole_grad(*downs).T, (2, 0, 4), upright)
        sums = [reduce_rows(part, (0, 2, 4), across) for part in (near, far)]
        tall_rows = sums[0].shape[0]
        grad_out = sums[0][:, :columns]
        groups = jnp.concatenate([sums[0][:, columns:], *sums[1:]], axis=1)
        groups = groups.reshape(tall_rows, KEY_VALUE_HEADS, SPAN)
        deep = GROUP * HEAD_SIZE
        grad_query = groups[:, :, :deep].reshape(tall_rows, columns)
        grad_key = groups[:, :, deep : deep + HEAD_SIZE].reshape(tall_rows, key_columns)
        grad_value = groups[:, :, deep + HEAD_SIZE :].reshape(tall_rows, key_columns)
    own = width // shards
    gain_sums = lax.dynamic_slice_in_dim(gain_sums, lax.axis_index("shard") * own, own, 1)
    return (
        mixed.T[None],
        grad_tokens.T[None],
        gain_sums[0],
        grad_query,
        grad_key,
        grad_value,
        grad_out,
        gain_sums[1],
        sum_gate,
        sum_up,
        sum_down,
    )


def solution(mesh):
    placed = (
        P(("rep", "shard"), None, None),
        P(("rep", "shard"), None),
        P("shard"),
        P("shard", None),
        P("shard", None),
        P("shard", None),
        P("shard", None),
        P("shard"),
        P("shard", None),
        P("shard", None),
        P("shard", None),
        P(("rep", "shard"), None, None),
    )
    return jax.shard_map(
        per_device,
        mesh=mesh,
        in_specs=placed,
        out_specs=(
            P(("rep", "shard"), None, None),
            P(("rep", "shard"), None, None),
            P("shard"),
            P("shard", None),
            P("shard", None),
            P("shard", None),
            P("shard", None),
            P("shard"),
            P("shard", None),
            P("shard", None),
            P("shard", None),
        ),
        check_vma=False,
    )
```

```python
from functools import partial

import jax
import jax.numpy as jnp
from jax import lax
from jax.experimental import pallas as pl
from jax.experimental.pallas import tpu as pltpu
from jax.sharding import PartitionSpec as P

QUERY_HEADS = 15
KEY_VALUE_HEADS = 5
HEAD_SIZE = 64


EPS = 1e-05
NEGATIVE = -1e30


def angles(documents, head_dim):
    segment_length = documents.shape[0]
    places = jnp.arange(segment_length, dtype=jnp.int32)
    begins = jnp.concatenate([jnp.ones((1,), dtype=jnp.bool_), documents[1:] != documents[:-1]])
    starting = lax.cummax(jnp.where(begins, places, 0), axis=0)
    offsets = (places - starting).astype(jnp.float32)
    rates = 10000.0 ** (-2.0 * jnp.arange(head_dim // 2).astype(jnp.float32) / head_dim)
    phases = offsets[:, None] * rates[None, :]
    return (jnp.cos(phases)[:, None, :], jnp.sin(phases)[:, None, :])


def bit_swap(count, bit):
    return [(i, i ^ bit) for i in range(count)]


def swap_rep(value, bit):
    return lax.ppermute(value, "rep", bit_swap(lax.axis_size("rep"), bit))


def swap_shard(value, bit):
    return lax.ppermute(value, "shard", bit_swap(lax.axis_size("shard"), bit))


def rep_bit(bit):
    return (lax.axis_index("rep") // bit) % 2


def place_pair(mine, other, bit, axis):
    low = jnp.concatenate([mine, other], axis=axis)
    high = jnp.concatenate([other, mine], axis=axis)
    return jnp.where(bit == 0, low, high)


def gather_rows(piece):
    shards = lax.axis_size("shard")
    rows, columns = piece.shape
    quarter = rows // 4
    core, side = rep_bit(1), rep_bit(2)
    part = lax.dynamic_slice_in_dim(piece, (core * 2 + side) * quarter, quarter, 0)
    held = part[None]
    bit = 1
    while bit < shards:
        held = jnp.concatenate([held, swap_shard(held, bit)], axis=0)
        bit *= 2
    others = held[1:]
    others = place_pair(others, swap_rep(others, 2), side, 1)
    others = place_pair(others, swap_rep(others, 1), core, 1)
    me = lax.axis_index("shard")
    if shards == 2:
        return place_pair(piece, others[0], me, 0)
    whole = jnp.zeros((shards, rows, columns), piece.dtype)
    whole = lax.dynamic_update_slice_in_dim(whole, piece[None], me, 0)
    for j in range(1, shards):
        whole = lax.dynamic_update_slice_in_dim(whole, others[j - 1][None], me ^ j, 0)
    return whole.reshape(shards * rows, columns)


def add_up(left, right):
    return (left.astype(jnp.float32) + right.astype(jnp.float32)).astype(jnp.bfloat16)


def halve(value, bit, axis, swap):
    half = value.shape[axis] // 2
    mine = lax.dynamic_slice_in_dim(value, bit * half, half, axis)
    theirs = lax.dynamic_slice_in_dim(value, (1 - bit) * half, half, axis)
    return add_up(mine, swap(theirs))


def halve_shard(value):
    bit = lax.axis_size("shard") // 2
    while bit:
        value = halve(
            value, (lax.axis_index("shard") // bit) % 2, 0, partial(swap_shard, bit=bit)
        )
        bit //= 2
    return value


def reduce_rows(grad, order, axes):
    shards = lax.axis_size("shard")
    rows, columns = grad.shape
    value = grad.astype(jnp.bfloat16).reshape(shards, rows // shards, columns)
    value = halve(value, rep_bit(1), axes[1], partial(swap_rep, bit=1))
    for step in order:
        if step == 0:
            value = halve_shard(value)
        else:
            value = halve(value, rep_bit(step), axes[step], partial(swap_rep, bit=step))
    bit = 8
    while bit < lax.axis_size("rep"):
        value = add_up(value, swap_rep(value, bit))
        bit *= 2
    for step in [s for s in reversed(order) if s] + [1]:
        value = place_pair(value, swap_rep(value, step), rep_bit(step), axes[step])
    return value[0].astype(jnp.float32)


LANES = 128
BLOCK = 256
GROUP = QUERY_HEADS // KEY_VALUE_HEADS
SPAN = (GROUP + 2) * HEAD_SIZE
WIDE = -(-SPAN // LANES) * LANES
SCALE = HEAD_SIZE**-0.5
ROOM = 56 * 1024 * 1024


def dot(left, right):
    return jnp.dot(left, right, preferred_element_type=jnp.float32)


def dot_nt(left, right):
    return lax.dot_general(left, right, (((1,), (1,)), ((), ())), preferred_element_type=jnp.float32)


def dot_tn(left, right):
    return lax.dot_general(left, right, (((0,), (0,)), ((), ())), preferred_element_type=jnp.float32)


def lanes_of(shape):
    return lax.broadcasted_iota(jnp.int32, shape, len(shape) - 1)


def turn(pair, cosine, sine):
    lane = lanes_of(pair.shape) % HEAD_SIZE
    half = HEAD_SIZE // 2
    partner = jnp.where(
        lane < half, pltpu.roll(pair, LANES - half, 1), pltpu.roll(pair, half, 1)
    )
    return pair * cosine + partner * sine


def three_parts(column):
    high = column.astype(jnp.bfloat16)
    rest = column - high.astype(jnp.float32)
    middle = rest.astype(jnp.bfloat16)
    low = (rest - middle.astype(jnp.float32)).astype(jnp.bfloat16)
    return high, middle, low


def put_parts(base, column, first):
    lane = lanes_of(base.shape)
    for k, part in enumerate(three_parts(column)):
        base = jnp.where(lane == first + k, part.astype(jnp.float32), base)
    return base


def call(kernel, grid, in_specs, out_specs, out_shape, scratch=(), flops=0, prefetch=0, move=0):
    return pl.pallas_call(
        kernel,
        grid_spec=pltpu.PrefetchScalarGridSpec(
            num_scalar_prefetch=prefetch,
            grid=grid,
            in_specs=in_specs,
            out_specs=out_specs,
            scratch_shapes=list(scratch),
        ),
        out_shape=out_shape,
        compiler_params=pltpu.CompilerParams(
            dimension_semantics=("arbitrary",) * len(grid), vmem_limit_bytes=ROOM
        ),
        cost_estimate=pl.CostEstimate(flops=flops, bytes_accessed=move, transcendentals=0),
    )


def struct(shape, dtype):
    return jax.ShapeDtypeStruct(shape, dtype)


def whole(shape):
    return pl.BlockSpec(shape, lambda *_: (0,) * len(shape))


def window(at_ref, core, side, rows):
    half = rows // 2
    return core * half + side * (half - rows * 4 // 15)


def fill_rows(at_ref, whole_ref, own_ref, parts):
    rows, tall = own_ref.shape[0], parts[0].shape[0]
    x, side, core = at_ref[0], at_ref[1], at_ref[2]
    whole_ref[pl.ds(pl.multiple_of(x * rows, 16), rows), :] = own_ref[...]
    for k, part in enumerate(parts):
        c, y = core ^ (k // 2), side ^ (k % 2)
        start = (1 - x) * rows + window(at_ref, c, y, rows)
        whole_ref[pl.ds(pl.multiple_of(start, 16), tall), :] = part[...]


def project_kernel(
    at_ref, x_ref, doc_ref, cos_ref, sin_ref, wq_ref, wk_ref, wv_ref, spare_ref, p0, p1, p2, p3,
    flip_ref, q_ref, k_ref, v_ref, w_ref, gains_ref, in_ref, own_ref,
):
    step = pl.program_id(0)

    @pl.when(step == 0)
    def _():
        w_key, w_value = wk_ref[...].T, wv_ref[...].T
        deep = GROUP * HEAD_SIZE
        pad = jnp.zeros_like(spare_ref)
        columns = []
        for g in range(KEY_VALUE_HEADS):
            span = slice(g * HEAD_SIZE, (g + 1) * HEAD_SIZE)
            columns += [wq_ref[:, g * deep : (g + 1) * deep], w_key[:, span], w_value[:, span]]
            columns.append(pad if g else spare_ref[...])
        own_ref[...] = jnp.concatenate(columns, axis=1)
        fill_rows(at_ref, w_ref, own_ref, (p0, p1, p2, p3))
        x = x_ref[...].astype(jnp.float32)
        inverse = lax.rsqrt(jnp.mean(x * x, axis=0, keepdims=True) + EPS)
        first = SPAN % LANES
        spare = w_ref[:, SPAN - first : SPAN - first + LANES].astype(jnp.float32)
        gains_ref[...] = spare.T[first : first + 8, :]
        gain = spare[:, first : first + 1]
        flip = (x * inverse * gain).astype(jnp.bfloat16)
        flip_ref[...] = flip
        in_ref[...] = flip.T

    y = dot(in_ref[...], w_ref[:, pl.ds(pl.multiple_of(step * WIDE, LANES), WIDE)])
    cosine, sine = cos_ref[...], sin_ref[...]
    first = turn(y[:, :LANES], cosine, sine)
    second = turn(y[:, LANES : 2 * LANES], cosine, sine)
    lane = lanes_of(first.shape)
    inner = lane < HEAD_SIZE
    doc = doc_ref[...]
    same = ((lane - HEAD_SIZE) == doc).astype(jnp.float32)
    q_ref[0] = jnp.where(inner, first * SCALE, same).astype(jnp.bfloat16)
    q_ref[1] = jnp.where(inner, pltpu.roll(first, HEAD_SIZE, 1) * SCALE, same).astype(jnp.bfloat16)
    q_ref[2] = jnp.where(inner, second * SCALE, same).astype(jnp.bfloat16)
    away = jnp.where(
        lane < HEAD_SIZE + 4,
        jnp.where((lane - HEAD_SIZE) == doc, 0.0, NEGATIVE),
        jnp.where(lane < HEAD_SIZE + 7, 1.0, 0.0),
    )
    k_ref[0] = jnp.where(inner, pltpu.roll(second, HEAD_SIZE, 1), away).astype(jnp.bfloat16)
    ones = jnp.where(lane < HEAD_SIZE + 3, 1.0, 0.0)
    v_ref[0] = jnp.where(inner, y[:, 2 * LANES :], ones).astype(jnp.bfloat16)


def project(at, x, documents, cosine, sine, own, parts):
    width, rows = x.shape
    table = whole((rows, LANES))
    across = parts[0].shape[1]
    return call(
        project_kernel,
        (KEY_VALUE_HEADS,),
        [whole((width, rows)), whole((rows, 1)), table, table]
        + [whole(w.shape) for w in own]
        + [whole(parts[0].shape)] * 4,
        [
            whole((width, rows)),
            pl.BlockSpec((GROUP, rows, LANES), lambda g, a: (g, 0, 0)),
            pl.BlockSpec((1, rows, LANES), lambda g, a: (g, 0, 0)),
            pl.BlockSpec((1, rows, LANES), lambda g, a: (g, 0, 0)),
            whole((width, across)),
            whole((8, width)),
        ],
        [
            struct((width, rows), jnp.bfloat16),
            struct((QUERY_HEADS, rows, LANES), jnp.bfloat16),
            struct((KEY_VALUE_HEADS, rows, LANES), jnp.bfloat16),
            struct((KEY_VALUE_HEADS, rows, LANES), jnp.bfloat16),
            struct((width, across), jnp.bfloat16),
            struct((8, width), jnp.float32),
        ],
        scratch=[
            pltpu.VMEM((rows, width), jnp.bfloat16),
            pltpu.VMEM((width // 2, across), jnp.bfloat16),
        ],
        flops=2 * rows * width * WIDE * KEY_VALUE_HEADS,
        prefetch=1,
        move=20_000_000,
    )(at, x, documents, cosine, sine, *own, *parts)


def attend_kernel(q_ref, k_ref, v_ref, o_ref, qb_ref):
    rows = q_ref.shape[1]
    deep = GROUP * BLOCK
    row = lax.broadcasted_iota(jnp.int32, (GROUP, BLOCK, BLOCK), 1).reshape(deep, BLOCK)
    below = lanes_of((deep, BLOCK)) <= row
    for i in range(rows // BLOCK):
        here = pl.ds(i * BLOCK, BLOCK)
        q = q_ref[:, here, :].reshape(deep, LANES)
        near = jnp.where(below, dot_nt(q, k_ref[0, here, :]), NEGATIVE)
        top = jnp.max(near, axis=-1, keepdims=True)
        if i:
            past = pl.ds(0, i * BLOCK)
            far = dot_nt(q, k_ref[0, past, :])
            top = jnp.maximum(top, jnp.max(far, axis=-1, keepdims=True))
            total = dot(jnp.exp(far - top).astype(jnp.bfloat16), v_ref[0, past, :])
            total += dot(jnp.exp(near - top).astype(jnp.bfloat16), v_ref[0, here, :])
        else:
            total = dot(jnp.exp(near - top).astype(jnp.bfloat16), v_ref[0, here, :])
        summed = total[:, HEAD_SIZE : HEAD_SIZE + 1]
        out = (total / summed).reshape(GROUP, BLOCK, LANES)
        o_ref[0, here, :] = jnp.concatenate(
            [out[h][:, :HEAD_SIZE] for h in range(GROUP)], axis=1
        ).astype(jnp.bfloat16)
        back = put_parts(q.astype(jnp.float32), -(top + jnp.log(summed)), HEAD_SIZE + 4)
        qb_ref[:, here, :] = back.astype(jnp.bfloat16).reshape(GROUP, BLOCK, LANES)


def attend(q, k, v, first, groups):
    rows = q.shape[1]
    one = pl.BlockSpec((1, rows, LANES), lambda g: (g + first, 0, 0))
    three = pl.BlockSpec((GROUP, rows, LANES), lambda g: (g + first, 0, 0))
    return call(
        attend_kernel,
        (groups,),
        [three, one, one],
        [
            pl.BlockSpec((1, rows, GROUP * HEAD_SIZE), lambda g: (g, 0, 0)),
            pl.BlockSpec((GROUP, rows, LANES), lambda g: (g, 0, 0)),
        ],
        [
            struct((groups, rows, GROUP * HEAD_SIZE), jnp.bfloat16),
            struct((groups * GROUP, rows, LANES), jnp.bfloat16),
        ],
        flops=2 * 4 * rows * rows * LANES * GROUP * groups,
        move=3_000_000 * groups,
    )(q, k, v)


def blend_kernel(
    at_ref, x_ref, dy_ref, o_ref, gain_ref, own_ref, p0, p1, p2, p3,
    mid_ref, in_ref, flip_ref, back_ref, w_ref,
):
    @pl.when(pl.program_id(0) == 0)
    def _():
        fill_rows(at_ref, w_ref, own_ref, (p0, p1, p2, p3))

    total = x_ref[...].astype(jnp.float32).T
    deep = GROUP * HEAD_SIZE
    for g in range(KEY_VALUE_HEADS):
        heads = o_ref[g]
        total += dot(heads, w_ref[pl.ds(g * deep, deep), :])
    mid_ref[...] = total
    inverse = lax.rsqrt(jnp.mean(total * total, axis=-1, keepdims=True) + EPS)
    entry = (total * inverse * gain_ref[...]).astype(jnp.bfloat16)
    in_ref[...] = entry
    flip_ref[...] = entry.T
    back_ref[...] = dy_ref[...].T


def head_specs(heads):
    deep = GROUP * HEAD_SIZE
    return [pl.BlockSpec((h.shape[0], BLOCK, deep), lambda i, a: (0, i, 0)) for h in heads]


def blend(at, x, dy, heads, gain, own, parts):
    width, rows = x.shape
    band = pl.BlockSpec((BLOCK, width), lambda i, a: (i, 0))
    side = pl.BlockSpec((width, BLOCK), lambda i, a: (0, i))
    return call(
        blend_kernel,
        (rows // BLOCK,),
        [side, side]
        + head_specs(heads)
        + [whole((1, width)), whole(own.shape)]
        + [whole(parts[0].shape)] * 4,
        [band, band, side, band],
        [
            struct((rows, width), jnp.float32),
            struct((rows, width), jnp.bfloat16),
            struct((width, rows), jnp.bfloat16),
            struct((rows, width), jnp.bfloat16),
        ],
        scratch=[pltpu.VMEM((2 * own.shape[0], width), jnp.bfloat16)],
        flops=2 * rows * width * width,
        prefetch=1,
        move=18_000_000,
    )(at, x, dy, *heads, gain, own, *parts)


def mix_kernel(
    at_ref, in_ref, flip_ref, dy_ref, back_ref, gate_own, g0, g1, up_own, u0, u1, down_own, d0, d1,
    y_ref, din_ref, gg_ref, gu_ref, gd_ref, gate_ref, up_ref, down_ref,
):
    step = pl.program_id(0)
    x, side = at_ref[0], at_ref[1]
    rows = gate_own.shape[0]
    mine = pl.ds(pl.multiple_of(x * rows, 16), rows)
    theirs = pl.ds(pl.multiple_of((1 - x) * rows, 16), rows)
    gate_ref[mine, :] = gate_own[...]
    up_ref[mine, :] = up_own[...]

    @pl.when(step == side)
    def _():
        gate_ref[theirs, :] = g0[...]
        up_ref[theirs, :] = u0[...]

    @pl.when(step != side)
    def _():
        gate_ref[theirs, :] = g1[...]
        up_ref[theirs, :] = u1[...]

    @pl.when(step == x)
    def _():
        down_ref[...] = down_own[...]

    @pl.when(step != x)
    def _():
        down_ref[pl.ds(pl.multiple_of(side * rows, 16), rows), :] = d0[...]
        down_ref[pl.ds(pl.multiple_of((1 - side) * rows, 16), rows), :] = d1[...]

    entry, dy = in_ref[...], dy_ref[...]
    w_gate, w_up, w_down = gate_ref[...], up_ref[...], down_ref[...]
    gate = dot(entry, w_gate)
    up = dot(entry, w_up)
    sigmoid = jax.nn.sigmoid(gate)
    active = gate * sigmoid
    hidden = (active * up).astype(jnp.bfloat16)
    hidden_grad = dot(dy, w_down)
    gate_grad = (hidden_grad * up * sigmoid * (1.0 + gate * (1.0 - sigmoid))).astype(jnp.bfloat16)
    up_grad = (hidden_grad * active).astype(jnp.bfloat16)
    gd_ref[0] = dot(back_ref[...], hidden).astype(jnp.bfloat16)
    gg_ref[...] = dot(flip_ref[...], gate_grad).astype(jnp.bfloat16)
    gu_ref[...] = dot(flip_ref[...], up_grad).astype(jnp.bfloat16)
    y = dot_nt(hidden, w_down)
    din = dot_nt(gate_grad, w_gate) + dot_nt(up_grad, w_up)

    @pl.when(step == 0)
    def _():
        y_ref[...] = y
        din_ref[...] = din

    @pl.when(step > 0)
    def _():
        y_ref[...] += y
        din_ref[...] += din


def mix(at, entry, flip, dy, back, gate, up, down):
    rows, width = entry.shape
    cut = gate[1].shape[1]
    full, turned = whole((rows, width)), whole((width, rows))
    side = pl.BlockSpec((width // 2, cut), lambda i, a: (0, 2 * i + a[3]))
    piece = whole((width // 2, cut))
    grad = pl.BlockSpec((width, cut), lambda i, a: (0, i))
    return call(
        mix_kernel,
        (2,),
        [full, turned, full, turned, side, piece, piece, side, piece, piece]
        + [pl.BlockSpec((width, cut), lambda i, a: (0, a[3])), piece, piece],
        [full, full, grad, grad, pl.BlockSpec((1, width, cut), lambda i, a: (i, 0, 0))],
        [
            struct((rows, width), jnp.float32),
            struct((rows, width), jnp.float32),
            struct((width, 2 * cut), jnp.bfloat16),
            struct((width, 2 * cut), jnp.bfloat16),
            struct((2, width, cut), jnp.bfloat16),
        ],
        scratch=[pltpu.VMEM((width, cut), jnp.bfloat16)] * 3,
        flops=2 * 9 * rows * width * cut * 2,
        prefetch=1,
        move=30_000_000,
    )(at, entry, flip, dy, back, *gate, *up, *down)


def middle_kernel(
    at_ref, mid_ref, y0_ref, y1_ref, d0_ref, d1_ref, dy_ref, o_ref, gain_ref,
    own_ref, p0, p1, p2, p3, mixed_ref, grad_ref, branch_ref, do_ref, gain_out, w_ref,
):
    step = pl.program_id(0)

    @pl.when(step == 0)
    def _():
        fill_rows(at_ref, w_ref, own_ref, (p0, p1, p2, p3))
        gain_out[...] = jnp.zeros_like(gain_out)

    middle = mid_ref[...]
    mixed_ref[...] = (middle + y0_ref[...] + y1_ref[...]).astype(jnp.bfloat16).T
    inverse = lax.rsqrt(jnp.mean(middle * middle, axis=-1, keepdims=True) + EPS)
    normed = middle * inverse
    back = d0_ref[...] + d1_ref[...]
    product = back * normed
    mean = jnp.mean(product * gain_ref[...], axis=-1, keepdims=True)
    grad = dy_ref[...].astype(jnp.float32) + inverse * (back * gain_ref[...] - normed * mean)
    grad_ref[...] = grad
    branch = grad.astype(jnp.bfloat16)
    branch_ref[...] = branch
    gain_out[...] += jnp.sum(product, axis=0, keepdims=True)
    deep = GROUP * HEAD_SIZE
    lane = lanes_of((BLOCK, LANES))
    inner = lane < HEAD_SIZE
    for g in range(KEY_VALUE_HEADS):
        heads = o_ref[g]
        upstream = dot_nt(branch, w_ref[pl.ds(g * deep, deep), :]).astype(jnp.bfloat16)
        upstream = upstream.astype(jnp.float32)
        both = upstream * heads.astype(jnp.float32)
        pair, pair_both = upstream[:, :LANES], both[:, :LANES]
        wide = (pair, pltpu.roll(pair, HEAD_SIZE, 1), upstream[:, LANES:])
        sums = (
            jnp.sum(jnp.where(inner, pair_both, 0.0), axis=-1, keepdims=True),
            jnp.sum(jnp.where(inner, 0.0, pair_both), axis=-1, keepdims=True),
            jnp.sum(both[:, LANES:], axis=-1, keepdims=True),
        )
        for h in range(GROUP):
            delta = -sums[h]
            high = delta.astype(jnp.bfloat16).astype(jnp.float32)
            low = delta - high
            own = wide[h]
            if own.shape[1] < LANES:
                own = jnp.concatenate([own, jnp.zeros_like(own)], axis=1)
            rest = jnp.where(lane == HEAD_SIZE, high, jnp.where(lane == HEAD_SIZE + 1, low, 0.0))
            do_ref[g * GROUP + h] = jnp.where(inner, own, rest).astype(jnp.bfloat16)


def middle_back(at, middle, y0, y1, d0, d1, dy, heads, gain, own, parts):
    rows, width = middle.shape
    band = pl.BlockSpec((BLOCK, width), lambda i, a: (i, 0))
    return call(
        middle_kernel,
        (rows // BLOCK,),
        [band] * 6
        + head_specs(heads)
        + [whole((1, width)), whole(own.shape)]
        + [whole(parts[0].shape)] * 4,
        [
            pl.BlockSpec((width, BLOCK), lambda i, a: (0, i)),
            band,
            band,
            pl.BlockSpec((QUERY_HEADS, BLOCK, LANES), lambda i, a: (0, i, 0)),
            whole((1, width)),
        ],
        [
            struct((width, rows), jnp.bfloat16),
            struct((rows, width), jnp.float32),
            struct((rows, width), jnp.bfloat16),
            struct((QUERY_HEADS, rows, LANES), jnp.bfloat16),
            struct((1, width), jnp.float32),
        ],
        scratch=[pltpu.VMEM((2 * own.shape[0], width), jnp.bfloat16)],
        flops=2 * rows * width * width,
        prefetch=1,
        move=30_000_000,
    )(at, middle, y0, y1, d0, d1, dy, *heads, gain, own, *parts)


def attend_back_kernel(q_ref, k_ref, v_ref, do_ref, cos_ref, sin_ref, out_ref, dq_ref):
    rows = q_ref.shape[1]
    count = rows // BLOCK
    after = lax.broadcasted_iota(jnp.int32, (BLOCK, BLOCK), 0) <= lanes_of((BLOCK, BLOCK))
    key_grads, value_grads = [], []
    for j in range(count):
        here = pl.ds(j * BLOCK, BLOCK)
        k, v = k_ref[0, here, :], v_ref[0, here, :]
        dk = jnp.zeros((BLOCK, LANES), jnp.float32)
        dv = jnp.zeros((BLOCK, LANES), jnp.float32)
        for h in range(GROUP):
            for start, size in ((j * BLOCK, BLOCK), ((j + 1) * BLOCK, rows - (j + 1) * BLOCK)):
                if not size:
                    continue
                span = pl.ds(start, size)
                q, do = q_ref[h, span, :], do_ref[h, span, :]
                scores = dot_nt(k, q)
                if start == j * BLOCK:
                    scores = jnp.where(after, scores, NEGATIVE)
                probs = jnp.exp(scores)
                score_grad = (probs * dot_nt(v, do)).astype(jnp.bfloat16)
                dv += dot(probs.astype(jnp.bfloat16), do)
                dk += dot(score_grad, q)
                dq = dot_tn(score_grad, k)
                if j == 0:
                    dq_ref[h, span, :] = dq
                else:
                    dq_ref[h, span, :] += dq
        key_grads.append(dk)
        value_grads.append(dv)
    cosine, sine = cos_ref[...], -sin_ref[...]
    half = HEAD_SIZE
    parts = [turn(dq_ref[h] * SCALE, cosine, sine)[:, :half] for h in range(GROUP)]
    parts.append(turn(jnp.concatenate(key_grads, axis=0), cosine, sine)[:, :half])
    parts.append(jnp.concatenate(value_grads, axis=0)[:, :half])
    parts.append(jnp.zeros((rows, WIDE - SPAN), jnp.float32))
    out_ref[0] = jnp.concatenate(parts, axis=1).astype(jnp.bfloat16)


def attend_back(q, k, v, do, cosine, sine, first, groups):
    rows = q.shape[1]
    one = pl.BlockSpec((1, rows, LANES), lambda g: (g + first, 0, 0))
    table = whole((rows, LANES))
    return call(
        attend_back_kernel,
        (groups,),
        [
            pl.BlockSpec((GROUP, rows, LANES), lambda g: (g + first, 0, 0)),
            one,
            one,
            pl.BlockSpec((GROUP, rows, LANES), lambda g: (g + first, 0, 0)),
            table,
            table,
        ],
        pl.BlockSpec((1, rows, WIDE), lambda g: (g, 0, 0)),
        struct((groups, rows, WIDE), jnp.bfloat16),
        scratch=[pltpu.VMEM((GROUP, rows, LANES), jnp.float32)],
        flops=2 * 10 * rows * rows * LANES * GROUP * groups,
        move=3_000_000 * groups,
    )(q, k, v, do, cosine, sine)


def weight_kernel(flip_ref, *refs):
    flip = flip_ref[...]
    parts = [
        dot(flip, ref[g])[:, :SPAN].astype(jnp.bfloat16)
        for ref in refs[:-1]
        for g in range(ref.shape[0])
    ]
    refs[-1][...] = jnp.concatenate(parts, axis=1)


def weight_grads(flip, backs):
    width, rows = flip.shape
    half = width // 2
    across = sum(b.shape[0] for b in backs) * SPAN
    return call(
        weight_kernel,
        (2,),
        [pl.BlockSpec((half, rows), lambda i: (i, 0))] + [whole(b.shape) for b in backs],
        pl.BlockSpec((half, across), lambda i: (i, 0)),
        struct((width, across), jnp.bfloat16),
        flops=2 * rows * width * across,
        move=10_000_000,
    )(flip, *backs)


def near_kernel(flip_ref, back_ref, branch_ref, o_ref, out_ref):
    deep = GROUP * HEAD_SIZE
    branch = branch_ref[...]
    for g in range(KEY_VALUE_HEADS):
        heads = o_ref[g]
        span = pl.ds(g * deep, deep)
        left = dot_tn(heads, branch)
        right = dot(flip_ref[span, :], back_ref[0])[:, :SPAN]
        out_ref[span, :] = jnp.concatenate([left, right], axis=1).astype(jnp.bfloat16)


def near_grads(flip, back, branch, heads):
    width, rows = flip.shape
    args = (flip, back, branch, *heads)
    return call(
        near_kernel,
        (1,),
        [whole(a.shape) for a in args],
        whole((width, width + SPAN)),
        struct((width, width + SPAN), jnp.bfloat16),
        flops=2 * rows * width * (width + SPAN),
        move=12_000_000,
    )(*args)


def finish_kernel(x_ref, mid_ref, *refs):
    *backs, gain_ref, w_ref, out_ref, gain_out = refs
    groups = [ref[g] for ref in backs for g in range(ref.shape[0])]
    x = x_ref[...].astype(jnp.float32).T
    inverse = lax.rsqrt(jnp.mean(x * x, axis=-1, keepdims=True) + EPS)
    normed = x * inverse
    back = jnp.zeros_like(x)
    for g in range(KEY_VALUE_HEADS):
        back += dot_nt(groups[g], w_ref[:, pl.ds(g * WIDE, WIDE)])
    product = back * normed

    @pl.when(pl.program_id(0) == 0)
    def _():
        gain_out[...] = jnp.zeros_like(gain_out)

    gain_out[...] += jnp.sum(product, axis=0, keepdims=True)
    mean = jnp.mean(product * gain_ref[...], axis=-1, keepdims=True)
    grad = mid_ref[...] + inverse * (back * gain_ref[...] - normed * mean)
    out_ref[...] = grad.astype(jnp.bfloat16).T


def finish(x, middle_grad, backs, gain, w_first):
    width, rows = x.shape
    side = pl.BlockSpec((width, BLOCK), lambda i: (0, i))
    return call(
        finish_kernel,
        (rows // BLOCK,),
        [side, pl.BlockSpec((BLOCK, width), lambda i: (i, 0))]
        + [pl.BlockSpec((b.shape[0], BLOCK, WIDE), lambda i: (0, i, 0)) for b in backs]
        + [whole((1, width)), whole(w_first.shape)],
        [side, whole((1, width))],
        [struct((width, rows), jnp.bfloat16), struct((1, width), jnp.float32)],
        flops=2 * rows * width * WIDE * KEY_VALUE_HEADS,
        move=14_000_000,
    )(x, middle_grad, *backs, gain, w_first)


def widen_kernel(at_ref, mine_ref, other_ref, out_ref):
    cut = mine_ref.shape[2]
    mine, other = mine_ref[0].astype(jnp.float32), other_ref[0].astype(jnp.float32)

    @pl.when(at_ref[2] == 0)
    def _():
        out_ref[:, :cut] = mine
        out_ref[:, cut:] = other

    @pl.when(at_ref[2] != 0)
    def _():
        out_ref[:, :cut] = other
        out_ref[:, cut:] = mine


def came_at(at, j, order):
    apart = {2: at[1] ^ (j // 2), 4: at[4] ^ (j % 2)}
    return apart[order[0]] + 2 * apart[order[1]]


def widen(at, mine, other, order, spread):
    _, rows, columns = mine.shape
    if spread:
        shape = (2 * rows, 4 * columns)
        out = pl.BlockSpec((rows, 2 * columns), lambda j, a: (j % 2, j // 2))
    else:
        shape = (4 * rows, 2 * columns)
        out = pl.BlockSpec((rows, 2 * columns), lambda j, a: (j, 0))
    return call(
        widen_kernel,
        (4,),
        [pl.BlockSpec((1, rows, columns), lambda j, a: (came_at(a, j, order), 0, 0))] * 2,
        out,
        struct(shape, jnp.float32),
        prefetch=1,
        move=10_000_000,
    )(at, mine, other)


def unpack_kernel(
    at_ref, near0, near1, far0, far1, q_ref, k_ref, v_ref, out_ref, near_ref, far_ref,
):
    core, side = at_ref[2], at_ref[1]
    rows, columns = near0.shape[1:]
    for j in range(4):
        at = came_at(at_ref, j, (4, 2))
        mine, other = near0[at].astype(jnp.float32), near1[at].astype(jnp.float32)
        left, right = jnp.where(core == 0, mine, other), jnp.where(core == 0, other, mine)
        near_ref[j * rows : (j + 1) * rows, :] = jnp.concatenate([left, right], axis=1)
    for c in range(2):
        for y in range(2):
            at = y ^ side
            mine, other = far0[at].astype(jnp.float32), far1[at].astype(jnp.float32)
            start = (2 * c + y) * mine.shape[0]
            far_ref[start : start + mine.shape[0], :] = jnp.where(core == c, mine, other)
    near, far = near_ref[...], far_ref[...]
    deep = GROUP * HEAD_SIZE
    split = near.shape[1] - SPAN
    groups = [near[:, split:]]
    groups += [far[:, g * SPAN : (g + 1) * SPAN] for g in range(KEY_VALUE_HEADS - 1)]
    out_ref[...] = near[:, :split]
    q_ref[...] = jnp.concatenate([g[:, :deep] for g in groups], axis=1)
    k_ref[...] = jnp.concatenate([g[:, deep : deep + HEAD_SIZE] for g in groups], axis=1).T
    v_ref[...] = jnp.concatenate([g[:, deep + HEAD_SIZE :] for g in groups], axis=1).T


def unpack(at, near, far):
    _, rows, columns = near[0].shape
    args = (*near, *far)
    tall = 4 * rows
    key_columns = KEY_VALUE_HEADS * HEAD_SIZE
    shapes = [
        (tall, QUERY_HEADS * HEAD_SIZE),
        (key_columns, tall),
        (key_columns, tall),
        (tall, 2 * columns - SPAN),
    ]
    return call(
        unpack_kernel,
        (1,),
        [whole(a.shape) for a in args],
        [whole(shape) for shape in shapes],
        [struct(shape, jnp.float32) for shape in shapes],
        scratch=[
            pltpu.VMEM((tall, 2 * columns), jnp.float32),
            pltpu.VMEM((tall, (KEY_VALUE_HEADS - 1) * SPAN), jnp.float32),
        ],
        prefetch=1,
        move=8_000_000,
    )(at, *args)


def tie(value, *others):
    return lax.optimization_barrier((value, *others))[0]


def spare_columns(gain_attn, gain_mlp):
    return jnp.pad(jnp.stack([gain_attn, gain_mlp], axis=1), ((0, 0), (0, WIDE - SPAN - 2)))


def first_rows(w_query, w_key, w_value, spare):
    deep = GROUP * HEAD_SIZE
    columns = []
    for g in range(KEY_VALUE_HEADS):
        columns.append(w_query[:, g * deep : (g + 1) * deep])
        columns.append(w_key[:, g * HEAD_SIZE : (g + 1) * HEAD_SIZE])
        columns.append(w_value[:, g * HEAD_SIZE : (g + 1) * HEAD_SIZE])
        columns.append(spare if g == 0 else jnp.zeros_like(spare))
    return jnp.concatenate(columns, axis=1)


def spread_rows(received):
    beside = swap_rep(received, 2)
    return [received, beside, swap_rep(received, 1), swap_rep(beside, 1)]


def start_sum(send, keep):
    return add_up(keep, swap_rep(send, 1))


def one_step(value, step, axes):
    if step == 0:
        return halve_shard(value)
    return halve(value, rep_bit(step), axes[step], partial(swap_rep, bit=step))


def over_z(value):
    bit = 8
    while bit < lax.axis_size("rep"):
        other = swap_rep(value, bit)
        value = value + other if value.dtype == jnp.float32 else add_up(value, other)
        bit *= 2
    return value


def begin_z(value):
    bit, last = 8, lax.axis_size("rep") // 2
    while bit < last:
        value = add_up(value, swap_rep(value, bit))
        bit *= 2
    return value, (swap_rep(value, last) if last >= 8 else jnp.zeros_like(value))


def begin_step(value, step, axes):
    axis, bit = axes[step], rep_bit(step)
    half = value.shape[axis] // 2
    mine = lax.dynamic_slice_in_dim(value, bit * half, half, axis)
    theirs = lax.dynamic_slice_in_dim(value, (1 - bit) * half, half, axis)
    return mine, swap_rep(theirs, step)


def end_sum(begun, after):
    return add_up(tie(begun[0], after), begun[1])


def back_step(value, step):
    return jnp.concatenate([value, swap_rep(value, step)], axis=0)


def split_cores(grad, axis):
    core = rep_bit(1)
    half = grad.shape[axis] // 2
    send = lax.dynamic_slice_in_dim(grad, (1 - core) * half, half, axis)
    keep = lax.dynamic_slice_in_dim(grad, core * half, half, axis)
    return send, keep


def per_device(
    tokens,
    segments,
    gain_attn,
    w_query,
    key_weight_matrix,
    value_weight_matrix,
    w_out,
    gain_mlp,
    w_gate,
    w_up,
    w_down,
    cotangent,
):
    shards = lax.axis_size("shard")
    fast = shards == 2
    rows, width = tokens.shape[1:]
    half = width // 2
    columns = QUERY_HEADS * HEAD_SIZE
    key_columns = KEY_VALUE_HEADS * HEAD_SIZE
    inner = w_gate.shape[1]
    cut = inner // 4
    x_t = tokens[0].T
    dy_t = cotangent[0].T
    tall = half * 4 // 15
    zero = jnp.int32(0)
    spare = spare_columns(gain_attn, gain_mlp)

    if fast:
        x, side, core, depth = lax.axis_index("shard"), rep_bit(2), rep_bit(1), rep_bit(4)
        x, side, core, depth = (v.astype(jnp.int32) for v in (x, side, core, depth))
        other = 1 - core
        start = window(None, core, side, half)
        narrow = partial(lax.dynamic_slice_in_dim, start_index=start, slice_size=tall, axis=0)
        part_first = first_rows(
            narrow(w_query),
            narrow(key_weight_matrix),
            narrow(value_weight_matrix),
            narrow(spare),
        )
        own_first = (w_query, key_weight_matrix.T, value_weight_matrix.T, spare)
        column = (2 * side + other) * cut
        beside = (2 * (1 - side) + other) * cut
        own_down = w_down.T
        part_up = lax.dynamic_slice_in_dim(w_up, column, cut, 1)
        part_first, part_up = lax.optimization_barrier((part_first, part_up))
        part_down = lax.dynamic_slice(own_down, (side * half, other * cut), (half, cut))
        part_down = tie(part_down, part_up)
        part_out = tie(narrow(w_out), part_down)
        part_gate = tie(lax.dynamic_slice_in_dim(w_gate, column, cut, 1), part_down)
        part_beside = tie(lax.dynamic_slice_in_dim(w_gate, beside, cut, 1), part_down)
        came_first = swap_shard(part_first, 1)
        came_up, came_down = swap_shard(part_up, 1), swap_shard(part_down, 1)
        came_out = swap_shard(part_out, 1)
        came_gate = [swap_shard(part_gate, 1), swap_shard(part_beside, 1)]
        parts_first = spread_rows(came_first)
        own_out, own_gate, own_up = w_out, w_gate, w_up
    else:
        x = side = core = depth = zero
        other = 1 - core
        full_first = [gather_rows(w) for w in (w_query, key_weight_matrix, value_weight_matrix)]
        full_out = gather_rows(w_out)
        starts = [half + window(None, c, y, half) for c in (0, 1) for y in (0, 1)]
        full_first.append(gather_rows(jnp.pad(spare, ((0, 0), (0, 64))))[:, : WIDE - SPAN])
        own_first = (
            full_first[0][:half], full_first[1][:half].T, full_first[2][:half].T,
            full_first[3][:half],
        )
        parts_first = [first_rows(*(w[s : s + tall] for w in full_first)) for s in starts]
        own_out, parts_out = full_out[:half], [full_out[s : s + tall] for s in starts]
        def cut_up(value):
            blocks = [value[half:, k * cut : (k + 1) * cut] for k in range(4)]
            return value[:half], [blocks[1], blocks[3], blocks[0], blocks[2]]

        own_gate, parts_gate = cut_up(gather_rows(w_gate))
        own_up, parts_up = cut_up(gather_rows(w_up))
        full_down = gather_rows(w_down).T
        own_down = full_down[:, : 2 * cut]
        parts_down = [
            full_down[r : r + half, (2 + c) * cut : (3 + c) * cut]
            for c in (1, 0)
            for r in (0, half)
        ]

    at = jnp.stack([x, side, core, core, depth])
    at_other = jnp.stack([x, side, core, other, depth])
    cosine, sine = angles(segments[0], HEAD_SIZE)
    cosine, sine = cosine[:, 0], sine[:, 0]
    cosine, sine = (
        jnp.concatenate([cosine] * 4, axis=1),
        jnp.concatenate([-sine, sine, -sine, sine], axis=1),
    )

    flip_one, q, k, v, w_first, gains = project(
        at, x_t, segments[0][:, None], cosine, sine, own_first, parts_first
    )
    gain_one, gain_two = gains[:1], gains[1:2]
    if fast:
        q, came_up, came_down, came_out = lax.optimization_barrier(
            (q, came_up, came_down, came_out)
        )
        parts_up, parts_down = spread_rows(came_up), spread_rows(came_down)
        parts_out = spread_rows(came_out)
    heads0, back0 = attend(q, k, v, 0, KEY_VALUE_HEADS)
    heads = (heads0,)
    if fast:
        came_gate = [tie(came, heads0) for came in came_gate]
        parts_gate = came_gate + [swap_rep(came, 1) for came in came_gate]
    middle, entry, flip, dy = blend(at, x_t, dy_t, heads, gain_two, own_out, parts_out)
    y0, d0, gate0, up0, down0 = mix(
        at_other, entry, flip, dy, dy_t,
        (own_gate, *parts_gate[:2]), (own_up, *parts_up[:2]), (own_down, *parts_down[:2]),
    )
    y1, d1, gate1, up1, down1 = mix(
        at, tie(entry, d0), flip, dy, dy_t,
        (own_gate, *parts_gate[2:]), (own_up, *parts_up[2:]), (own_down, *parts_down[2:]),
    )
    wide, tower, low = {2: 2, 4: 1}, {2: 1, 4: 1}, {2: 1}
    cube = (2, half, -1)
    if fast:
        gate = start_sum(gate0.reshape(cube), gate1.reshape(cube))
        up = start_sum(up0.reshape(cube), up1.reshape(cube))
        down = start_sum(down0, down1)
        y1, gate, up, down = lax.optimization_barrier((y1, gate, up, down))
        gate, up, down = one_step(gate, 0, wide), one_step(up, 4, wide), one_step(down, 2, tower)
    mixed, middle_grad, branch, do, grad_gain_two = middle_back(
        at, middle, y0, y1, d0, d1, dy, heads, gain_two, own_out, parts_out
    )
    backs = []

    def group_back(do, groups=1):
        g = sum(back.shape[0] for back in backs)
        backs.append(attend_back(back0, k, v, do, cosine, sine, g, groups))

    group_back(do)
    if fast:
        gate, up, down, backs[0] = lax.optimization_barrier((gate, up, down, backs[0]))
        gate, up, down = one_step(gate, 2, wide), one_step(up, 0, wide), one_step(down, 4, tower)
    near = near_grads(flip_one, backs[0], branch, heads)
    group_back(tie(do, near))
    if fast:
        near = start_sum(*split_cores(near.reshape(cube), 2))
        gate, up, down, near, backs[1] = lax.optimization_barrier(
            (gate, up, down, near, backs[1])
        )
        gate, up, down = one_step(gate, 4, wide), one_step(up, 2, wide), one_step(down, 0, tower)
        near = begin_step(near, 2, tower)
    group_back(tie(do, backs[1]))
    if fast:
        gate, up, down, backs[2] = lax.optimization_barrier((gate, up, down, backs[2]))
        gate, up, down = begin_z(gate), begin_z(up), begin_z(down)
    group_back(tie(do, backs[2]), 2)
    if fast:
        gate, up, down, near = (end_sum(part, backs[3]) for part in (gate, up, down, near))
        gate, up, near, backs[3] = lax.optimization_barrier((gate, up, near, backs[3]))
        gate, up, near = back_step(gate, 4), back_step(up, 2), one_step(near, 4, tower)
    far = weight_grads(flip_one, backs[1:])
    if fast:
        far = start_sum(*split_cores(far.reshape(cube), 1))
        far, gate, down, near, middle_grad = lax.optimization_barrier(
            (far, gate, down, near, middle_grad)
        )
        far, near = one_step(far, 0, low), one_step(near, 0, tower)
        gate, down = back_step(gate, 2), back_step(down, 4)
    grad_tokens, grad_gain_one = finish(x_t, middle_grad, backs, gain_one, w_first)
    gain_sums = jnp.concatenate([grad_gain_one, grad_gain_two])
    if fast:
        far, near, up, gate, down, gain_sums = lax.optimization_barrier(
            (far, near, up, gate, down, gain_sums)
        )
        far = one_step(far, 2, low)
        gain_sums += swap_shard(gain_sums, 1)
        near, up = over_z(near), back_step(up, 4)
        sum_gate = widen(at, gate, swap_rep(gate, 1), (4, 2), True)
        far, gain_sums, near = lax.optimization_barrier((far, gain_sums, near))
        far = over_z(far)
        gain_sums += swap_rep(gain_sums, 1)
        near, down = back_step(near, 4), back_step(down, 2)
        far, gain_sums, near, up, sum_gate = lax.optimization_barrier(
            (far, gain_sums, near, up, sum_gate)
        )
        far = add_up(far, swap_rep(far, 4))
        gain_sums = over_z(gain_sums)
        near = back_step(near, 2)
        sum_up = widen(at, up, swap_rep(up, 1), (2, 4), True)
        far, gain_sums, near, down = lax.optimization_barrier((far, gain_sums, near, down))
        far = back_step(far, 2)
        gain_sums += swap_rep(gain_sums, 2)
        other_near = swap_rep(near, 1)
        sum_down = widen(at, down, swap_rep(down, 1), (4, 2), False).T
        far, other_near, gain_sums, sum_up, sum_down = lax.optimization_barrier(
            (far, other_near, gain_sums, sum_up, sum_down)
        )
        gain_sums += swap_rep(gain_sums, 4)
        grad_query, grad_key, grad_value, grad_out = unpack(
            at, (near, other_near), (far, swap_rep(far, 1))
        )
        grad_key, grad_value = grad_key.T, grad_value.T
    else:
        def whole_grad(two, one):
            both = jnp.stack([one.reshape(width, 2, cut), two.reshape(width, 2, cut)], axis=2)
            return both.reshape(width, inner)

        gain_sums = lax.psum(gain_sums, ("rep", "shard"))
        across, upright = {1: 2, 2: 2, 4: 1}, {1: 1, 2: 1, 4: 1}
        sum_gate = reduce_rows(whole_grad(gate0, gate1), (0, 2, 4), across)
        sum_up = reduce_rows(whole_grad(up0, up1), (4, 0, 2), across)
        downs = [d.transpose(1, 0, 2) for d in (down0, down1)]
        sum_down = reduce_rows(whole_grad(*downs).T, (2, 0, 4), upright)
        sums = [reduce_rows(part, (0, 2, 4), across) for part in (near, far)]
        tall_rows = sums[0].shape[0]
        grad_out = sums[0][:, :columns]
        groups = jnp.concatenate([sums[0][:, columns:], *sums[1:]], axis=1)
        groups = groups.reshape(tall_rows, KEY_VALUE_HEADS, SPAN)
        deep = GROUP * HEAD_SIZE
        grad_query = groups[:, :, :deep].reshape(tall_rows, columns)
        grad_key = groups[:, :, deep : deep + HEAD_SIZE].reshape(tall_rows, key_columns)
        grad_value = groups[:, :, deep + HEAD_SIZE :].reshape(tall_rows, key_columns)
    own = width // shards
    gain_sums = lax.dynamic_slice_in_dim(gain_sums, lax.axis_index("shard") * own, own, 1)
    return (
        mixed.T[None],
        grad_tokens.T[None],
        gain_sums[0],
        grad_query,
        grad_key,
        grad_value,
        grad_out,
        gain_sums[1],
        sum_gate,
        sum_up,
        sum_down,
    )


def solution(mesh):
    placed = (
        P(("rep", "shard"), None, None),
        P(("rep", "shard"), None),
        P("shard"),
        P("shard", None),
        P("shard", None),
        P("shard", None),
        P("shard", None),
        P("shard"),
        P("shard", None),
        P("shard", None),
        P("shard", None),
        P(("rep", "shard"), None, None),
    )
    return jax.shard_map(
        per_device,
        mesh=mesh,
        in_specs=placed,
        out_specs=(
            P(("rep", "shard"), None, None),
            P(("rep", "shard"), None, None),
            P("shard"),
            P("shard", None),
            P("shard", None),
            P("shard", None),
            P("shard", None),
            P("shard"),
            P("shard", None),
            P("shard", None),
            P("shard", None),
        ),
        check_vma=False,
    )
```
